256 devices in a mesh: sample: 16 (over x_hi, z), atom: 16 (over y, x_lo, core).
Axes of the slice: x: 4 (x_hi: 2, x_lo: 2; x = x_hi * 2 + x_lo), y: 4, z: 8, core: 2. Of those that a mesh axis runs over, the one named last changes fastest.
Arguments:
- atom_state: bfloat16 [16, 16384, 128], P('sample', 'atom'), may hold values from -6 to 6
- norm_gain: float32 [128], replicated, may hold values from 0.25 to 1.75
- query_weight: bfloat16 [128, 128], replicated, may hold values from -0.5 to 0.5
- key_weight: bfloat16 [128, 128], replicated, may hold values from -0.5 to 0.5
- value_weight: bfloat16 [128, 128], replicated, may hold values from -0.5 to 0.5
- out_weight: bfloat16 [128, 128], replicated, may hold values from -0.5 to 0.5
- token_weight: bfloat16 [128, 768], replicated, may hold values from -0.5 to 0.5
- pair_bias: float32 [512, 4, 32, 128], P('atom'), may hold values from -4 to 300
- key_start: int32 [512], P('atom'), may hold values from 0 to 16256, as said below
- atom_token: int32 [16384], replicated, may hold values from 0 to 2047, as said below
- cotangent_state: bfloat16 [16, 16384, 128], P('sample', 'atom'), may hold values from -6 to 6
- cotangent_tokens: bfloat16 [16, 2048, 768], P('sample', 'atom'), may hold values from -6 to 6
Outputs:
- state_out: bfloat16 [16, 16384, 128], P('sample', 'atom')
- token_rows: bfloat16 [16, 2048, 768], P('sample', 'atom')
- grad_state: float32 [16, 16384, 128], P('sample', 'atom')
- grad_gain: float32 [128], replicated
- grad_query: float32 [128, 128], replicated
- grad_key: float32 [128, 128], replicated
- grad_value: float32 [128, 128], replicated
- grad_output: float32 [128, 128], replicated
- grad_token: float32 [128, 768], replicated
The draws below stay inside these ranges and needn't reach their ends.
Inputs may be any that keep to these rules, and one draw needn't show every extreme that they name: Window w reads key atoms key_start[w] to key_start[w] + 127; key_start[w] - 32 * w lies between 32 // 2 - 128 // 2 - 32 and 32 // 2 - 128 // 2 + 32 except where it is clipped into the grid. `atom_token`: nondecreasing along the atoms; every token has one atom or more; atom 0 belongs to token 0; for 0 < b < 16 the first atom of token b * 128 lies between 128 and 256 atoms after atom b * 1024, and both ends are reached.
All inputs are finite; a program needn't handle non-finite values.
Results may differ from the reference program's by a relative error of at most 0.012.
Values may be sent and summed in bfloat16 or wider, within the bound.
A program may use at most 64 MiB of HBM per device.

```python
import math
import jax
import jax.numpy as jnp
from jax import lax

CHANNELS = 128
HEADS = 4
TOKEN_WIDTH = 768
QW = 32
KEYS = 128
ATOM_DEV = 1024
TOK_DEV = 128
SAMPLES = 16
ATOMS = 16384
TOKENS = 2048
WINDOWS = 512


def draw_pair_bias(key, part):
    key = jax.random.fold_in(key, 5)
    base_key = jax.random.fold_in(key, 0)
    shape = (WINDOWS, HEADS, QW, KEYS)
    values = jnp.clip(jax.random.normal(base_key, shape, jnp.float32), -4.0, 4.0)
    return values.astype(jnp.float32)


def draw_key_start(key, part):
    key = jax.random.fold_in(key, 7)
    jitter_key, chosen_key = jax.random.split(key, 2)
    window_pos = jnp.arange(WINDOWS, dtype=jnp.int32)
    jitter = jax.random.randint(jitter_key, (WINDOWS,), -QW, QW + 1, dtype=jnp.int32)
    chosen = jax.random.permutation(chosen_key, WINDOWS - 8) + 4
    jitter = jitter.at[chosen[0]].set(-QW).at[chosen[1]].set(QW)
    starting = window_pos * QW + QW // 2 - KEYS // 2 + jitter
    return jnp.clip(starting, 0, ATOMS - KEYS).astype(jnp.int32)


def draw_atom_token(key, part):
    key = jax.random.fold_in(key, 11)
    shift_key, chosen_key, weight_key = jax.random.split(key, 3)
    block_count = ATOMS // ATOM_DEV
    extent = ATOM_DEV // 4
    least = ATOM_DEV // 8
    shifts = jax.random.randint(shift_key, (block_count + 1,), least, extent + 1, dtype=jnp.int32)
    chosen = jax.random.permutation(chosen_key, block_count - 1) + 1
    shifts = shifts.at[chosen[0]].set(least).at[chosen[1]].set(extent)
    shifts = shifts.at[0].set(0).at[block_count].set(0)
    bounds = jnp.arange(block_count + 1, dtype=jnp.int32) * ATOM_DEV + shifts
    weights = jax.random.randint(weight_key, (block_count, TOK_DEV), 1, 5, dtype=jnp.int32)
    earlier = jnp.cumsum(weights, axis=1) - weights
    weight_sum = jnp.sum(weights, axis=1, keepdims=True)
    length = (bounds[1:] - bounds[:-1])[:, None]
    starting = (bounds[:-1, None] + length * earlier // weight_sum).reshape(-1)
    positions = jnp.arange(ATOMS, dtype=jnp.int32)
    return (jnp.searchsorted(starting, positions, side='right') - 1).astype(jnp.int32)


def steps_of(own_key, dims, cuts, smallest, largest):
    def one(axis_at, parts):
        steps = jax.random.uniform(jax.random.fold_in(jax.random.fold_in(own_key, 6), axis_at), (parts,), jnp.float32, smallest / len(cuts), largest / len(cuts))
        return jnp.repeat(jnp.exp(steps), dims[axis_at] // parts).reshape((-1,) + (1,) * (len(dims) - axis_at - 1))

    factor_of = one(*cuts[0])
    for cut in cuts[1:]:
        factor_of = factor_of * one(*cut)
    return factor_of


def normal_values(rng, dims, deviation, limit, pieces=(), kind=jnp.bfloat16):
    entries = deviation * jax.random.normal(rng, dims, jnp.float32)
    if pieces:
        entries = entries * steps_of(rng, dims, pieces, -0.22, 0.18)
    return jnp.clip(entries, -limit, limit).astype(kind)


def setup_inputs(seed: int = 0) -> dict:
    arg_keys = jax.random.split(jax.random.key(seed), 13)
    atom_state = normal_values(arg_keys[0], (SAMPLES, ATOMS, CHANNELS), 1.0, 6.0, ((0, 16), (1, 16)))
    norm_gain = jnp.clip(1.0 + 0.15 * jax.random.normal(arg_keys[1], (CHANNELS,), jnp.float32), 0.25, 1.75)
    query_weight = normal_values(arg_keys[2], (CHANNELS, CHANNELS), CHANNELS ** -0.5, 0.5)
    key_weight = normal_values(arg_keys[3], (CHANNELS, CHANNELS), CHANNELS ** -0.5, 0.5)
    value_weight = normal_values(arg_keys[4], (CHANNELS, CHANNELS), CHANNELS ** -0.5, 0.5)
    out_weight = normal_values(arg_keys[5], (CHANNELS, CHANNELS), CHANNELS ** -0.5, 0.5)
    token_weight = normal_values(arg_keys[6], (CHANNELS, TOKEN_WIDTH), CHANNELS ** -0.5, 0.5)
    pair_bias = draw_pair_bias(jax.random.fold_in(arg_keys[12], 71), 0)
    key_start = draw_key_start(jax.random.fold_in(arg_keys[12], 71), 0)
    atom_token = draw_atom_token(jax.random.fold_in(arg_keys[12], 71), 0)
    cotangent_state = normal_values(arg_keys[10], (SAMPLES, ATOMS, CHANNELS), 1.0, 6.0, ((0, 16), (1, 16)))
    cotangent_tokens = normal_values(arg_keys[11], (SAMPLES, TOKENS, TOKEN_WIDTH), 1.0, 6.0, ((0, 16), (1, 16)))
    return dict(atom_state=atom_state, norm_gain=norm_gain, query_weight=query_weight, key_weight=key_weight, value_weight=value_weight, out_weight=out_weight, token_weight=token_weight, pair_bias=pair_bias, key_start=key_start, atom_token=atom_token, cotangent_state=cotangent_state, cotangent_tokens=cotangent_tokens)


norm_eps = 1e-05
highest = lax.Precision.HIGHEST

def normalize(state_rows, norm_gain):
    widened = state_rows.astype(jnp.float32)
    average = lax.optimization_barrier(jnp.mean(widened, axis=-1, keepdims=True))
    centred = widened - average
    variance = lax.optimization_barrier(jnp.mean(centred * centred, axis=-1, keepdims=True))
    inverse = lax.rsqrt(variance + norm_eps)
    unit_rows = centred * inverse
    return (unit_rows, inverse, (unit_rows * norm_gain).astype(jnp.bfloat16))

def widen(matrix):
    return matrix.astype(jnp.float32)

def project(left, right):
    return jnp.dot(left, right, preferred_element_type=jnp.float32)

def lowered(values):
    return lax.optimization_barrier(values.astype(jnp.bfloat16)).astype(jnp.float32)

def silu_slope(values):
    sigma = jax.nn.sigmoid(values)
    return sigma * (1.0 + values * (1.0 - sigma))

def reference(atom_state, norm_gain, query_weight, key_weight, value_weight, out_weight, token_weight, pair_bias, key_start, atom_token, cotangent_state, cotangent_tokens):
    head_dim = CHANNELS // HEADS
    factor = head_dim ** (-0.5)
    offsets = key_start[:, None] + jnp.arange(KEYS, dtype=jnp.int32)[None, :]
    counts = jax.ops.segment_sum(jnp.ones((ATOMS,), jnp.float32), atom_token, TOKENS)
    atom_counts = jnp.take(counts, atom_token)

    def one_sample(inputs):
        state, sample_back, tokens_back = inputs
        unit_rows, inverse, normed = normalize(state, norm_gain)
        queries = project(normed, query_weight).astype(jnp.bfloat16)
        keys_all = project(normed, key_weight).astype(jnp.bfloat16)
        values_all = project(normed, value_weight).astype(jnp.bfloat16)
        query_heads = widen(queries).reshape(WINDOWS, QW, HEADS, head_dim)
        key_heads = widen(jnp.take(keys_all, offsets, axis=0)).reshape(WINDOWS, KEYS, HEADS, head_dim)
        value_heads = widen(jnp.take(values_all, offsets, axis=0)).reshape(WINDOWS, KEYS, HEADS, head_dim)
        scores = jnp.einsum('wqhd,wkhd->whqk', query_heads, key_heads) * factor + pair_bias.astype(jnp.float32)
        softmaxed = jax.nn.softmax(scores, axis=-1)
        softmaxed_low = lowered(softmaxed)
        attended = jnp.einsum('whqk,wkhd->wqhd', softmaxed_low, value_heads).astype(jnp.bfloat16).reshape(ATOMS, CHANNELS)
        state_out = (widen(state) + project(attended, out_weight)).astype(jnp.bfloat16)
        before = project(state_out, token_weight)
        totals = jax.ops.segment_sum(jax.nn.silu(before), atom_token, TOKENS)
        token_rows = (totals / counts[:, None]).astype(jnp.bfloat16)
        per_atom = widen(jnp.take(tokens_back, atom_token, axis=0)) / atom_counts[:, None]
        active_back = (per_atom * silu_slope(before)).astype(jnp.bfloat16)
        token_sum = project(state_out.T, active_back)
        state_back = (widen(sample_back) + project(active_back, token_weight.T)).astype(jnp.bfloat16)
        output_sum = project(attended.T, state_back)
        attended_back = project(state_back, out_weight.T).astype(jnp.bfloat16)
        heads_back = widen(attended_back).reshape(WINDOWS, QW, HEADS, head_dim)
        softmax_back = jnp.einsum('wqhd,wkhd->whqk', heads_back, value_heads)
        scores_back = softmaxed * (softmax_back - lax.optimization_barrier(jnp.sum(softmaxed * softmax_back, axis=-1, keepdims=True)))
        scores_low = lowered(scores_back)
        query_back = (jnp.einsum('whqk,wkhd->wqhd', scores_low, key_heads) * factor).reshape(ATOMS, CHANNELS)
        keys_back = (jnp.einsum('whqk,wqhd->wkhd', scores_low, query_heads) * factor).reshape(WINDOWS, KEYS, CHANNELS)
        values_back = jnp.einsum('whqk,wqhd->wkhd', softmaxed_low, heads_back).reshape(WINDOWS, KEYS, CHANNELS)
        key_total = jnp.zeros((ATOMS, CHANNELS), jnp.float32).at[offsets].add(keys_back)
        value_total = jnp.zeros((ATOMS, CHANNELS), jnp.float32).at[offsets].add(values_back)
        normed_full = widen(normed)
        query_sum = jnp.dot(normed_full.T, query_back, precision=highest)
        key_sum = jnp.dot(normed_full.T, key_total, precision=highest)
        value_sum = jnp.dot(normed_full.T, value_total, precision=highest)
        normed_back = jnp.dot(query_back, widen(query_weight).T, precision=highest)
        normed_back = normed_back + jnp.dot(key_total, widen(key_weight).T, precision=highest)
        normed_back = normed_back + jnp.dot(value_total, widen(value_weight).T, precision=highest)
        gain_sum = lax.optimization_barrier(jnp.sum(unit_rows * normed_back, axis=0))
        unit_back = normed_back * norm_gain
        grad_rows = widen(state_back) + inverse * (unit_back - lax.optimization_barrier(jnp.mean(unit_back, axis=-1, keepdims=True)) - unit_rows * lax.optimization_barrier(jnp.mean(unit_back * unit_rows, axis=-1, keepdims=True)))
        return (state_out, token_rows, grad_rows, gain_sum, query_sum, key_sum, value_sum, output_sum, token_sum)
    results = lax.map(one_sample, (atom_state, cotangent_state, cotangent_tokens))
    rescale = 1.0 / math.sqrt(SAMPLES * ATOMS)
    return (results[0], results[1], results[2], lax.optimization_barrier(jnp.sum(results[3], axis=0)) * rescale, lax.optimization_barrier(jnp.sum(results[4], axis=0)) * rescale, lax.optimization_barrier(jnp.sum(results[5], axis=0)) * rescale, lax.optimization_barrier(jnp.sum(results[6], axis=0)) * rescale, lax.optimization_barrier(jnp.sum(results[7], axis=0)) * rescale, lax.optimization_barrier(jnp.sum(results[8], axis=0)) * rescale)
```

```python
import functools
import math

import jax
import jax.numpy as jnp
from jax import lax
from jax.experimental import pallas as pl
from jax.experimental.pallas import tpu as pltpu
from jax.sharding import PartitionSpec as P

MESH = pl.DeviceIdType.MESH
norm_eps = 1e-05
f32 = jnp.float32
bf16 = jnp.bfloat16


def nn(a, b):
    return lax.dot_general(a, b, (((1,), (0,)), ((), ())), preferred_element_type=f32)


def nt(a, b):
    return lax.dot_general(a, b, (((1,), (1,)), ((), ())), preferred_element_type=f32)


def tn(a, b):
    return lax.dot_general(a, b, (((0,), (0,)), ((), ())), preferred_element_type=f32)


def kernel(
    sizes,
    state_hbm,
    gain_ref,
    wq_hbm,
    wk_hbm,
    wv_hbm,
    wo_hbm,
    wt_hbm,
    bias_hbm,
    start_ref,
    token_ref,
    cots_hbm,
    ctok_hbm,
    state_out_hbm,
    rows_out_hbm,
    grad_out_hbm,
    late_out_hbm,
    early_out_hbm,
    state,
    w3,
    wo,
    wt,
    bias,
    cots,
    ctok,
    ctok_low,
    halo,
    unit,
    inverse,
    normed,
    queries,
    kvf,
    kvw,
    probs,
    attended,
    state_out,
    sel_cat,
    sel_t,
    sel_tlow,
    tokens_back,
    inv_own,
    silu,
    active,
    state_back,
    attended_back,
    low_part,
    high_part,
    rows_out,
    shift,
    spread,
    query_back,
    spread_low,
    nback,
    nback_send,
    nback_recv,
    grad_out,
    e_src,
    e_rx1,
    e_sum,
    e_rx2,
    e_fin,
    l_src,
    l_rx1,
    l_sum,
    l_rx2,
    l_fin,
    head_mask,
    load_sem,
    out_sem,
    send_sem,
    recv_sem,
):
    A, B, rows, channels, windows, heads, qw, keys, toks, width = sizes
    margin = keys // 2 + qw // 2
    full = rows + 2 * margin
    span = keys + 2 * qw
    head_dim = channels // heads
    factor = head_dim ** (-0.5)
    fold = 2 * channels // A
    half = channels // A
    me = lax.axis_index("atom")
    smp = lax.axis_index("sample")
    left = {"atom": lax.rem(me + A - 1, A)}
    right = {"atom": lax.rem(me + 1, A)}

    def load(src, dst, index):
        return pltpu.make_async_copy(src, dst, load_sem.at[index])

    loads = [
        load(state_hbm.at[0], state, 0),
        load(wq_hbm, w3.at[:, pl.ds(0, channels)], 1),
        load(wk_hbm, w3.at[:, pl.ds(channels, channels)], 2),
        load(wv_hbm, w3.at[:, pl.ds(2 * channels, channels)], 3),
        load(bias_hbm, bias, 4),
        load(wo_hbm, wo, 5),
        load(wt_hbm, wt, 6),
        load(cots_hbm.at[0], cots, 7),
        load(ctok_hbm.at[0], ctok, 8),
    ]
    for copy in loads:
        copy.start()

    barrier = pltpu.get_barrier_semaphore()

    def greet(d, _):
        pl.semaphore_signal(
            barrier, inc=1, device_id={"atom": lax.rem(me + d, A)}, device_id_type=MESH
        )
        return 0

    def greet_sample(d, _):
        pl.semaphore_signal(
            barrier, inc=1, device_id={"sample": lax.rem(smp + d, B)}, device_id_type=MESH
        )
        return 0

    lax.fori_loop(1, A, greet, 0)
    lax.fori_loop(1, B, greet_sample, 0)

    def send(src, dst, index, device):
        return pltpu.make_async_remote_copy(
            src_ref=src,
            dst_ref=dst,
            send_sem=send_sem.at[index],
            recv_sem=recv_sem.at[index],
            device_id=device,
            device_id_type=MESH,
        )

    def wait_bytes(ref, sem):
        pltpu.make_async_copy(ref, ref, sem).wait()

    def norm(x):
        x = x.astype(f32)
        average = jnp.mean(x, axis=-1, keepdims=True)
        centred = x - average
        variance = jnp.mean(centred * centred, axis=-1, keepdims=True)
        inv = lax.rsqrt(variance + norm_eps)
        unit_rows = centred * inv
        return unit_rows, inv, (unit_rows * gain_ref[...]).astype(bf16)

    for index in range(4):
        loads[index].wait()

    lanes = lax.broadcasted_iota(jnp.int32, (keys, channels), 1)
    subs = lax.broadcasted_iota(jnp.int32, (keys, channels), 0)
    head_mask[...] = jnp.where(subs // qw == lanes // head_dim, 1.0, 0.0).astype(bf16)

    block = 256

    def project(c, _):
        r = pl.multiple_of(c * block, block)
        unit_rows, inv, low = norm(state[pl.ds(r, block), :])
        unit[pl.ds(margin + r, block), :] = unit_rows
        inverse[pl.ds(r, block), :] = jnp.broadcast_to(inv, (block, channels))
        normed[pl.ds(margin + r, block), :] = low
        qkv = nn(low, w3[...]).astype(bf16)
        queries[pl.ds(r, block), :] = qkv[:, :channels]
        kvf[0, pl.ds(margin + r, block), :] = qkv[:, channels : 2 * channels].astype(f32)
        kvf[1, pl.ds(margin + r, block), :] = qkv[:, 2 * channels :].astype(f32)
        return 0

    lax.fori_loop(0, rows // block, project, 0)

    pl.semaphore_wait(barrier, A + B - 2)

    halo_left = send(
        state_hbm.at[0, pl.ds(rows - margin, margin), :], halo.at[0], 0, right
    )
    halo_right = send(state_hbm.at[0, pl.ds(0, margin), :], halo.at[1], 1, left)
    tokens_up = send(ctok_hbm.at[0], ctok_low, 2, right)
    halo_left.start()
    halo_right.start()
    tokens_up.start()

    spread[...] = jnp.zeros((2, full, channels), f32)
    for slot in range(4):
        shift[slot, pl.ds(0, 2 * qw), :] = jnp.zeros((2 * qw, channels), f32)
        shift[slot, pl.ds(2 * qw + keys, 2 * qw), :] = jnp.zeros((2 * qw, channels), f32)

    per_tile = rows // 128
    base = (me * toks).astype(f32)
    lower = base - toks
    sub_id = subs.astype(f32)
    lane_id = lanes.astype(f32)
    count_own = jnp.zeros((toks, 128), f32)
    count_low = jnp.zeros((toks, 128), f32)
    for r in range(per_tile):
        row = token_ref[pl.ds(me * per_tile + r, 1), :].astype(f32)
        spot = jnp.broadcast_to(row, (128, 128))
        hit = jnp.where(spot - base == sub_id, 1.0, 0.0)
        count_own = count_own + hit
        sel_t[:, pl.ds(r * 128, 128)] = hit.astype(bf16)
        if r < 2:
            hit = jnp.where(spot - lower == sub_id, 1.0, 0.0)
            count_low = count_low + hit
            sel_tlow[:, pl.ds(r * 128, 128)] = hit.astype(bf16)
        column = spot.T - lower
        sel_cat[pl.ds(r * 128, 128), pl.ds(0, 128)] = jnp.where(
            column == lane_id, 1.0, 0.0
        ).astype(bf16)
        sel_cat[pl.ds(r * 128, 128), pl.ds(128, 128)] = jnp.where(
            column == lane_id + toks, 1.0, 0.0
        ).astype(bf16)
    has_above = jnp.where(me < A - 1, 1.0, 0.0)
    above = jnp.minimum(me + 1, A - 1) * per_tile
    for r in range(2):
        row = token_ref[pl.ds(above + r, 1), :].astype(f32)
        spot = jnp.broadcast_to(row, (128, 128))
        count_own = count_own + jnp.where(spot - base == sub_id, has_above, 0.0)
    has_below = jnp.where(me > 0, 1.0, 0.0)
    below = jnp.maximum(me - 1, 0) * per_tile
    for r in range(per_tile):
        row = token_ref[pl.ds(below + r, 1), :].astype(f32)
        spot = jnp.broadcast_to(row, (128, 128))
        count_low = count_low + jnp.where(spot - lower == sub_id, has_below, 0.0)

    def inverted(count):
        total = jnp.sum(count, axis=-1, keepdims=True)
        return jnp.where(total > 0.0, 1.0 / jnp.maximum(total, 1.0), 0.0)

    inverse_own = inverted(count_own)
    inverse_low = inverted(count_low)
    inv_own[...] = jnp.broadcast_to(inverse_own, (toks, 128))
    loads[8].wait()
    tokens_back[pl.ds(toks, toks), :] = (ctok[...].astype(f32) * inverse_own).astype(bf16)

    first_atom = me * rows
    last_base = A * rows - span

    def spread_heads(x):
        return jnp.concatenate([x] * heads, axis=0) * head_mask[...]

    def gather_heads(x):
        lane = lax.broadcasted_iota(jnp.int32, (qw, channels), 1)
        out = x[0:qw]
        for h in range(1, heads):
            out = jnp.where(lane >= h * head_dim, x[h * qw : (h + 1) * qw], out)
        return out

    def forward(w):
        place = jnp.clip(start_ref[w] - first_atom + margin, 0, full - keys)
        k = kvf[0, pl.ds(place, keys), :].astype(bf16)
        v = kvf[1, pl.ds(place, keys), :].astype(bf16)
        kvw[w, :, pl.ds(0, channels)] = k
        kvw[w, :, pl.ds(channels, channels)] = v
        q0 = pl.multiple_of(w * qw, qw)
        q = spread_heads(queries[pl.ds(q0, qw), :])
        s = nt(q, k) * factor + bias[w]
        e = jnp.exp(s - jnp.max(s, axis=-1, keepdims=True))
        p = (e / jnp.sum(e, axis=-1, keepdims=True)).astype(bf16)
        probs[w] = p
        attended[pl.ds(q0, qw), :] = gather_heads(nn(p, v)).astype(bf16)

    near = (margin + qw - 1) // qw
    loads[4].wait()

    def forward_pair(i, _):
        for k in range(2):
            forward(lax.rem(2 * i + k + near, windows))
        return 0

    inner = (windows - 2 * near) // 2
    lax.fori_loop(0, inner, forward_pair, 0)

    halo_left.wait_recv()
    halo_right.wait_recv()
    for side in range(2):
        there = (me > 0) if side == 0 else (me < A - 1)
        at = 0 if side == 0 else margin + rows
        keep = jnp.where(there, 1.0, 0.0)
        x = jnp.where(jnp.full((margin, channels), keep) > 0.0, halo[side].astype(f32), 0.0)
        unit_rows, _, low = norm(x)
        unit[pl.ds(at, margin), :] = unit_rows
        normed[pl.ds(at, margin), :] = low
        kv = nn(low, w3[:, channels:]).astype(bf16).astype(f32)
        kvf[0, pl.ds(at, margin), :] = kv[:, :channels]
        kvf[1, pl.ds(at, margin), :] = kv[:, channels:]

    lax.fori_loop(inner, windows // 2, forward_pair, 0)

    tokens_up.wait_recv()
    tokens_back[pl.ds(0, toks), :] = (ctok_low[...].astype(f32) * inverse_low).astype(bf16)
    for index in range(5, 8):
        loads[index].wait()

    def token_part(c):
        r = c * block if isinstance(c, int) else pl.multiple_of(c * block, block)
        here = pl.ds(r, block)
        out = (state[here, :].astype(f32) + nn(attended[here, :], wo[...])).astype(bf16)
        state_out[here, :] = out
        before = nn(out, wt[...])
        sigma = 0.5 * jnp.tanh(0.5 * before) + 0.5
        act = before * sigma
        silu[here, :] = act.astype(bf16)
        slope = sigma + act - act * sigma
        per_atom = nn(sel_cat[here, :], tokens_back[...])
        back = (per_atom * slope).astype(bf16)
        active[here, :] = back
        sback = (cots[here, :].astype(f32) + nt(back, wt[...])).astype(bf16)
        state_back[here, :] = sback
        attended_back[here, :] = nt(sback, wo[...]).astype(bf16)

    token_part(0)
    low_part[...] = nn(sel_tlow[...], silu[pl.ds(0, 256), :]).astype(bf16)
    part_down = send(low_part, high_part, 3, left)
    part_down.start()
    lax.fori_loop(1, rows // block, lambda c, _: (token_part(c), 0)[1], 0)

    def store(src, dst, index):
        return pltpu.make_async_copy(src, dst, out_sem.at[index])

    out_state = store(state_out, state_out_hbm.at[0], 0)
    out_state.start()

    def folded(x):
        x = x.reshape(A, half, x.shape[-1])
        mid = x.shape[-1] // 2
        return jnp.concatenate([x[..., :mid], x[..., mid:]], axis=1)

    def stacked(x, y):
        return jnp.concatenate(
            [x.reshape(A, half, channels), y.reshape(A, half, channels)], axis=1
        )

    token_sum = tn(state_out[...], active[...])
    e_src[:, :, pl.ds(0, width // 2)] = folded(token_sum).astype(bf16)
    output_sum = tn(attended[...], state_back[...])
    output_high = output_sum.astype(bf16).astype(f32)
    e_src[:, :, pl.ds(width // 2, channels)] = stacked(
        output_high, output_sum - output_high
    ).astype(bf16)

    def scatter(src, rx, index):
        def one(d, _):
            peer = lax.rem(me + d, A)
            send(src.at[peer], rx.at[d], index, {"atom": peer}).start()
            return 0

        lax.fori_loop(1, A, one, 0)

    def scattered(src, rx, part, rx2, index):
        wait_bytes(rx.at[pl.ds(1, A - 1)], recv_sem.at[index])
        total = src[me].astype(f32)
        for d in range(1, A):
            total = total + rx[d].astype(f32)
        low = total.astype(bf16)
        part[...] = low
        rx2[smp] = low

    def exchange(part, rx2, index):
        def one(d, _):
            peer = lax.rem(smp + d, B)
            send(part, rx2.at[smp], index, {"sample": peer}).start()
            return 0

        lax.fori_loop(1, B, one, 0)

    def exchanged(rx2, fin, index):
        wait_bytes(rx2.at[pl.ds(0, B - 1)], recv_sem.at[index])
        total = rx2[0].astype(f32)
        for d in range(1, B):
            total = total + rx2[d].astype(f32)
        fin[me] = total.astype(bf16)

    def gather(fin, index):
        def one(d, _):
            peer = lax.rem(me + d, A)
            send(fin.at[me], fin.at[me], index, {"atom": peer}).start()
            return 0

        lax.fori_loop(1, A, one, 0)

    def gathered(fin, index):
        wait_bytes(fin.at[pl.ds(0, A - 1)], recv_sem.at[index])

    scatter(e_src, e_rx1, 4)

    def backward(w, slot):
        base_atom = jnp.clip(first_atom + w * qw - margin, 0, last_base)
        off = jnp.clip(start_ref[w] - base_atom, 0, 2 * qw)
        kv = kvw[w]
        q0 = pl.multiple_of(w * qw, qw)
        q = spread_heads(queries[pl.ds(q0, qw), :])
        da = spread_heads(attended_back[pl.ds(q0, qw), :])
        p = probs[w]
        pf = p.astype(f32)
        weighted = pf * nt(da, kv[:, channels:])
        ds = (weighted - pf * jnp.sum(weighted, axis=-1, keepdims=True)).astype(bf16)
        dq = gather_heads(nn(ds, kv[:, :channels]))
        query_back[pl.ds(q0, qw), :] = (dq * factor).astype(bf16)
        to = pl.ds(pl.multiple_of(base_atom - first_atom + margin, 16), span)
        for part, rows_back in enumerate((tn(ds, q) * factor, tn(p, da))):
            shift[2 * slot + part, pl.ds(2 * qw, keys), :] = rows_back
            moved = shift[2 * slot + part, pl.ds(2 * qw - off, span), :]
            spread[part, to, :] = spread[part, to, :] + moved

    def backward_pair(i, _):
        for k in range(2):
            backward(2 * i + k, k)
        return 0

    lax.fori_loop(0, windows // 4, backward_pair, 0)
    scattered(e_src, e_rx1, e_sum, e_rx2, 4)
    exchange(e_sum, e_rx2, 5)
    lax.fori_loop(windows // 4, windows // 2, backward_pair, 0)
    exchanged(e_rx2, e_fin, 5)
    gather(e_fin, 6)

    spread_low[:, pl.ds(0, channels)] = spread[0].astype(bf16)
    spread_low[:, pl.ds(channels, channels)] = spread[1].astype(bf16)
    nback[...] = nt(spread_low[...], w3[:, channels:])
    nback_send[0] = nback[pl.ds(0, margin), :].astype(bf16)
    nback_send[1] = nback[pl.ds(margin + rows, margin), :].astype(bf16)
    back_left = send(nback_send.at[0], nback_recv.at[1], 7, left)
    back_right = send(nback_send.at[1], nback_recv.at[0], 8, right)
    back_left.start()
    back_right.start()
    own = pl.ds(margin, rows)
    nback[own, :] = nback[own, :] + nt(query_back[...], w3[:, :channels])
    query_sum = tn(normed[own, :], query_back[...])
    pair_sum = tn(normed[...], spread_low[...])
    gain_part = jnp.sum((unit[...] * nback[...]).reshape(full // 8, 8, channels), axis=0)
    gain_rows = jnp.concatenate([gain_part, jnp.zeros((channels - 8, channels), f32)], axis=0)
    l_src[:, :, pl.ds(0, channels)] = stacked(query_sum, pair_sum[:, :channels]).astype(bf16)
    l_src[:, :, pl.ds(channels, channels)] = stacked(pair_sum[:, channels:], gain_rows).astype(
        bf16
    )
    scatter(l_src, l_rx1, 9)

    part_down.wait_recv()
    own_part = nn(sel_t[...], silu[...])
    rows_out[...] = (
        (own_part + high_part[...].astype(f32)) * inv_own[:, pl.ds(0, 1)]
    ).astype(bf16)
    out_rows = store(rows_out, rows_out_hbm.at[0], 1)
    out_rows.start()

    def norm_back(r, count, extra):
        here = pl.ds(r, count)
        there = pl.ds(margin + r, count)
        nb = nback[there, :]
        if extra is not None:
            nb = nb + extra
        ub = nb * gain_ref[...]
        un = unit[there, :]
        grad_out[here, :] = state_back[here, :].astype(f32) + inverse[here, :] * (
            ub
            - jnp.mean(ub, axis=-1, keepdims=True)
            - un * jnp.mean(ub * un, axis=-1, keepdims=True)
        )

    for r in range(0, rows - 2 * margin, 216):
        norm_back(margin + r, min(216, rows - 2 * margin - r), None)
    back_left.wait_recv()
    back_right.wait_recv()
    norm_back(0, margin, nback_recv[0].astype(f32))
    norm_back(rows - margin, margin, nback_recv[1].astype(f32))
    out_grad = store(grad_out, grad_out_hbm.at[0], 2)
    out_grad.start()

    scattered(l_src, l_rx1, l_sum, l_rx2, 9)
    exchange(l_sum, l_rx2, 10)
    gathered(e_fin, 6)
    out_early = store(e_fin, early_out_hbm, 3)
    out_early.start()
    exchanged(l_rx2, l_fin, 10)
    gather(l_fin, 11)
    gathered(l_fin, 11)
    out_late = store(l_fin, late_out_hbm, 4)
    out_late.start()

    for copy in (halo_left, halo_right, tokens_up, part_down, back_left, back_right):
        copy.wait_send()
    for index, ref, count in (
        (4, e_rx1, A),
        (5, e_rx2, B),
        (6, e_fin, A),
        (9, l_rx1, A),
        (10, l_rx2, B),
        (11, l_fin, A),
    ):
        wait_bytes(ref.at[pl.ds(0, count - 1)], send_sem.at[index])
    for copy in (out_state, out_rows, out_grad, out_early, out_late):
        copy.wait()


def on_device(
    A,
    B,
    atom_state,
    norm_gain,
    query_weight,
    key_weight,
    value_weight,
    out_weight,
    token_weight,
    pair_bias,
    key_start,
    atom_token,
    cotangent_state,
    cotangent_tokens,
):
    _, rows, channels = atom_state.shape
    windows, heads, qw, keys = pair_bias.shape
    toks, width = cotangent_tokens.shape[1:]
    sizes = (A, B, rows, channels, windows, heads, qw, keys, toks, width)
    margin = keys // 2 + qw // 2
    full = rows + 2 * margin
    span = keys + 2 * qw
    fold = 2 * channels // A
    half = channels // A
    early = width // 2 + channels
    late = 2 * channels
    any_spec = pl.BlockSpec(memory_space=pl.ANY)
    vmem = pl.BlockSpec(memory_space=pltpu.VMEM)
    smem = pl.BlockSpec(memory_space=pltpu.SMEM)
    V = pltpu.VMEM
    DMA = pltpu.SemaphoreType.DMA
    outs = pl.pallas_call(
        functools.partial(kernel, sizes),
        out_shape=(
            jax.ShapeDtypeStruct((1, rows, channels), bf16),
            jax.ShapeDtypeStruct((1, toks, width), bf16),
            jax.ShapeDtypeStruct((1, rows, channels), f32),
            jax.ShapeDtypeStruct((A, fold, late), bf16),
            jax.ShapeDtypeStruct((A, fold, early), bf16),
        ),
        in_specs=[any_spec, vmem]
        + [any_spec] * 6
        + [smem, vmem]
        + [any_spec] * 2,
        out_specs=(any_spec,) * 5,
        scratch_shapes=[
            V((rows, channels), bf16),
            V((channels, 3 * channels), bf16),
            V((channels, channels), bf16),
            V((channels, width), bf16),
            V((windows, heads * qw, keys), f32),
            V((rows, channels), bf16),
            V((toks, width), bf16),
            V((toks, width), bf16),
            V((2, margin, channels), bf16),
            V((full, channels), f32),
            V((rows, channels), f32),
            V((full, channels), bf16),
            V((rows, channels), bf16),
            V((2, full, channels), f32),
            V((windows, keys, 2 * channels), bf16),
            V((windows, heads * qw, keys), bf16),
            V((rows, channels), bf16),
            V((rows, channels), bf16),
            V((rows, 2 * toks), bf16),
            V((toks, rows), bf16),
            V((toks, 256), bf16),
            V((2 * toks, width), bf16),
            V((toks, 128), f32),
            V((rows, width), bf16),
            V((rows, width), bf16),
            V((rows, channels), bf16),
            V((rows, channels), bf16),
            V((toks, width), bf16),
            V((toks, width), bf16),
            V((toks, width), bf16),
            V((4, keys + 4 * qw, channels), f32),
            V((2, full, channels), f32),
            V((rows, channels), bf16),
            V((full, 2 * channels), bf16),
            V((full, channels), f32),
            V((2, margin, channels), bf16),
            V((2, margin, channels), bf16),
            V((rows, channels), f32),
            V((A, fold, early), bf16),
            V((A, fold, early), bf16),
            V((fold, early), bf16),
            V((B, fold, early), bf16),
            V((A, fold, early), bf16),
            V((A, fold, late), bf16),
            V((A, fold, late), bf16),
            V((fold, late), bf16),
            V((B, fold, late), bf16),
            V((A, fold, late), bf16),
            V((keys, channels), bf16),
            DMA((9,)),
            DMA((5,)),
            DMA((12,)),
            DMA((12,)),
        ],
        compiler_params=pltpu.CompilerParams(
            collective_id=0, has_side_effects=True, vmem_limit_bytes=48 * 1024 * 1024
        ),
        name="atom_block",
    )(
        atom_state,
        norm_gain.reshape(1, channels),
        query_weight,
        key_weight,
        value_weight,
        out_weight,
        token_weight,
        pair_bias.reshape(windows, heads * qw, keys),
        key_start,
        atom_token.reshape(-1, 128),
        cotangent_state,
        cotangent_tokens,
    )
    state_out, token_rows, grad_state, late_sum, early_sum = outs
    rescale = 1.0 / math.sqrt(B * A * rows)
    late_sum = late_sum.astype(f32) * rescale
    early_sum = early_sum.astype(f32) * rescale
    square = (channels, channels)
    grad_query = late_sum[:, :half, :channels].reshape(square)
    grad_key = late_sum[:, half:, :channels].reshape(square)
    grad_value = late_sum[:, :half, channels:].reshape(square)
    grad_gain = jnp.sum(late_sum[:, half:, channels:], axis=(0, 1))
    grad_token = jnp.concatenate(
        [early_sum[:, :half, : width // 2], early_sum[:, half:, : width // 2]], axis=-1
    ).reshape(channels, width)
    grad_output = (
        early_sum[:, :half, width // 2 :] + early_sum[:, half:, width // 2 :]
    ).reshape(square)
    return (
        state_out,
        token_rows,
        grad_state,
        grad_gain,
        grad_query,
        grad_key,
        grad_value,
        grad_output,
        grad_token,
    )


def solution(mesh):
    return jax.shard_map(
        functools.partial(on_device, mesh.shape["atom"], mesh.shape["sample"]),
        mesh=mesh,
        in_specs=(
            P("sample", "atom", None),
            P(),
            P(),
            P(),
            P(),
            P(),
            P(),
            P("atom", None, None, None),
            P("atom"),
            P(),
            P("sample", "atom", None),
            P("sample", "atom", None),
        ),
        out_specs=(
            P("sample", "atom", None),
            P("sample", "atom", None),
            P("sample", "atom", None),
            P(),
            P(),
            P(),
            P(),
            P(),
            P(),
        ),
        check_vma=False,
    )
```

```python
import functools
import math

import jax
import jax.numpy as jnp
from jax import lax
from jax.experimental import pallas as pl
from jax.experimental.pallas import tpu as pltpu
from jax.sharding import PartitionSpec as P

MESH = pl.DeviceIdType.MESH
norm_eps = 1e-05
f32 = jnp.float32
bf16 = jnp.bfloat16


def nn(a, b):
    return lax.dot_general(a, b, (((1,), (0,)), ((), ())), preferred_element_type=f32)


def nt(a, b):
    return lax.dot_general(a, b, (((1,), (1,)), ((), ())), preferred_element_type=f32)


def tn(a, b):
    return lax.dot_general(a, b, (((0,), (0,)), ((), ())), preferred_element_type=f32)


def kernel(
    sizes,
    state_hbm,
    gain_hbm,
    wq_hbm,
    wk_hbm,
    wv_hbm,
    wo_hbm,
    wt_hbm,
    bias_hbm,
    start_hbm,
    token_hbm,
    cots_hbm,
    ctok_hbm,
    state_out_hbm,
    rows_out_hbm,
    grad_out_hbm,
    late_out_hbm,
    early_out_hbm,
    gain_ref,
    start_ref,
    token_ref,
    state,
    w3,
    wo,
    wt,
    bias,
    cots,
    ctok,
    ctok_low,
    halo,
    unit,
    inverse,
    normed,
    queries,
    kvf,
    kvw,
    probs,
    attended,
    state_out,
    sel_cat,
    sel_t,
    sel_tlow,
    tokens_back,
    inv_own,
    silu,
    active,
    state_back,
    attended_back,
    low_part,
    high_part,
    rows_out,
    shift,
    spread,
    query_back,
    spread_low,
    nback,
    nback_send,
    nback_recv,
    grad_out,
    e_src,
    e_rx1,
    e_sum,
    e_rx2,
    e_fin,
    l_src,
    l_rx1,
    l_sum,
    l_rx2,
    l_fin,
    head_mask,
    mean_mat,
    load_sem,
    out_sem,
    send_sem,
    recv_sem,
):
    A, B, rows, channels, windows, heads, qw, keys, toks, width = sizes
    margin = keys // 2 + qw // 2
    full = rows + 2 * margin
    span = keys + 2 * qw
    head_dim = channels // heads
    factor = head_dim ** (-0.5)
    fold = 2 * channels // A
    half = channels // A
    me = lax.axis_index("atom")
    smp = lax.axis_index("sample")
    left = {"atom": lax.rem(me + A - 1, A)}
    right = {"atom": lax.rem(me + 1, A)}

    tile = rows // 128
    below = pl.multiple_of(jnp.maximum(me - 1, 0) * tile, 8)
    above = pl.multiple_of(jnp.minimum(me + 1, A - 1) * tile, 8)

    def load(src, dst, index):
        return pltpu.make_async_copy(src, dst, load_sem.at[index])

    loads = [
        load(state_hbm.at[0], state, 0),
        load(wq_hbm, w3.at[:, pl.ds(0, channels)], 1),
        load(wk_hbm, w3.at[:, pl.ds(channels, channels)], 2),
        load(wv_hbm, w3.at[:, pl.ds(2 * channels, channels)], 3),
        load(bias_hbm, bias, 4),
        load(wo_hbm, wo, 5),
        load(wt_hbm, wt, 6),
        load(cots_hbm.at[0], cots, 7),
        load(ctok_hbm.at[0], ctok, 8),
        load(gain_hbm, gain_ref, 9),
        load(start_hbm, start_ref, 10),
        load(token_hbm.at[pl.ds(below, tile)], token_ref.at[pl.ds(0, tile)], 11),
        load(token_hbm.at[pl.ds(pl.multiple_of(me * tile, 8), tile)], token_ref.at[pl.ds(tile, tile)], 12),
        load(token_hbm.at[pl.ds(above, tile)], token_ref.at[pl.ds(2 * tile, tile)], 13),
    ]
    barrier = pltpu.get_barrier_semaphore()

    def greet(d, _):
        pl.semaphore_signal(
            barrier, inc=1, device_id={"atom": lax.rem(me + d, A)}, device_id_type=MESH
        )
        return 0

    def greet_sample(d, _):
        pl.semaphore_signal(
            barrier, inc=1, device_id={"sample": lax.rem(smp + d, B)}, device_id_type=MESH
        )
        return 0

    lax.fori_loop(1, A, greet, 0)
    lax.fori_loop(1, B, greet_sample, 0)

    for copy in loads:
        copy.start()

    def send(src, dst, index, device):
        return pltpu.make_async_remote_copy(
            src_ref=src,
            dst_ref=dst,
            send_sem=send_sem.at[index],
            recv_sem=recv_sem.at[index],
            device_id=device,
            device_id_type=MESH,
        )

    def wait_bytes(ref, sem):
        pltpu.make_async_copy(ref, ref, sem).wait()

    def norm(x):
        average = nn(x, mean_mat[pl.ds(0, channels), pl.ds(0, channels)])
        centred = x.astype(f32) - average
        square = (centred * centred).astype(bf16)
        variance = nn(square, mean_mat[pl.ds(0, channels), pl.ds(0, channels)])
        inv = lax.rsqrt(variance + norm_eps)
        unit_rows = centred * inv
        return unit_rows, inv, (unit_rows * gain_ref[...]).astype(bf16)

    for index in (0, 1, 2, 3, 9):
        loads[index].wait()

    lanes = lax.broadcasted_iota(jnp.int32, (keys, channels), 1)
    subs = lax.broadcasted_iota(jnp.int32, (keys, channels), 0)
    mean_mat[...] = jnp.zeros((2 * channels, 2 * channels), bf16)
    mean_mat[pl.ds(0, channels), pl.ds(0, channels)] = jnp.full(
        (channels, channels), 1.0 / channels, bf16
    )
    mean_mat[pl.ds(channels, channels), pl.ds(channels, channels)] = jnp.full(
        (channels, channels), 1.0 / channels, bf16
    )
    kvw[:, :, pl.ds(2 * channels, channels)] = jnp.ones((windows, keys, channels), bf16)
    head_mask[...] = jnp.where(subs // qw == lanes // head_dim, 1.0, 0.0).astype(bf16)

    block = 256
    group = 8

    def project(c, _):
        r = pl.multiple_of(c * block, block)
        unit_rows, inv, low = norm(state[pl.ds(r, block), :])
        unit[pl.ds(margin + r, block), :] = unit_rows
        inverse[pl.ds(r, block), :] = inv
        normed[pl.ds(margin + r, block), :] = low
        qkv = nn(low, w3[...]).astype(bf16)
        queries[pl.ds(r, block), :] = qkv[:, :channels]
        kvf[0, pl.ds(margin + r, block), :] = qkv[:, channels : 2 * channels].astype(f32)
        kvf[1, pl.ds(margin + r, block), :] = qkv[:, 2 * channels :].astype(f32)
        return 0

    lax.fori_loop(0, rows // block, project, 0)

    pl.semaphore_wait(barrier, A + B - 2)

    halo_left = send(
        state_hbm.at[0, pl.ds(rows - margin, margin), :], halo.at[0], 0, right
    )
    halo_right = send(state_hbm.at[0, pl.ds(0, margin), :], halo.at[1], 1, left)
    tokens_up = send(ctok_hbm.at[0], ctok_low, 2, right)
    halo_left.start()
    halo_right.start()
    tokens_up.start()

    spread[...] = jnp.zeros((2, full, channels), f32)
    for slot in range(2 * group):
        shift[slot, pl.ds(0, 2 * qw), :] = jnp.zeros((2 * qw, channels), f32)
        shift[slot, pl.ds(2 * qw + keys, 2 * qw), :] = jnp.zeros((2 * qw, channels), f32)

    for index in (11, 12, 13):
        loads[index].wait()
    base = (me * toks).astype(f32)
    lower = base - toks
    sub_id = subs.astype(f32)
    lane_id = lanes.astype(f32)
    count_own = jnp.zeros((toks, 128), f32)
    count_low = jnp.zeros((toks, 128), f32)
    for r in range(tile):
        row = token_ref[pl.ds(tile + r, 1), :].astype(f32)
        spot = jnp.broadcast_to(row, (128, 128))
        hit = jnp.where(spot - base == sub_id, 1.0, 0.0)
        count_own = count_own + hit
        sel_t[:, pl.ds(r * 128, 128)] = hit.astype(bf16)
        if r < 2:
            hit = jnp.where(spot - lower == sub_id, 1.0, 0.0)
            count_low = count_low + hit
            sel_tlow[:, pl.ds(r * 128, 128)] = hit.astype(bf16)
        column = (spot - lower).astype(bf16).T.astype(f32)
        sel_cat[pl.ds(r * 128, 128), pl.ds(0, 128)] = jnp.where(
            column == lane_id, 1.0, 0.0
        ).astype(bf16)
        sel_cat[pl.ds(r * 128, 128), pl.ds(128, 128)] = jnp.where(
            column == lane_id + toks, 1.0, 0.0
        ).astype(bf16)
    has_above = jnp.where(me < A - 1, 1.0, 0.0)
    for r in range(2):
        row = token_ref[pl.ds(2 * tile + r, 1), :].astype(f32)
        spot = jnp.broadcast_to(row, (128, 128))
        count_own = count_own + jnp.where(spot - base == sub_id, has_above, 0.0)
    has_below = jnp.where(me > 0, 1.0, 0.0)
    for r in range(tile):
        row = token_ref[pl.ds(r, 1), :].astype(f32)
        spot = jnp.broadcast_to(row, (128, 128))
        count_low = count_low + jnp.where(spot - lower == sub_id, has_below, 0.0)

    def inverted(count):
        total = jnp.sum(count, axis=-1, keepdims=True)
        return jnp.where(total > 0.0, 1.0 / jnp.maximum(total, 1.0), 0.0)

    inverse_own = inverted(count_own)
    inverse_low = inverted(count_low)
    inv_own[...] = jnp.broadcast_to(inverse_own, (toks, 128))
    loads[8].wait()
    tokens_back[pl.ds(toks, toks), :] = (ctok[...].astype(f32) * inverse_own).astype(bf16)

    first_atom = me * rows
    last_base = A * rows - span

    def spread_heads(x):
        return jnp.concatenate([x] * heads, axis=0) * head_mask[...]

    def gather_heads(x):
        lane = lax.broadcasted_iota(jnp.int32, (qw, channels), 1)
        out = x[0:qw]
        for h in range(1, heads):
            out = jnp.where(lane >= h * head_dim, x[h * qw : (h + 1) * qw], out)
        return out

    def forward(w):
        place = jnp.clip(start_ref[w] - first_atom + margin, 0, full - keys)
        k = kvf[0, pl.ds(place, keys), :].astype(bf16)
        v = kvf[1, pl.ds(place, keys), :].astype(bf16)
        kvw[w, :, pl.ds(0, channels)] = k
        kvw[w, :, pl.ds(channels, channels)] = v
        q0 = pl.multiple_of(w * qw, qw)
        q = spread_heads(queries[pl.ds(q0, qw), :])
        s = nt(q, k) * factor + bias[w]
        e = jnp.exp(s - jnp.max(s, axis=-1, keepdims=True))
        mixed = nn(e.astype(bf16), kvw[w, :, pl.ds(channels, 2 * channels)])
        scale = 1.0 / mixed[:, channels:]
        probs[w] = (e * scale).astype(bf16)
        attended[pl.ds(q0, qw), :] = gather_heads(mixed[:, :channels] * scale).astype(bf16)

    near = group // 2
    loads[4].wait()
    loads[10].wait()

    def forward_group(i, _):
        for k in range(group):
            forward(lax.rem(group * i + k + near, windows))
        return 0

    inner = windows // group - 1
    lax.fori_loop(0, inner, forward_group, 0)

    halo_left.wait_recv()
    halo_right.wait_recv()
    for side in range(2):
        there = (me > 0) if side == 0 else (me < A - 1)
        at = 0 if side == 0 else margin + rows
        keep = jnp.where(there, 1.0, 0.0)
        x = jnp.where(jnp.full((margin, channels), keep) > 0.0, halo[side].astype(f32), 0.0)
        unit_rows, _, low = norm(x.astype(bf16))
        unit[pl.ds(at, margin), :] = unit_rows
        normed[pl.ds(at, margin), :] = low
        kv = nn(low, w3[:, channels:]).astype(bf16).astype(f32)
        kvf[0, pl.ds(at, margin), :] = kv[:, :channels]
        kvf[1, pl.ds(at, margin), :] = kv[:, channels:]

    lax.fori_loop(inner, inner + 1, forward_group, 0)

    tokens_up.wait_recv()
    tokens_back[pl.ds(0, toks), :] = (ctok_low[...].astype(f32) * inverse_low).astype(bf16)
    for index in range(5, 8):
        loads[index].wait()

    def token_part(c):
        r = c * block if isinstance(c, int) else pl.multiple_of(c * block, block)
        here = pl.ds(r, block)
        out = (state[here, :].astype(f32) + nn(attended[here, :], wo[...])).astype(bf16)
        state_out[here, :] = out
        before = nn(out, wt[...])
        sigma = 0.5 * jnp.tanh(0.5 * before) + 0.5
        act = before * sigma
        silu[here, :] = act.astype(bf16)
        slope = sigma + act - act * sigma
        per_atom = nn(sel_cat[here, :], tokens_back[...])
        back = (per_atom * slope).astype(bf16)
        active[here, :] = back
        sback = (cots[here, :].astype(f32) + nt(back, wt[...])).astype(bf16)
        state_back[here, :] = sback
        aback = nt(sback, wo[...]).astype(bf16)
        attended_back[here, pl.ds(0, channels)] = aback
        attended_back[here, pl.ds(channels, channels)] = (
            -aback.astype(f32) * attended[here, :].astype(f32)
        ).astype(bf16)

    token_part(0)
    low_part[...] = nn(sel_tlow[...], silu[pl.ds(0, 256), :]).astype(bf16)
    part_down = send(low_part, high_part, 3, left)
    part_down.start()
    lax.fori_loop(1, rows // block, lambda c, _: (token_part(c), 0)[1], 0)

    def store(src, dst, index):
        return pltpu.make_async_copy(src, dst, out_sem.at[index])

    out_state = store(state_out, state_out_hbm.at[0], 0)
    out_state.start()

    def folded(x):
        x = x.reshape(A, half, x.shape[-1])
        mid = x.shape[-1] // 2
        return jnp.concatenate([x[..., :mid], x[..., mid:]], axis=1)

    def stacked(x, y):
        return jnp.concatenate(
            [x.reshape(A, half, channels), y.reshape(A, half, channels)], axis=1
        )

    token_sum = tn(state_out[...], active[...])
    e_src[:, :, pl.ds(0, width // 2)] = folded(token_sum).astype(bf16)
    output_sum = tn(attended[...], state_back[...])
    output_high = output_sum.astype(bf16).astype(f32)
    e_src[:, :, pl.ds(width // 2, channels)] = stacked(
        output_high, output_sum - output_high
    ).astype(bf16)

    def scatter(src, rx, index):
        def one(d, _):
            peer = lax.rem(me + d, A)
            send(src.at[peer], rx.at[d], index, {"atom": peer}).start()
            return 0

        lax.fori_loop(1, A, one, 0)

    def scattered(src, rx, part, rx2, index):
        wait_bytes(rx.at[pl.ds(1, A - 1)], recv_sem.at[index])
        total = src[me].astype(f32)
        for d in range(1, A):
            total = total + rx[d].astype(f32)
        low = total.astype(bf16)
        part[...] = low
        rx2[smp] = low

    def exchange(part, rx2, index):
        def one(d, _):
            peer = lax.rem(smp + d, B)
            send(part, rx2.at[smp], index, {"sample": peer}).start()
            return 0

        lax.fori_loop(1, B, one, 0)

    def exchanged(rx2, fin, index):
        wait_bytes(rx2.at[pl.ds(0, B - 1)], recv_sem.at[index])
        total = rx2[0].astype(f32)
        for d in range(1, B):
            total = total + rx2[d].astype(f32)
        fin[me] = total.astype(bf16)

    def gather(fin, index):
        def one(d, _):
            peer = lax.rem(me + d, A)
            send(fin.at[me], fin.at[me], index, {"atom": peer}).start()
            return 0

        lax.fori_loop(1, A, one, 0)

    def gathered(fin, index):
        wait_bytes(fin.at[pl.ds(0, A - 1)], recv_sem.at[index])

    scatter(e_src, e_rx1, 4)

    def backward(w, slot):
        base_atom = jnp.clip(first_atom + w * qw - margin, 0, last_base)
        off = jnp.clip(start_ref[w] - base_atom, 0, 2 * qw)
        kv = kvw[w]
        q0 = pl.multiple_of(w * qw, qw)
        q = spread_heads(queries[pl.ds(q0, qw), :])
        da = spread_heads(attended_back[pl.ds(q0, qw), pl.ds(0, channels)])
        delta = spread_heads(attended_back[pl.ds(q0, qw), pl.ds(channels, channels)])
        p = probs[w]
        centred = nt(jnp.concatenate([da, delta], axis=1), kv[:, channels:])
        ds = (p.astype(f32) * centred).astype(bf16)
        dq = gather_heads(nn(ds, kv[:, :channels]))
        query_back[pl.ds(q0, qw), :] = (dq * factor).astype(bf16)
        to = pl.ds(pl.multiple_of(base_atom - first_atom + margin, 16), span)
        for part, rows_back in enumerate((tn(ds, q) * factor, tn(p, da))):
            shift[2 * slot + part, pl.ds(2 * qw, keys), :] = rows_back
            moved = shift[2 * slot + part, pl.ds(2 * qw - off, span), :]
            spread[part, to, :] = spread[part, to, :] + moved

    def backward_group(i, _):
        for k in range(group):
            backward(group * i + k, k)
        return 0

    lax.fori_loop(0, windows // group // 2, backward_group, 0)
    scattered(e_src, e_rx1, e_sum, e_rx2, 4)
    exchange(e_sum, e_rx2, 5)
    lax.fori_loop(windows // group // 2, windows // group, backward_group, 0)
    exchanged(e_rx2, e_fin, 5)
    gather(e_fin, 6)

    spread_low[:, pl.ds(0, channels)] = spread[0].astype(bf16)
    spread_low[:, pl.ds(channels, channels)] = spread[1].astype(bf16)
    nback[...] = nt(spread_low[...], w3[:, channels:])
    nback_send[0] = nback[pl.ds(0, margin), :].astype(bf16)
    nback_send[1] = nback[pl.ds(margin + rows, margin), :].astype(bf16)
    back_left = send(nback_send.at[0], nback_recv.at[1], 7, left)
    back_right = send(nback_send.at[1], nback_recv.at[0], 8, right)
    back_left.start()
    back_right.start()
    own = pl.ds(margin, rows)
    nback[own, :] = nback[own, :] + nt(query_back[...], w3[:, :channels])
    query_sum = tn(normed[own, :], query_back[...])
    pair_sum = tn(normed[...], spread_low[...])
    gain_part = jnp.sum((unit[...] * nback[...]).reshape(full // 8, 8, channels), axis=0)
    gain_rows = jnp.concatenate([gain_part, jnp.zeros((channels - 8, channels), f32)], axis=0)
    l_src[:, :, pl.ds(0, channels)] = stacked(query_sum, pair_sum[:, :channels]).astype(bf16)
    l_src[:, :, pl.ds(channels, channels)] = stacked(pair_sum[:, channels:], gain_rows).astype(
        bf16
    )
    scatter(l_src, l_rx1, 9)

    part_down.wait_recv()
    own_part = nn(sel_t[...], silu[...])
    rows_out[...] = (
        (own_part + high_part[...].astype(f32)) * inv_own[:, pl.ds(0, 1)]
    ).astype(bf16)
    out_rows = store(rows_out, rows_out_hbm.at[0], 1)
    out_rows.start()

    def norm_back(r, count, extra):
        here = pl.ds(r, count)
        there = pl.ds(margin + r, count)
        nb = nback[there, :]
        if extra is not None:
            nb = nb + extra
        ub = nb * gain_ref[...]
        un = unit[there, :]
        means = nn(jnp.concatenate([ub, ub * un], axis=1).astype(bf16), mean_mat[...])
        grad_out[here, :] = state_back[here, :].astype(f32) + inverse[here, :] * (
            ub - means[:, :channels] - un * means[:, channels:]
        )

    for r in range(0, rows - 2 * margin, 288):
        norm_back(margin + r, min(288, rows - 2 * margin - r), None)
    back_left.wait_recv()
    back_right.wait_recv()
    norm_back(0, margin, nback_recv[0].astype(f32))
    norm_back(rows - margin, margin, nback_recv[1].astype(f32))
    out_grad = store(grad_out, grad_out_hbm.at[0], 2)
    out_grad.start()

    scattered(l_src, l_rx1, l_sum, l_rx2, 9)
    exchange(l_sum, l_rx2, 10)
    gathered(e_fin, 6)
    out_early = store(e_fin, early_out_hbm, 3)
    out_early.start()
    exchanged(l_rx2, l_fin, 10)
    gather(l_fin, 11)
    gathered(l_fin, 11)
    out_late = store(l_fin, late_out_hbm, 4)
    out_late.start()

    for copy in (halo_left, halo_right, tokens_up, part_down, back_left, back_right):
        copy.wait_send()
    for index, ref, count in (
        (4, e_rx1, A),
        (5, e_rx2, B),
        (6, e_fin, A),
        (9, l_rx1, A),
        (10, l_rx2, B),
        (11, l_fin, A),
    ):
        wait_bytes(ref.at[pl.ds(0, count - 1)], send_sem.at[index])
    for copy in (out_state, out_rows, out_grad, out_early, out_late):
        copy.wait()


def finish(
    scale,
    state_hbm,
    rows_hbm,
    grad_hbm,
    late_hbm,
    early_hbm,
    state_out,
    rows_out,
    grad_out,
    gain_out,
    query_out,
    key_out,
    value_out,
    output_out,
    token_out,
    grad,
    state,
    token_rows,
    late,
    early,
    gain,
    square,
    token,
    in_sem,
    out_sem,
):
    A, fold, wide = early.shape
    half = fold // 2
    channels = A * half
    width = token.shape[1]
    get_late = pltpu.make_async_copy(late_hbm, late, in_sem.at[0])
    get_early = pltpu.make_async_copy(early_hbm, early, in_sem.at[1])
    get_early.start()
    get_late.start()
    gets = [
        pltpu.make_async_copy(src, dst, in_sem.at[2 + index])
        for index, (src, dst) in enumerate(
            ((grad_hbm, grad), (state_hbm, state), (rows_hbm, token_rows))
        )
    ]
    for get in gets:
        get.start()
    puts = []

    def put(src, dst, index):
        copy = pltpu.make_async_copy(src, dst, out_sem.at[index])
        copy.start()
        puts.append(copy)

    for index, (src, dst) in enumerate(
        ((grad, grad_out), (state, state_out), (token_rows, rows_out))
    ):
        gets[index].wait()
        put(src, dst, index)
    get_early.wait()
    low = early[:, :half, :].astype(f32) * scale
    high = early[:, half:, :].astype(f32) * scale
    mid = width // 2
    token[:, pl.ds(0, mid)] = low[..., :mid].reshape(channels, mid)
    token[:, pl.ds(mid, mid)] = high[..., :mid].reshape(channels, mid)
    put(token, token_out, 3)
    square[3] = (low[..., mid:] + high[..., mid:]).reshape(channels, channels)
    put(square.at[3], output_out, 4)
    get_late.wait()
    low = late[:, :half, :].astype(f32) * scale
    high = late[:, half:, :].astype(f32) * scale
    square[0] = low[..., :channels].reshape(channels, channels)
    square[1] = high[..., :channels].reshape(channels, channels)
    square[2] = low[..., channels:].reshape(channels, channels)
    put(square.at[0], query_out, 5)
    put(square.at[1], key_out, 6)
    put(square.at[2], value_out, 7)
    gain[...] = jnp.sum(high[..., channels:].reshape(channels, channels), axis=0, keepdims=True)
    put(gain, gain_out, 8)
    for copy in puts:
        copy.wait()


def on_device(
    A,
    B,
    atom_state,
    norm_gain,
    query_weight,
    key_weight,
    value_weight,
    out_weight,
    token_weight,
    pair_bias,
    key_start,
    atom_token,
    cotangent_state,
    cotangent_tokens,
):
    _, rows, channels = atom_state.shape
    windows, heads, qw, keys = pair_bias.shape
    toks, width = cotangent_tokens.shape[1:]
    sizes = (A, B, rows, channels, windows, heads, qw, keys, toks, width)
    margin = keys // 2 + qw // 2
    full = rows + 2 * margin
    span = keys + 2 * qw
    fold = 2 * channels // A
    half = channels // A
    early = width // 2 + channels
    late = 2 * channels
    any_spec = pl.BlockSpec(memory_space=pltpu.HBM)
    V = pltpu.VMEM
    DMA = pltpu.SemaphoreType.DMA
    outs = pl.pallas_call(
        functools.partial(kernel, sizes),
        out_shape=(
            jax.ShapeDtypeStruct((1, rows, channels), bf16),
            jax.ShapeDtypeStruct((1, toks, width), bf16),
            jax.ShapeDtypeStruct((1, rows, channels), f32),
            jax.ShapeDtypeStruct((A, fold, late), bf16),
            jax.ShapeDtypeStruct((A, fold, early), bf16),
        ),
        in_specs=[any_spec] * 12,
        out_specs=(any_spec,) * 5,
        scratch_shapes=[
            V((1, channels), f32),
            pltpu.SMEM((windows,), jnp.int32),
            V((3 * rows // 128, 128), jnp.int32),
            V((rows, channels), bf16),
            V((channels, 3 * channels), bf16),
            V((channels, channels), bf16),
            V((channels, width), bf16),
            V((windows, heads * qw, keys), f32),
            V((rows, channels), bf16),
            V((toks, width), bf16),
            V((toks, width), bf16),
            V((2, margin, channels), bf16),
            V((full, channels), f32),
            V((rows, channels), f32),
            V((full, channels), bf16),
            V((rows, channels), bf16),
            V((2, full, channels), f32),
            V((windows, keys, 3 * channels), bf16),
            V((windows, heads * qw, keys), bf16),
            V((rows, channels), bf16),
            V((rows, channels), bf16),
            V((rows, 2 * toks), bf16),
            V((toks, rows), bf16),
            V((toks, 256), bf16),
            V((2 * toks, width), bf16),
            V((toks, 128), f32),
            V((rows, width), bf16),
            V((rows, width), bf16),
            V((rows, channels), bf16),
            V((rows, 2 * channels), bf16),
            V((toks, width), bf16),
            V((toks, width), bf16),
            V((toks, width), bf16),
            V((16, keys + 4 * qw, channels), f32),
            V((2, full, channels), f32),
            V((rows, channels), bf16),
            V((full, 2 * channels), bf16),
            V((full, channels), f32),
            V((2, margin, channels), bf16),
            V((2, margin, channels), bf16),
            V((rows, channels), f32),
            V((A, fold, early), bf16),
            V((A, fold, early), bf16),
            V((fold, early), bf16),
            V((B, fold, early), bf16),
            V((A, fold, early), bf16),
            V((A, fold, late), bf16),
            V((A, fold, late), bf16),
            V((fold, late), bf16),
            V((B, fold, late), bf16),
            V((A, fold, late), bf16),
            V((keys, channels), bf16),
            V((2 * channels, 2 * channels), bf16),
            DMA((14,)),
            DMA((5,)),
            DMA((12,)),
            DMA((12,)),
        ],
        compiler_params=pltpu.CompilerParams(
            collective_id=0, has_side_effects=True, vmem_limit_bytes=62 * 1024 * 1024
        ),
        name="atom_block",
    )(
        atom_state,
        norm_gain.reshape(1, channels),
        query_weight,
        key_weight,
        value_weight,
        out_weight,
        token_weight,
        pair_bias.reshape(windows, heads * qw, keys),
        key_start,
        atom_token.reshape(-1, 128),
        cotangent_state,
        cotangent_tokens,
    )
    rescale = 1.0 / math.sqrt(B * A * rows)
    square = jax.ShapeDtypeStruct((channels, channels), f32)
    done = pl.pallas_call(
        functools.partial(finish, rescale),
        out_shape=(
            jax.ShapeDtypeStruct((1, rows, channels), bf16),
            jax.ShapeDtypeStruct((1, toks, width), bf16),
            jax.ShapeDtypeStruct((1, rows, channels), f32),
            jax.ShapeDtypeStruct((1, channels), f32),
            square,
            square,
            square,
            square,
            jax.ShapeDtypeStruct((channels, width), f32),
        ),
        in_specs=[any_spec] * 5,
        out_specs=(any_spec,) * 9,
        scratch_shapes=[
            V((1, rows, channels), f32),
            V((1, rows, channels), bf16),
            V((1, toks, width), bf16),
            V((A, fold, late), bf16),
            V((A, fold, early), bf16),
            V((1, channels), f32),
            V((4, channels, channels), f32),
            V((channels, width), f32),
            DMA((5,)),
            DMA((9,)),
        ],
        compiler_params=pltpu.CompilerParams(vmem_limit_bytes=62 * 1024 * 1024),
        name="finish",
    )(*outs)
    return done[:3] + (done[3].reshape(channels),) + done[4:]


def solution(mesh):
    return jax.shard_map(
        functools.partial(on_device, mesh.shape["atom"], mesh.shape["sample"]),
        mesh=mesh,
        in_specs=(
            P("sample", "atom", None),
            P(),
            P(),
            P(),
            P(),
            P(),
            P(),
            P("atom", None, None, None),
            P("atom"),
            P(),
            P("sample", "atom", None),
            P("sample", "atom", None),
        ),
        out_specs=(
            P("sample", "atom", None),
            P("sample", "atom", None),
            P("sample", "atom", None),
            P(),
            P(),
            P(),
            P(),
            P(),
            P(),
        ),
        check_vma=False,
    )
```

```python
import functools
import math

import jax
import jax.numpy as jnp
from jax import lax
from jax.experimental import pallas as pl
from jax.experimental.pallas import tpu as pltpu
from jax.sharding import PartitionSpec as P

MESH = pl.DeviceIdType.MESH
norm_eps = 1e-05
f32 = jnp.float32
bf16 = jnp.bfloat16


def nn(a, b):
    return lax.dot_general(a, b, (((1,), (0,)), ((), ())), preferred_element_type=f32)


def nt(a, b):
    return lax.dot_general(a, b, (((1,), (1,)), ((), ())), preferred_element_type=f32)


def tn(a, b):
    return lax.dot_general(a, b, (((0,), (0,)), ((), ())), preferred_element_type=f32)


def kernel(
    sizes,
    state_hbm,
    gain_hbm,
    wq_hbm,
    wk_hbm,
    wv_hbm,
    wo_hbm,
    wt_hbm,
    bias_hbm,
    start_hbm,
    token_hbm,
    cots_hbm,
    ctok_hbm,
    state_out_hbm,
    rows_out_hbm,
    grad_out_hbm,
    late_out_hbm,
    early_out_hbm,
    gain_ref,
    start_ref,
    token_ref,
    state,
    w3,
    wo,
    wt,
    bias,
    cots,
    ctok,
    ctok_low,
    halo,
    unit,
    inverse,
    normed,
    queries,
    kvf,
    kvw,
    probs,
    attended,
    state_out,
    sel_cat,
    sel_t,
    sel_tlow,
    tokens_back,
    inv_own,
    silu,
    active,
    state_back,
    attended_back,
    low_part,
    high_part,
    rows_out,
    shift,
    spread,
    query_back,
    spread_low,
    nback,
    nback_send,
    nback_recv,
    grad_out,
    e_src,
    e_rx1,
    e_sum,
    e_rx2,
    e_fin,
    l_src,
    l_rx1,
    l_sum,
    l_rx2,
    l_fin,
    head_mask,
    mean_mat,
    load_sem,
    out_sem,
    send_sem,
    recv_sem,
):
    A, B, planes, rows, channels, windows, heads, qw, keys, toks, width = sizes
    margin = keys // 2 + qw // 2
    full = rows + 2 * margin
    span = keys + 2 * qw
    head_dim = channels // heads
    factor = head_dim ** (-0.5)
    G = A * planes
    Z = B // planes
    half = 2 * channels // G
    me = lax.axis_index("atom")
    smp = lax.axis_index("sample")
    left = {"atom": lax.rem(me + A - 1, A)}
    right = {"atom": lax.rem(me + 1, A)}

    tile = rows // 128
    below = pl.multiple_of(jnp.maximum(me - 1, 0) * tile, 8)
    above = pl.multiple_of(jnp.minimum(me + 1, A - 1) * tile, 8)

    def load(src, dst, index):
        return pltpu.make_async_copy(src, dst, load_sem.at[index])

    loads = [
        load(state_hbm.at[0], state, 0),
        load(wq_hbm, w3.at[:, pl.ds(0, channels)], 1),
        load(wk_hbm, w3.at[:, pl.ds(channels, channels)], 2),
        load(wv_hbm, w3.at[:, pl.ds(2 * channels, channels)], 3),
        load(bias_hbm, bias, 4),
        load(wo_hbm, wo, 5),
        load(wt_hbm, wt, 6),
        load(cots_hbm.at[0], cots, 7),
        load(ctok_hbm.at[0], ctok, 8),
        load(gain_hbm, gain_ref, 9),
        load(start_hbm, start_ref, 10),
        load(token_hbm.at[pl.ds(below, tile)], token_ref.at[pl.ds(0, tile)], 11),
        load(token_hbm.at[pl.ds(pl.multiple_of(me * tile, 8), tile)], token_ref.at[pl.ds(tile, tile)], 12),
        load(token_hbm.at[pl.ds(above, tile)], token_ref.at[pl.ds(2 * tile, tile)], 13),
    ]
    barrier = pltpu.get_barrier_semaphore()

    rank = lax.div(smp, Z) * A + me
    depth = lax.rem(smp, Z)

    def plane_peer(p):
        return {"sample": lax.div(p, A) * Z + depth, "atom": lax.rem(p, A)}

    def line_peer(q):
        return {"sample": lax.div(smp, Z) * Z + q}

    def greet(d, _):
        pl.semaphore_signal(
            barrier, inc=1, device_id=plane_peer(lax.rem(rank + d, G)), device_id_type=MESH
        )
        return 0

    def greet_line(d, _):
        pl.semaphore_signal(
            barrier, inc=1, device_id=line_peer(lax.rem(depth + d, Z)), device_id_type=MESH
        )
        return 0

    lax.fori_loop(1, G, greet, 0)
    lax.fori_loop(1, Z, greet_line, 0)

    for copy in loads:
        copy.start()

    def send(src, dst, index, device):
        return pltpu.make_async_remote_copy(
            src_ref=src,
            dst_ref=dst,
            send_sem=send_sem.at[index],
            recv_sem=recv_sem.at[index],
            device_id=device,
            device_id_type=MESH,
        )

    def wait_bytes(ref, sem):
        pltpu.make_async_copy(ref, ref, sem).wait()

    def norm(x):
        average = nn(x, mean_mat[pl.ds(0, channels), pl.ds(0, channels)])
        centred = x.astype(f32) - average
        square = (centred * centred).astype(bf16)
        variance = nn(square, mean_mat[pl.ds(0, channels), pl.ds(0, channels)])
        inv = lax.rsqrt(variance + norm_eps)
        unit_rows = centred * inv
        return unit_rows, inv, (unit_rows * gain_ref[...]).astype(bf16)

    for index in (0, 1, 2, 3, 9):
        loads[index].wait()

    lanes = lax.broadcasted_iota(jnp.int32, (keys, channels), 1)
    subs = lax.broadcasted_iota(jnp.int32, (keys, channels), 0)
    mean_mat[...] = jnp.zeros((2 * channels, 2 * channels), bf16)
    mean_mat[pl.ds(0, channels), pl.ds(0, channels)] = jnp.full(
        (channels, channels), 1.0 / channels, bf16
    )
    mean_mat[pl.ds(channels, channels), pl.ds(channels, channels)] = jnp.full(
        (channels, channels), 1.0 / channels, bf16
    )
    kvw[:, :, pl.ds(2 * channels, channels)] = jnp.ones((windows, keys, channels), bf16)
    head_mask[...] = jnp.where(subs // qw == lanes // head_dim, 1.0, 0.0).astype(bf16)

    block = 256
    group = 8

    def project(c, _):
        r = pl.multiple_of(c * block, block)
        unit_rows, inv, low = norm(state[pl.ds(r, block), :])
        unit[pl.ds(margin + r, block), :] = unit_rows
        inverse[pl.ds(r, block), :] = inv
        normed[pl.ds(margin + r, block), :] = low
        qkv = nn(low, w3[...]).astype(bf16)
        queries[pl.ds(r, block), :] = qkv[:, :channels]
        kvf[0, pl.ds(margin + r, block), :] = qkv[:, channels : 2 * channels].astype(f32)
        kvf[1, pl.ds(margin + r, block), :] = qkv[:, 2 * channels :].astype(f32)
        return 0

    lax.fori_loop(0, rows // block, project, 0)

    pl.semaphore_wait(barrier, G + Z - 2)

    halo_left = send(
        state_hbm.at[0, pl.ds(rows - margin, margin), :], halo.at[0], 0, right
    )
    halo_right = send(state_hbm.at[0, pl.ds(0, margin), :], halo.at[1], 1, left)
    tokens_up = send(ctok_hbm.at[0], ctok_low, 2, right)
    halo_left.start()
    halo_right.start()
    tokens_up.start()

    spread[...] = jnp.zeros((2, full, channels), f32)
    for slot in range(2 * group):
        shift[slot, pl.ds(0, 2 * qw), :] = jnp.zeros((2 * qw, channels), f32)
        shift[slot, pl.ds(2 * qw + keys, 2 * qw), :] = jnp.zeros((2 * qw, channels), f32)

    for index in (11, 12, 13):
        loads[index].wait()
    base = (me * toks).astype(f32)
    lower = base - toks
    sub_id = subs.astype(f32)
    lane_id = lanes.astype(f32)
    count_own = jnp.zeros((toks, 128), f32)
    count_low = jnp.zeros((toks, 128), f32)
    for r in range(tile):
        row = token_ref[pl.ds(tile + r, 1), :].astype(f32)
        spot = jnp.broadcast_to(row, (128, 128))
        hit = jnp.where(spot - base == sub_id, 1.0, 0.0)
        count_own = count_own + hit
        sel_t[:, pl.ds(r * 128, 128)] = hit.astype(bf16)
        if r < 2:
            hit = jnp.where(spot - lower == sub_id, 1.0, 0.0)
            count_low = count_low + hit
            sel_tlow[:, pl.ds(r * 128, 128)] = hit.astype(bf16)
        column = (spot - lower).astype(bf16).T.astype(f32)
        sel_cat[pl.ds(r * 128, 128), pl.ds(0, 128)] = jnp.where(
            column == lane_id, 1.0, 0.0
        ).astype(bf16)
        sel_cat[pl.ds(r * 128, 128), pl.ds(128, 128)] = jnp.where(
            column == lane_id + toks, 1.0, 0.0
        ).astype(bf16)
    has_above = jnp.where(me < A - 1, 1.0, 0.0)
    for r in range(2):
        row = token_ref[pl.ds(2 * tile + r, 1), :].astype(f32)
        spot = jnp.broadcast_to(row, (128, 128))
        count_own = count_own + jnp.where(spot - base == sub_id, has_above, 0.0)
    has_below = jnp.where(me > 0, 1.0, 0.0)
    for r in range(tile):
        row = token_ref[pl.ds(r, 1), :].astype(f32)
        spot = jnp.broadcast_to(row, (128, 128))
        count_low = count_low + jnp.where(spot - lower == sub_id, has_below, 0.0)

    def inverted(count):
        total = jnp.sum(count, axis=-1, keepdims=True)
        return jnp.where(total > 0.0, 1.0 / jnp.maximum(total, 1.0), 0.0)

    inverse_own = inverted(count_own)
    inverse_low = inverted(count_low)
    inv_own[...] = jnp.broadcast_to(inverse_own, (toks, 128))
    loads[8].wait()
    tokens_back[pl.ds(toks, toks), :] = (ctok[...].astype(f32) * inverse_own).astype(bf16)

    first_atom = me * rows
    last_base = A * rows - span

    def spread_heads(x):
        return jnp.concatenate([x] * heads, axis=0) * head_mask[...]

    def gather_heads(x):
        lane = lax.broadcasted_iota(jnp.int32, (qw, channels), 1)
        out = x[0:qw]
        for h in range(1, heads):
            out = jnp.where(lane >= h * head_dim, x[h * qw : (h + 1) * qw], out)
        return out

    def forward(w):
        place = jnp.clip(start_ref[w] - first_atom + margin, 0, full - keys)
        k = kvf[0, pl.ds(place, keys), :].astype(bf16)
        v = kvf[1, pl.ds(place, keys), :].astype(bf16)
        kvw[w, :, pl.ds(0, channels)] = k
        kvw[w, :, pl.ds(channels, channels)] = v
        q0 = pl.multiple_of(w * qw, qw)
        q = spread_heads(queries[pl.ds(q0, qw), :])
        s = nt(q, k) * factor + bias[w]
        e = jnp.exp(s - jnp.max(s, axis=-1, keepdims=True))
        mixed = nn(e.astype(bf16), kvw[w, :, pl.ds(channels, 2 * channels)])
        scale = 1.0 / mixed[:, channels:]
        probs[w] = (e * scale).astype(bf16)
        attended[pl.ds(q0, qw), :] = gather_heads(mixed[:, :channels] * scale).astype(bf16)

    near = group // 2
    loads[4].wait()
    loads[10].wait()

    def forward_group(i, _):
        for k in range(group):
            forward(lax.rem(group * i + k + near, windows))
        return 0

    inner = windows // group - 1
    lax.fori_loop(0, inner, forward_group, 0)

    halo_left.wait_recv()
    halo_right.wait_recv()
    for side in range(2):
        there = (me > 0) if side == 0 else (me < A - 1)
        at = 0 if side == 0 else margin + rows
        keep = jnp.where(there, 1.0, 0.0)
        x = jnp.where(jnp.full((margin, channels), keep) > 0.0, halo[side].astype(f32), 0.0)
        unit_rows, _, low = norm(x.astype(bf16))
        unit[pl.ds(at, margin), :] = unit_rows
        normed[pl.ds(at, margin), :] = low
        kv = nn(low, w3[:, channels:]).astype(bf16).astype(f32)
        kvf[0, pl.ds(at, margin), :] = kv[:, :channels]
        kvf[1, pl.ds(at, margin), :] = kv[:, channels:]

    lax.fori_loop(inner, inner + 1, forward_group, 0)

    tokens_up.wait_recv()
    tokens_back[pl.ds(0, toks), :] = (ctok_low[...].astype(f32) * inverse_low).astype(bf16)
    for index in range(5, 8):
        loads[index].wait()

    def token_part(c):
        r = c * block if isinstance(c, int) else pl.multiple_of(c * block, block)
        here = pl.ds(r, block)
        out = (state[here, :].astype(f32) + nn(attended[here, :], wo[...])).astype(bf16)
        state_out[here, :] = out
        before = nn(out, wt[...])
        sigma = 0.5 * jnp.tanh(0.5 * before) + 0.5
        act = before * sigma
        silu[here, :] = act.astype(bf16)
        slope = sigma + act - act * sigma
        per_atom = nn(sel_cat[here, :], tokens_back[...])
        back = (per_atom * slope).astype(bf16)
        active[here, :] = back
        sback = (cots[here, :].astype(f32) + nt(back, wt[...])).astype(bf16)
        state_back[here, :] = sback
        aback = nt(sback, wo[...]).astype(bf16)
        attended_back[here, pl.ds(0, channels)] = aback
        attended_back[here, pl.ds(channels, channels)] = (
            -aback.astype(f32) * attended[here, :].astype(f32)
        ).astype(bf16)

    token_part(0)
    low_part[...] = nn(sel_tlow[...], silu[pl.ds(0, 256), :]).astype(bf16)
    part_down = send(low_part, high_part, 3, left)
    part_down.start()
    lax.fori_loop(1, rows // block, lambda c, _: (token_part(c), 0)[1], 0)

    def store(src, dst, index):
        return pltpu.make_async_copy(src, dst, out_sem.at[index])

    out_state = store(state_out, state_out_hbm.at[0], 0)
    out_state.start()

    def stacked(x, y):
        return jnp.concatenate(
            [x.reshape(G // 2, half, channels), y.reshape(G // 2, half, channels)], axis=1
        ).astype(bf16)

    first, second = pl.ds(0, G // 2), pl.ds(G // 2, G // 2)

    token_sum = tn(state_out[...], active[...])
    pieces = [token_sum[:, c : c + channels] for c in range(0, width, channels)]
    output_sum = tn(attended[...], state_back[...])
    output_high = output_sum.astype(bf16).astype(f32)
    e_src[first, :, pl.ds(0, channels)] = stacked(pieces[0], pieces[1])
    e_src[first, :, pl.ds(channels, channels)] = stacked(pieces[2], pieces[3])
    e_src[second, :, pl.ds(0, channels)] = stacked(pieces[4], pieces[5])
    e_src[second, :, pl.ds(channels, channels)] = stacked(output_high, output_sum - output_high)

    def scatter(src, rx, index):
        def one(d, _):
            peer = lax.rem(rank + d, G)
            send(src.at[peer], rx.at[d], index, plane_peer(peer)).start()
            return 0

        lax.fori_loop(1, G, one, 0)

    def scattered(src, rx, part, rx2, index):
        wait_bytes(rx.at[pl.ds(1, G - 1)], recv_sem.at[index])
        total = src[rank].astype(f32)
        for d in range(1, G):
            total = total + rx[d].astype(f32)
        low = total.astype(bf16)
        part[...] = low
        rx2[depth] = low

    def exchange(part, rx2, index):
        def one(d, _):
            peer = lax.rem(depth + d, Z)
            send(part, rx2.at[depth], index, line_peer(peer)).start()
            return 0

        lax.fori_loop(1, Z, one, 0)

    def exchanged(rx2, fin, index):
        wait_bytes(rx2.at[pl.ds(0, Z - 1)], recv_sem.at[index])
        total = rx2[0].astype(f32)
        for d in range(1, Z):
            total = total + rx2[d].astype(f32)
        fin[rank] = total.astype(bf16)

    def gather(fin, index):
        def one(d, _):
            peer = lax.rem(rank + d, G)
            send(fin.at[rank], fin.at[rank], index, plane_peer(peer)).start()
            return 0

        lax.fori_loop(1, G, one, 0)

    def gathered(fin, index):
        wait_bytes(fin.at[pl.ds(0, G - 1)], recv_sem.at[index])

    scatter(e_src, e_rx1, 4)

    def backward(w, slot):
        base_atom = jnp.clip(first_atom + w * qw - margin, 0, last_base)
        off = jnp.clip(start_ref[w] - base_atom, 0, 2 * qw)
        kv = kvw[w]
        q0 = pl.multiple_of(w * qw, qw)
        q = spread_heads(queries[pl.ds(q0, qw), :])
        da = spread_heads(attended_back[pl.ds(q0, qw), pl.ds(0, channels)])
        delta = spread_heads(attended_back[pl.ds(q0, qw), pl.ds(channels, channels)])
        p = probs[w]
        centred = nt(jnp.concatenate([da, delta], axis=1), kv[:, channels:])
        ds = (p.astype(f32) * centred).astype(bf16)
        dq = gather_heads(nn(ds, kv[:, :channels]))
        query_back[pl.ds(q0, qw), :] = (dq * factor).astype(bf16)
        to = pl.ds(pl.multiple_of(base_atom - first_atom + margin, 16), span)
        for part, rows_back in enumerate((tn(ds, q) * factor, tn(p, da))):
            shift[2 * slot + part, pl.ds(2 * qw, keys), :] = rows_back
            moved = shift[2 * slot + part, pl.ds(2 * qw - off, span), :]
            spread[part, to, :] = spread[part, to, :] + moved

    def backward_group(i, _):
        for k in range(group):
            backward(group * i + k, k)
        return 0

    lax.fori_loop(0, windows // group, backward_group, 0)
    scattered(e_src, e_rx1, e_sum, e_rx2, 4)
    exchange(e_sum, e_rx2, 5)

    own = pl.ds(margin, rows)
    spread_low[:, pl.ds(0, channels)] = spread[0].astype(bf16)
    spread_low[:, pl.ds(channels, channels)] = spread[1].astype(bf16)
    query_sum = tn(normed[own, :], query_back[...])
    pair_sum = tn(normed[...], spread_low[...])
    weighted = (
        w3[:, :channels].astype(f32) * query_sum
        + w3[:, channels : 2 * channels].astype(f32) * pair_sum[:, :channels]
        + w3[:, 2 * channels :].astype(f32) * pair_sum[:, channels:]
    )
    gain_part = jnp.sum(weighted.T.reshape(channels // 8, 8, channels), axis=0) / gain_ref[...]
    gain_rows = jnp.concatenate([gain_part, jnp.zeros((channels - 8, channels), f32)], axis=0)
    l_src[first] = stacked(query_sum, pair_sum[:, :channels])
    l_src[second] = stacked(pair_sum[:, channels:], gain_rows)
    scatter(l_src, l_rx1, 9)

    nback[...] = nt(spread_low[...], w3[:, channels:])
    nback_send[0] = nback[pl.ds(0, margin), :].astype(bf16)
    nback_send[1] = nback[pl.ds(margin + rows, margin), :].astype(bf16)
    back_left = send(nback_send.at[0], nback_recv.at[1], 7, left)
    back_right = send(nback_send.at[1], nback_recv.at[0], 8, right)
    back_left.start()
    back_right.start()
    nback[own, :] = nback[own, :] + nt(query_back[...], w3[:, :channels])

    part_down.wait_recv()
    own_part = nn(sel_t[...], silu[...])
    rows_out[...] = (
        (own_part + high_part[...].astype(f32)) * inv_own[:, pl.ds(0, 1)]
    ).astype(bf16)
    out_rows = store(rows_out, rows_out_hbm.at[0], 1)
    out_rows.start()

    def norm_back(r, count, extra):
        here = pl.ds(r, count)
        there = pl.ds(margin + r, count)
        nb = nback[there, :]
        if extra is not None:
            nb = nb + extra
        ub = nb * gain_ref[...]
        un = unit[there, :]
        means = nn(jnp.concatenate([ub, ub * un], axis=1).astype(bf16), mean_mat[...])
        grad_out[here, :] = state_back[here, :].astype(f32) + inverse[here, :] * (
            ub - means[:, :channels] - un * means[:, channels:]
        )

    for r in range(0, rows - 2 * margin, 288):
        norm_back(margin + r, min(288, rows - 2 * margin - r), None)
    scattered(l_src, l_rx1, l_sum, l_rx2, 9)
    exchange(l_sum, l_rx2, 10)
    exchanged(e_rx2, e_fin, 5)
    gather(e_fin, 6)
    back_left.wait_recv()
    back_right.wait_recv()
    norm_back(0, margin, nback_recv[0].astype(f32))
    norm_back(rows - margin, margin, nback_recv[1].astype(f32))
    out_grad = store(grad_out, grad_out_hbm.at[0], 2)
    out_grad.start()
    exchanged(l_rx2, l_fin, 10)
    gather(l_fin, 11)
    gathered(e_fin, 6)
    out_early = store(e_fin, early_out_hbm, 3)
    out_early.start()
    gathered(l_fin, 11)
    out_late = store(l_fin, late_out_hbm, 4)
    out_late.start()

    for copy in (halo_left, halo_right, tokens_up, part_down, back_left, back_right):
        copy.wait_send()
    for index, ref, count in (
        (4, e_rx1, G),
        (5, e_rx2, Z),
        (6, e_fin, G),
        (9, l_rx1, G),
        (10, l_rx2, Z),
        (11, l_fin, G),
    ):
        wait_bytes(ref.at[pl.ds(0, count - 1)], send_sem.at[index])
    for copy in (out_state, out_rows, out_grad, out_early, out_late):
        copy.wait()


def finish(
    scale,
    state_hbm,
    rows_hbm,
    grad_hbm,
    late_hbm,
    early_hbm,
    state_out,
    rows_out,
    grad_out,
    gain_out,
    query_out,
    key_out,
    value_out,
    output_out,
    token_out,
    grad,
    state,
    token_rows,
    late,
    early,
    gain,
    square,
    token,
    in_sem,
    out_sem,
):
    G, fold, _ = early.shape
    half = fold // 2
    channels = late.shape[2]
    first, second = slice(0, G // 2), slice(G // 2, G)
    upper, lower = slice(0, half), slice(half, fold)

    def matrix(ref, part, piece, column):
        chunk = ref[part, piece, column * channels : (column + 1) * channels]
        return chunk.astype(f32).reshape(channels, channels) * scale

    get_late = pltpu.make_async_copy(late_hbm, late, in_sem.at[0])
    get_early = pltpu.make_async_copy(early_hbm, early, in_sem.at[1])
    get_early.start()
    get_late.start()
    gets = [
        pltpu.make_async_copy(src, dst, in_sem.at[2 + index])
        for index, (src, dst) in enumerate(
            ((grad_hbm, grad), (state_hbm, state), (rows_hbm, token_rows))
        )
    ]
    for get in gets:
        get.start()
    puts = []

    def put(src, dst, index):
        copy = pltpu.make_async_copy(src, dst, out_sem.at[index])
        copy.start()
        puts.append(copy)

    for index, (src, dst) in enumerate(
        ((grad, grad_out), (state, state_out), (token_rows, rows_out))
    ):
        gets[index].wait()
        put(src, dst, index)
    get_early.wait()
    places = ((first, 0), (first, 1), (second, 0))
    for index, (part, column) in enumerate(places):
        for k, piece in enumerate((upper, lower)):
            to = pl.ds((2 * index + k) * channels, channels)
            token[:, to] = matrix(early, part, piece, column)
    put(token, token_out, 3)
    square[3] = matrix(early, second, upper, 1) + matrix(early, second, lower, 1)
    put(square.at[3], output_out, 4)
    get_late.wait()
    square[0] = matrix(late, first, upper, 0)
    square[1] = matrix(late, first, lower, 0)
    square[2] = matrix(late, second, upper, 0)
    put(square.at[0], query_out, 5)
    put(square.at[1], key_out, 6)
    put(square.at[2], value_out, 7)
    gain[...] = jnp.sum(matrix(late, second, lower, 0), axis=0, keepdims=True)
    put(gain, gain_out, 8)
    for copy in puts:
        copy.wait()


def on_device(
    A,
    B,
    atom_state,
    norm_gain,
    query_weight,
    key_weight,
    value_weight,
    out_weight,
    token_weight,
    pair_bias,
    key_start,
    atom_token,
    cotangent_state,
    cotangent_tokens,
):
    _, rows, channels = atom_state.shape
    windows, heads, qw, keys = pair_bias.shape
    toks, width = cotangent_tokens.shape[1:]
    planes = 2
    sizes = (A, B, planes, rows, channels, windows, heads, qw, keys, toks, width)
    margin = keys // 2 + qw // 2
    full = rows + 2 * margin
    span = keys + 2 * qw
    G = A * planes
    Z = B // planes
    fold = 4 * channels // G
    early = 2 * channels
    late = channels
    any_spec = pl.BlockSpec(memory_space=pltpu.HBM)
    V = pltpu.VMEM
    DMA = pltpu.SemaphoreType.DMA
    outs = pl.pallas_call(
        functools.partial(kernel, sizes),
        out_shape=(
            jax.ShapeDtypeStruct((1, rows, channels), bf16),
            jax.ShapeDtypeStruct((1, toks, width), bf16),
            jax.ShapeDtypeStruct((1, rows, channels), f32),
            jax.ShapeDtypeStruct((G, fold, late), bf16),
            jax.ShapeDtypeStruct((G, fold, early), bf16),
        ),
        in_specs=[any_spec] * 12,
        out_specs=(any_spec,) * 5,
        scratch_shapes=[
            V((1, channels), f32),
            pltpu.SMEM((windows,), jnp.int32),
            V((3 * rows // 128, 128), jnp.int32),
            V((rows, channels), bf16),
            V((channels, 3 * channels), bf16),
            V((channels, channels), bf16),
            V((channels, width), bf16),
            V((windows, heads * qw, keys), f32),
            V((rows, channels), bf16),
            V((toks, width), bf16),
            V((toks, width), bf16),
            V((2, margin, channels), bf16),
            V((full, channels), f32),
            V((rows, channels), f32),
            V((full, channels), bf16),
            V((rows, channels), bf16),
            V((2, full, channels), f32),
            V((windows, keys, 3 * channels), bf16),
            V((windows, heads * qw, keys), bf16),
            V((rows, channels), bf16),
            V((rows, channels), bf16),
            V((rows, 2 * toks), bf16),
            V((toks, rows), bf16),
            V((toks, 256), bf16),
            V((2 * toks, width), bf16),
            V((toks, 128), f32),
            V((rows, width), bf16),
            V((rows, width), bf16),
            V((rows, channels), bf16),
            V((rows, 2 * channels), bf16),
            V((toks, width), bf16),
            V((toks, width), bf16),
            V((toks, width), bf16),
            V((16, keys + 4 * qw, channels), f32),
            V((2, full, channels), f32),
            V((rows, channels), bf16),
            V((full, 2 * channels), bf16),
            V((full, channels), f32),
            V((2, margin, channels), bf16),
            V((2, margin, channels), bf16),
            V((rows, channels), f32),
            V((G, fold, early), bf16),
            V((G, fold, early), bf16),
            V((fold, early), bf16),
            V((Z, fold, early), bf16),
            V((G, fold, early), bf16),
            V((G, fold, late), bf16),
            V((G, fold, late), bf16),
            V((fold, late), bf16),
            V((Z, fold, late), bf16),
            V((G, fold, late), bf16),
            V((keys, channels), bf16),
            V((2 * channels, 2 * channels), bf16),
            DMA((14,)),
            DMA((5,)),
            DMA((12,)),
            DMA((12,)),
        ],
        compiler_params=pltpu.CompilerParams(
            collective_id=0, has_side_effects=True, vmem_limit_bytes=62 * 1024 * 1024
        ),
        name="atom_block",
    )(
        atom_state,
        norm_gain.reshape(1, channels),
        query_weight,
        key_weight,
        value_weight,
        out_weight,
        token_weight,
        pair_bias.reshape(windows, heads * qw, keys),
        key_start,
        atom_token.reshape(-1, 128),
        cotangent_state,
        cotangent_tokens,
    )
    rescale = 1.0 / math.sqrt(B * A * rows)
    square = jax.ShapeDtypeStruct((channels, channels), f32)
    done = pl.pallas_call(
        functools.partial(finish, rescale),
        out_shape=(
            jax.ShapeDtypeStruct((1, rows, channels), bf16),
            jax.ShapeDtypeStruct((1, toks, width), bf16),
            jax.ShapeDtypeStruct((1, rows, channels), f32),
            jax.ShapeDtypeStruct((1, channels), f32),
            square,
            square,
            square,
            square,
            jax.ShapeDtypeStruct((channels, width), f32),
        ),
        in_specs=[any_spec] * 5,
        out_specs=(any_spec,) * 9,
        scratch_shapes=[
            V((1, rows, channels), f32),
            V((1, rows, channels), bf16),
            V((1, toks, width), bf16),
            V((G, fold, late), bf16),
            V((G, fold, early), bf16),
            V((1, channels), f32),
            V((4, channels, channels), f32),
            V((channels, width), f32),
            DMA((5,)),
            DMA((9,)),
        ],
        compiler_params=pltpu.CompilerParams(vmem_limit_bytes=62 * 1024 * 1024),
        name="finish",
    )(*outs)
    return done[:3] + (done[3].reshape(channels),) + done[4:]


def solution(mesh):
    return jax.shard_map(
        functools.partial(on_device, mesh.shape["atom"], mesh.shape["sample"]),
        mesh=mesh,
        in_specs=(
            P("sample", "atom", None),
            P(),
            P(),
            P(),
            P(),
            P(),
            P(),
            P("atom", None, None, None),
            P("atom"),
            P(),
            P("sample", "atom", None),
            P("sample", "atom", None),
        ),
        out_specs=(
            P("sample", "atom", None),
            P("sample", "atom", None),
            P("sample", "atom", None),
            P(),
            P(),
            P(),
            P(),
            P(),
            P(),
        ),
        check_vma=False,
    )
```

```python
import functools
import math

import jax
import jax.numpy as jnp
from jax import lax
from jax.experimental import pallas as pl
from jax.experimental.pallas import tpu as pltpu
from jax.sharding import PartitionSpec as P

MESH = pl.DeviceIdType.MESH
norm_eps = 1e-05
f32 = jnp.float32
bf16 = jnp.bfloat16


def nn(a, b):
    return lax.dot_general(a, b, (((1,), (0,)), ((), ())), preferred_element_type=f32)


def nt(a, b):
    return lax.dot_general(a, b, (((1,), (1,)), ((), ())), preferred_element_type=f32)


def tn(a, b):
    return lax.dot_general(a, b, (((0,), (0,)), ((), ())), preferred_element_type=f32)


def kernel(
    sizes,
    state_hbm,
    gain_hbm,
    wq_hbm,
    wk_hbm,
    wv_hbm,
    wo_hbm,
    wt_hbm,
    bias_hbm,
    start_hbm,
    token_hbm,
    cots_hbm,
    ctok_hbm,
    state_out_hbm,
    rows_out_hbm,
    grad_out_hbm,
    late_out_hbm,
    early_out_hbm,
    gain_ref,
    start_ref,
    token_ref,
    state,
    w3,
    wo,
    wt,
    bias,
    cots,
    ctok,
    ctok_low,
    halo,
    unit,
    inverse,
    normed,
    queries,
    kvf,
    kvw,
    probs,
    attended,
    state_out,
    sel_cat,
    sel_t,
    sel_tlow,
    tokens_back,
    inv_own,
    silu,
    active,
    state_back,
    attended_back,
    low_part,
    high_part,
    rows_out,
    shift,
    spread,
    query_back,
    spread_low,
    nback,
    nback_send,
    nback_recv,
    grad_out,
    e_src,
    e_rx1,
    e_sum,
    e_rx2,
    e_fin,
    l_src,
    l_rx1,
    l_sum,
    l_rx2,
    l_fin,
    head_mask,
    mean_mat,
    load_sem,
    out_sem,
    send_sem,
    recv_sem,
):
    A, B, planes, rows, channels, windows, heads, qw, keys, toks, width = sizes
    margin = keys // 2 + qw // 2
    full = rows + 2 * margin
    span = keys + 2 * qw
    head_dim = channels // heads
    factor = head_dim ** (-0.5)
    G = A * planes
    Z = B // planes
    half = 2 * channels // G
    me = lax.axis_index("atom")
    smp = lax.axis_index("sample")
    left = {"atom": lax.rem(me + A - 1, A)}
    right = {"atom": lax.rem(me + 1, A)}

    tile = rows // 128
    below = pl.multiple_of(jnp.maximum(me - 1, 0) * tile, 8)
    above = pl.multiple_of(jnp.minimum(me + 1, A - 1) * tile, 8)

    def load(src, dst, index):
        return pltpu.make_async_copy(src, dst, load_sem.at[index])

    loads = [
        load(state_hbm.at[0], state, 0),
        load(wq_hbm, w3.at[:, pl.ds(0, channels)], 1),
        load(wk_hbm, w3.at[:, pl.ds(channels, channels)], 2),
        load(wv_hbm, w3.at[:, pl.ds(2 * channels, channels)], 3),
        load(bias_hbm, bias, 4),
        load(wo_hbm, wo, 5),
        load(wt_hbm, wt, 6),
        load(cots_hbm.at[0], cots, 7),
        load(ctok_hbm.at[0], ctok, 8),
        load(gain_hbm, gain_ref, 9),
        load(start_hbm, start_ref, 10),
        load(token_hbm.at[pl.ds(below, tile)], token_ref.at[pl.ds(0, tile)], 11),
        load(token_hbm.at[pl.ds(pl.multiple_of(me * tile, 8), tile)], token_ref.at[pl.ds(tile, tile)], 12),
        load(token_hbm.at[pl.ds(above, tile)], token_ref.at[pl.ds(2 * tile, tile)], 13),
    ]
    barrier = pltpu.get_barrier_semaphore()

    rank = lax.div(smp, Z) * A + me
    depth = lax.rem(smp, Z)

    def plane_peer(p):
        return {"sample": lax.div(p, A) * Z + depth, "atom": lax.rem(p, A)}

    def line_peer(q):
        return {"sample": lax.div(smp, Z) * Z + q}

    def greet(d, _):
        pl.semaphore_signal(
            barrier, inc=1, device_id=plane_peer(lax.rem(rank + d, G)), device_id_type=MESH
        )
        return 0

    def greet_line(d, _):
        pl.semaphore_signal(
            barrier, inc=1, device_id=line_peer(lax.rem(depth + d, Z)), device_id_type=MESH
        )
        return 0

    lax.fori_loop(1, G, greet, 0)
    lax.fori_loop(1, Z, greet_line, 0)

    for copy in loads:
        copy.start()

    def send(src, dst, index, device):
        return pltpu.make_async_remote_copy(
            src_ref=src,
            dst_ref=dst,
            send_sem=send_sem.at[index],
            recv_sem=recv_sem.at[index],
            device_id=device,
            device_id_type=MESH,
        )

    def wait_bytes(ref, sem):
        pltpu.make_async_copy(ref, ref, sem).wait()

    def norm(x):
        average = nn(x, mean_mat[pl.ds(0, channels), pl.ds(0, channels)])
        centred = x.astype(f32) - average
        square = (centred * centred).astype(bf16)
        variance = nn(square, mean_mat[pl.ds(0, channels), pl.ds(0, channels)])
        inv = lax.rsqrt(variance + norm_eps)
        unit_rows = centred * inv
        return unit_rows, inv, (unit_rows * gain_ref[...]).astype(bf16)

    for index in (0, 1, 2, 3, 9):
        loads[index].wait()

    lanes = lax.broadcasted_iota(jnp.int32, (keys, channels), 1)
    subs = lax.broadcasted_iota(jnp.int32, (keys, channels), 0)
    mean_mat[...] = jnp.zeros((2 * channels, 2 * channels), bf16)
    mean_mat[pl.ds(0, channels), pl.ds(0, channels)] = jnp.full(
        (channels, channels), 1.0 / channels, bf16
    )
    mean_mat[pl.ds(channels, channels), pl.ds(channels, channels)] = jnp.full(
        (channels, channels), 1.0 / channels, bf16
    )
    head_mask[...] = jnp.where(subs // qw == lanes // head_dim, 1.0, 0.0).astype(bf16)

    block = 256
    group = 8

    def project(c, _):
        r = pl.multiple_of(c * block, block)
        unit_rows, inv, low = norm(state[pl.ds(r, block), :])
        unit[pl.ds(margin + r, block), :] = unit_rows
        inverse[pl.ds(r, block), :] = inv
        normed[pl.ds(margin + r, block), :] = low
        qkv = nn(low, w3[...]).astype(bf16)
        queries[pl.ds(r, block), :] = qkv[:, :channels]
        kvf[0, pl.ds(margin + r, block), :] = qkv[:, channels : 2 * channels].astype(f32)
        kvf[1, pl.ds(margin + r, block), :] = qkv[:, 2 * channels :].astype(f32)
        return 0

    lax.fori_loop(0, rows // block, project, 0)

    pl.semaphore_wait(barrier, G + Z - 2)

    halo_left = send(
        state_hbm.at[0, pl.ds(rows - margin, margin), :], halo.at[0], 0, right
    )
    halo_right = send(state_hbm.at[0, pl.ds(0, margin), :], halo.at[1], 1, left)
    tokens_up = send(ctok_hbm.at[0], ctok_low, 2, right)
    halo_left.start()
    halo_right.start()
    tokens_up.start()

    spread[...] = jnp.zeros((2, full, channels), f32)
    for slot in range(2 * group):
        shift[slot, pl.ds(0, 2 * qw), :] = jnp.zeros((2 * qw, channels), f32)
        shift[slot, pl.ds(2 * qw + keys, 2 * qw), :] = jnp.zeros((2 * qw, channels), f32)

    for index in (11, 12, 13):
        loads[index].wait()
    base = (me * toks).astype(f32)
    lower = base - toks
    sub_id = subs.astype(f32)
    lane_id = lanes.astype(f32)
    count_own = jnp.zeros((toks, 128), f32)
    count_low = jnp.zeros((toks, 128), f32)
    for r in range(tile):
        row = token_ref[pl.ds(tile + r, 1), :].astype(f32)
        spot = jnp.broadcast_to(row, (128, 128))
        hit = jnp.where(spot - base == sub_id, 1.0, 0.0)
        count_own = count_own + hit
        sel_t[:, pl.ds(r * 128, 128)] = hit.astype(bf16)
        if r < 2:
            hit = jnp.where(spot - lower == sub_id, 1.0, 0.0)
            count_low = count_low + hit
            sel_tlow[:, pl.ds(r * 128, 128)] = hit.astype(bf16)
        column = (spot - lower).astype(bf16).T.astype(f32)
        sel_cat[pl.ds(r * 128, 128), pl.ds(0, 128)] = jnp.where(
            column == lane_id, 1.0, 0.0
        ).astype(bf16)
        sel_cat[pl.ds(r * 128, 128), pl.ds(128, 128)] = jnp.where(
            column == lane_id + toks, 1.0, 0.0
        ).astype(bf16)
    has_above = jnp.where(me < A - 1, 1.0, 0.0)
    for r in range(2):
        row = token_ref[pl.ds(2 * tile + r, 1), :].astype(f32)
        spot = jnp.broadcast_to(row, (128, 128))
        count_own = count_own + jnp.where(spot - base == sub_id, has_above, 0.0)
    has_below = jnp.where(me > 0, 1.0, 0.0)
    for r in range(tile):
        row = token_ref[pl.ds(r, 1), :].astype(f32)
        spot = jnp.broadcast_to(row, (128, 128))
        count_low = count_low + jnp.where(spot - lower == sub_id, has_below, 0.0)

    def inverted(count):
        total = jnp.sum(count, axis=-1, keepdims=True)
        return jnp.where(total > 0.0, 1.0 / jnp.maximum(total, 1.0), 0.0)

    inverse_own = inverted(count_own)
    inverse_low = inverted(count_low)
    inv_own[...] = jnp.broadcast_to(inverse_own, (toks, 128))
    loads[8].wait()
    tokens_back[pl.ds(toks, toks), :] = (ctok[...].astype(f32) * inverse_own).astype(bf16)

    first_atom = me * rows
    last_base = A * rows - span

    def spread_heads(x):
        return jnp.concatenate([x] * heads, axis=0) * head_mask[...]

    def gather_heads(x):
        lane = lax.broadcasted_iota(jnp.int32, (qw, channels), 1)
        out = x[0:qw]
        for h in range(1, heads):
            out = jnp.where(lane >= h * head_dim, x[h * qw : (h + 1) * qw], out)
        return out

    def forward(ws):
        queries_of, keys_of, values_of, scores, weights, mixes = [], [], [], [], [], []
        for w in ws:
            place = jnp.clip(start_ref[w] - first_atom + margin, 0, full - keys)
            keys_of.append(kvf[0, pl.ds(place, keys), :].astype(bf16))
            values_of.append(kvf[1, pl.ds(place, keys), :].astype(bf16))
            q0 = pl.multiple_of(w * qw, qw)
            queries_of.append(spread_heads(queries[pl.ds(q0, qw), :]))
        for w, q, k in zip(ws, queries_of, keys_of):
            scores.append(nt(q, k) * factor + bias[w])
        for s in scores:
            weights.append(jnp.exp(s - jnp.max(s, axis=-1, keepdims=True)))
        ones = jnp.ones((keys, channels), bf16)
        for e, v in zip(weights, values_of):
            mixes.append(nn(e.astype(bf16), jnp.concatenate([v, ones], axis=1)))
        for w, e, mixed, k, v in zip(ws, weights, mixes, keys_of, values_of):
            scale = 1.0 / mixed[:, channels:]
            probs[w] = (e * scale).astype(bf16)
            q0 = pl.multiple_of(w * qw, qw)
            attended[pl.ds(q0, qw), :] = gather_heads(mixed[:, :channels] * scale).astype(bf16)
            kvw[w, :, pl.ds(0, channels)] = k
            kvw[w, :, pl.ds(channels, channels)] = v

    near = group // 2
    loads[4].wait()
    loads[10].wait()

    def forward_group(i, _):
        forward([lax.rem(group * i + j + near, windows) for j in range(group)])
        return 0

    inner = windows // group - 1
    lax.fori_loop(0, inner, forward_group, 0)

    halo_left.wait_recv()
    halo_right.wait_recv()
    for side in range(2):
        there = (me > 0) if side == 0 else (me < A - 1)
        at = 0 if side == 0 else margin + rows
        keep = jnp.where(there, 1.0, 0.0)
        x = jnp.where(jnp.full((margin, channels), keep) > 0.0, halo[side].astype(f32), 0.0)
        unit_rows, _, low = norm(x.astype(bf16))
        unit[pl.ds(at, margin), :] = unit_rows
        normed[pl.ds(at, margin), :] = low
        kv = nn(low, w3[:, channels:]).astype(bf16).astype(f32)
        kvf[0, pl.ds(at, margin), :] = kv[:, :channels]
        kvf[1, pl.ds(at, margin), :] = kv[:, channels:]

    lax.fori_loop(inner, inner + 1, forward_group, 0)

    tokens_up.wait_recv()
    tokens_back[pl.ds(0, toks), :] = (ctok_low[...].astype(f32) * inverse_low).astype(bf16)
    for index in range(5, 8):
        loads[index].wait()

    def token_part(c):
        r = c * block if isinstance(c, int) else pl.multiple_of(c * block, block)
        here = pl.ds(r, block)
        out = (state[here, :].astype(f32) + nn(attended[here, :], wo[...])).astype(bf16)
        state_out[here, :] = out
        before = nn(out, wt[...])
        sigma = 0.5 * jnp.tanh(0.5 * before) + 0.5
        act = before * sigma
        silu[here, :] = act.astype(bf16)
        slope = sigma + act - act * sigma
        per_atom = nn(sel_cat[here, :], tokens_back[...])
        back = (per_atom * slope).astype(bf16)
        active[here, :] = back
        sback = (cots[here, :].astype(f32) + nt(back, wt[...])).astype(bf16)
        state_back[here, :] = sback
        aback = nt(sback, wo[...]).astype(bf16)
        attended_back[here, pl.ds(0, channels)] = aback
        attended_back[here, pl.ds(channels, channels)] = (
            -aback.astype(f32) * attended[here, :].astype(f32)
        ).astype(bf16)

    token_part(0)
    low_part[...] = nn(sel_tlow[...], silu[pl.ds(0, 256), :]).astype(bf16)
    part_down = send(low_part, high_part, 3, left)
    part_down.start()
    lax.fori_loop(1, rows // block, lambda c, _: (token_part(c), 0)[1], 0)

    def store(src, dst, index):
        return pltpu.make_async_copy(src, dst, out_sem.at[index])

    out_state = store(state_out, state_out_hbm.at[0], 0)
    out_state.start()

    def stacked(x, y):
        return jnp.concatenate(
            [x.reshape(G // 2, half, channels), y.reshape(G // 2, half, channels)], axis=1
        ).astype(bf16)

    first, second = pl.ds(0, G // 2), pl.ds(G // 2, G // 2)

    token_sum = tn(state_out[...], active[...])
    pieces = [token_sum[:, c : c + channels] for c in range(0, width, channels)]
    output_sum = tn(attended[...], state_back[...])
    output_high = output_sum.astype(bf16).astype(f32)
    e_src[first, :, pl.ds(0, channels)] = stacked(pieces[0], pieces[1])
    e_src[first, :, pl.ds(channels, channels)] = stacked(pieces[2], pieces[3])
    e_src[second, :, pl.ds(0, channels)] = stacked(pieces[4], pieces[5])
    e_src[second, :, pl.ds(channels, channels)] = stacked(output_high, output_sum - output_high)

    def scatter(src, rx, index):
        def one(d, _):
            peer = lax.rem(rank + d, G)
            send(src.at[peer], rx.at[d], index, plane_peer(peer)).start()
            return 0

        lax.fori_loop(1, G, one, 0)

    def scattered(src, rx, part, rx2, index):
        wait_bytes(rx.at[pl.ds(1, G - 1)], recv_sem.at[index])
        total = src[rank].astype(f32)
        for d in range(1, G):
            total = total + rx[d].astype(f32)
        low = total.astype(bf16)
        part[...] = low
        rx2[depth] = low

    def exchange(part, rx2, index):
        def one(d, _):
            peer = lax.rem(depth + d, Z)
            send(part, rx2.at[depth], index, line_peer(peer)).start()
            return 0

        lax.fori_loop(1, Z, one, 0)

    def exchanged(rx2, fin, index):
        wait_bytes(rx2.at[pl.ds(0, Z - 1)], recv_sem.at[index])
        total = rx2[0].astype(f32)
        for d in range(1, Z):
            total = total + rx2[d].astype(f32)
        fin[rank] = total.astype(bf16)

    def gather(fin, index):
        def one(d, _):
            peer = lax.rem(rank + d, G)
            send(fin.at[rank], fin.at[rank], index, plane_peer(peer)).start()
            return 0

        lax.fori_loop(1, G, one, 0)

    def gathered(fin, index):
        wait_bytes(fin.at[pl.ds(0, G - 1)], recv_sem.at[index])

    scatter(e_src, e_rx1, 4)

    def backward(ws, slots):
        state_of = []
        for w in ws:
            kv = kvw[w]
            q0 = pl.multiple_of(w * qw, qw)
            q = spread_heads(queries[pl.ds(q0, qw), :])
            da = spread_heads(attended_back[pl.ds(q0, qw), pl.ds(0, channels)])
            delta = spread_heads(attended_back[pl.ds(q0, qw), pl.ds(channels, channels)])
            state_of.append((kv, q0, q, da, delta, probs[w]))
        ones = jnp.ones((keys, channels), bf16)
        centred = [
            nt(
                jnp.concatenate([da, delta], axis=1),
                jnp.concatenate([kv[:, channels:], ones], axis=1),
            )
            for kv, q0, q, da, delta, p in state_of
        ]
        lows = [
            (st[5].astype(f32) * c).astype(bf16) for st, c in zip(state_of, centred)
        ]
        for ds, (kv, q0, q, da, delta, p) in zip(lows, state_of):
            dq = gather_heads(nn(ds, kv[:, :channels]))
            query_back[pl.ds(q0, qw), :] = (dq * factor).astype(bf16)
        for slot, ds, (kv, q0, q, da, delta, p) in zip(slots, lows, state_of):
            shift[2 * slot, pl.ds(2 * qw, keys), :] = tn(ds, q) * factor
            shift[2 * slot + 1, pl.ds(2 * qw, keys), :] = tn(p, da)
        for w, slot in zip(ws, slots):
            base_atom = jnp.clip(first_atom + w * qw - margin, 0, last_base)
            off = jnp.clip(start_ref[w] - base_atom, 0, 2 * qw)
            to = pl.ds(pl.multiple_of(base_atom - first_atom + margin, 16), span)
            for part in range(2):
                moved = shift[2 * slot + part, pl.ds(2 * qw - off, span), :]
                spread[part, to, :] = spread[part, to, :] + moved

    def backward_group(i, _):
        backward([group * i + j for j in range(group)], list(range(group)))
        return 0

    lax.fori_loop(0, windows // group, backward_group, 0)
    scattered(e_src, e_rx1, e_sum, e_rx2, 4)
    exchange(e_sum, e_rx2, 5)

    own = pl.ds(margin, rows)
    spread_low[:, pl.ds(0, channels)] = spread[0].astype(bf16)
    spread_low[:, pl.ds(channels, channels)] = spread[1].astype(bf16)
    query_sum = tn(normed[own, :], query_back[...])
    pair_sum = tn(normed[...], spread_low[...])
    weighted = (
        w3[:, :channels].astype(f32) * query_sum
        + w3[:, channels : 2 * channels].astype(f32) * pair_sum[:, :channels]
        + w3[:, 2 * channels :].astype(f32) * pair_sum[:, channels:]
    )
    gain_part = jnp.sum(weighted.T.reshape(channels // 8, 8, channels), axis=0) / gain_ref[...]
    gain_rows = jnp.concatenate([gain_part, jnp.zeros((channels - 8, channels), f32)], axis=0)
    l_src[first] = stacked(query_sum, pair_sum[:, :channels])
    l_src[second] = stacked(pair_sum[:, channels:], gain_rows)
    scatter(l_src, l_rx1, 9)

    nback[...] = nt(spread_low[...], w3[:, channels:])
    nback_send[0] = nback[pl.ds(0, margin), :].astype(bf16)
    nback_send[1] = nback[pl.ds(margin + rows, margin), :].astype(bf16)
    back_left = send(nback_send.at[0], nback_recv.at[1], 7, left)
    back_right = send(nback_send.at[1], nback_recv.at[0], 8, right)
    back_left.start()
    back_right.start()
    nback[own, :] = nback[own, :] + nt(query_back[...], w3[:, :channels])

    part_down.wait_recv()
    own_part = nn(sel_t[...], silu[...])
    rows_out[...] = (
        (own_part + high_part[...].astype(f32)) * inv_own[:, pl.ds(0, 1)]
    ).astype(bf16)
    out_rows = store(rows_out, rows_out_hbm.at[0], 1)
    out_rows.start()

    def norm_back(r, count, extra):
        here = pl.ds(r, count)
        there = pl.ds(margin + r, count)
        nb = nback[there, :]
        if extra is not None:
            nb = nb + extra
        ub = nb * gain_ref[...]
        un = unit[there, :]
        means = nn(jnp.concatenate([ub, ub * un], axis=1).astype(bf16), mean_mat[...])
        grad_out[here, :] = state_back[here, :].astype(f32) + inverse[here, :] * (
            ub - means[:, :channels] - un * means[:, channels:]
        )

    for r in range(0, rows - 2 * margin, 288):
        norm_back(margin + r, min(288, rows - 2 * margin - r), None)
    scattered(l_src, l_rx1, l_sum, l_rx2, 9)
    exchange(l_sum, l_rx2, 10)
    exchanged(e_rx2, e_fin, 5)
    gather(e_fin, 6)
    back_left.wait_recv()
    back_right.wait_recv()
    norm_back(0, margin, nback_recv[0].astype(f32))
    norm_back(rows - margin, margin, nback_recv[1].astype(f32))
    out_grad = store(grad_out, grad_out_hbm.at[0], 2)
    out_grad.start()
    exchanged(l_rx2, l_fin, 10)
    gather(l_fin, 11)
    gathered(e_fin, 6)
    out_early = store(e_fin, early_out_hbm, 3)
    out_early.start()
    gathered(l_fin, 11)
    out_late = store(l_fin, late_out_hbm, 4)
    out_late.start()

    for copy in (halo_left, halo_right, tokens_up, part_down, back_left, back_right):
        copy.wait_send()
    for index, ref, count in (
        (4, e_rx1, G),
        (5, e_rx2, Z),
        (6, e_fin, G),
        (9, l_rx1, G),
        (10, l_rx2, Z),
        (11, l_fin, G),
    ):
        wait_bytes(ref.at[pl.ds(0, count - 1)], send_sem.at[index])
    for copy in (out_state, out_rows, out_grad, out_early, out_late):
        copy.wait()


def finish(
    scale,
    state_hbm,
    rows_hbm,
    grad_hbm,
    late_hbm,
    early_hbm,
    state_out,
    rows_out,
    grad_out,
    gain_out,
    query_out,
    key_out,
    value_out,
    output_out,
    token_out,
    grad,
    state,
    token_rows,
    late,
    early,
    gain,
    square,
    token,
    in_sem,
    out_sem,
):
    G, fold, _ = early.shape
    half = fold // 2
    channels = late.shape[2]
    first, second = slice(0, G // 2), slice(G // 2, G)
    upper, lower = slice(0, half), slice(half, fold)

    def matrix(ref, part, piece, column):
        chunk = ref[part, piece, column * channels : (column + 1) * channels]
        return chunk.astype(f32).reshape(channels, channels) * scale

    get_late = pltpu.make_async_copy(late_hbm, late, in_sem.at[0])
    get_early = pltpu.make_async_copy(early_hbm, early, in_sem.at[1])
    get_early.start()
    get_late.start()
    gets = [
        pltpu.make_async_copy(src, dst, in_sem.at[2 + index])
        for index, (src, dst) in enumerate(
            ((grad_hbm, grad), (state_hbm, state), (rows_hbm, token_rows))
        )
    ]
    for get in gets:
        get.start()
    puts = []

    def put(src, dst, index):
        copy = pltpu.make_async_copy(src, dst, out_sem.at[index])
        copy.start()
        puts.append(copy)

    for index, (src, dst) in enumerate(
        ((grad, grad_out), (state, state_out), (token_rows, rows_out))
    ):
        gets[index].wait()
        put(src, dst, index)
    get_early.wait()
    places = ((first, 0), (first, 1), (second, 0))
    for index, (part, column) in enumerate(places):
        for k, piece in enumerate((upper, lower)):
            to = pl.ds((2 * index + k) * channels, channels)
            token[:, to] = matrix(early, part, piece, column)
    put(token, token_out, 3)
    square[3] = matrix(early, second, upper, 1) + matrix(early, second, lower, 1)
    put(square.at[3], output_out, 4)
    get_late.wait()
    square[0] = matrix(late, first, upper, 0)
    square[1] = matrix(late, first, lower, 0)
    square[2] = matrix(late, second, upper, 0)
    put(square.at[0], query_out, 5)
    put(square.at[1], key_out, 6)
    put(square.at[2], value_out, 7)
    gain[...] = jnp.sum(matrix(late, second, lower, 0), axis=0, keepdims=True)
    put(gain, gain_out, 8)
    for copy in puts:
        copy.wait()


def on_device(
    A,
    B,
    atom_state,
    norm_gain,
    query_weight,
    key_weight,
    value_weight,
    out_weight,
    token_weight,
    pair_bias,
    key_start,
    atom_token,
    cotangent_state,
    cotangent_tokens,
):
    _, rows, channels = atom_state.shape
    windows, heads, qw, keys = pair_bias.shape
    toks, width = cotangent_tokens.shape[1:]
    planes = 2
    sizes = (A, B, planes, rows, channels, windows, heads, qw, keys, toks, width)
    margin = keys // 2 + qw // 2
    full = rows + 2 * margin
    span = keys + 2 * qw
    G = A * planes
    Z = B // planes
    fold = 4 * channels // G
    early = 2 * channels
    late = channels
    any_spec = pl.BlockSpec(memory_space=pltpu.HBM)
    V = pltpu.VMEM
    DMA = pltpu.SemaphoreType.DMA
    outs = pl.pallas_call(
        functools.partial(kernel, sizes),
        out_shape=(
            jax.ShapeDtypeStruct((1, rows, channels), bf16),
            jax.ShapeDtypeStruct((1, toks, width), bf16),
            jax.ShapeDtypeStruct((1, rows, channels), f32),
            jax.ShapeDtypeStruct((G, fold, late), bf16),
            jax.ShapeDtypeStruct((G, fold, early), bf16),
        ),
        in_specs=[any_spec] * 12,
        out_specs=(any_spec,) * 5,
        scratch_shapes=[
            V((1, channels), f32),
            pltpu.SMEM((windows,), jnp.int32),
            V((3 * rows // 128, 128), jnp.int32),
            V((rows, channels), bf16),
            V((channels, 3 * channels), bf16),
            V((channels, channels), bf16),
            V((channels, width), bf16),
            V((windows, heads * qw, keys), f32),
            V((rows, channels), bf16),
            V((toks, width), bf16),
            V((toks, width), bf16),
            V((2, margin, channels), bf16),
            V((full, channels), f32),
            V((rows, channels), f32),
            V((full, channels), bf16),
            V((rows, channels), bf16),
            V((2, full, channels), f32),
            V((windows, keys, 2 * channels), bf16),
            V((windows, heads * qw, keys), bf16),
            V((rows, channels), bf16),
            V((rows, channels), bf16),
            V((rows, 2 * toks), bf16),
            V((toks, rows), bf16),
            V((toks, 256), bf16),
            V((2 * toks, width), bf16),
            V((toks, 128), f32),
            V((rows, width), bf16),
            V((rows, width), bf16),
            V((rows, channels), bf16),
            V((rows, 2 * channels), bf16),
            V((toks, width), bf16),
            V((toks, width), bf16),
            V((toks, width), bf16),
            V((16, keys + 4 * qw, channels), f32),
            V((2, full, channels), f32),
            V((rows, channels), bf16),
            V((full, 2 * channels), bf16),
            V((full, channels), f32),
            V((2, margin, channels), bf16),
            V((2, margin, channels), bf16),
            V((rows, channels), f32),
            V((G, fold, early), bf16),
            V((G, fold, early), bf16),
            V((fold, early), bf16),
            V((Z, fold, early), bf16),
            V((G, fold, early), bf16),
            V((G, fold, late), bf16),
            V((G, fold, late), bf16),
            V((fold, late), bf16),
            V((Z, fold, late), bf16),
            V((G, fold, late), bf16),
            V((keys, channels), bf16),
            V((2 * channels, 2 * channels), bf16),
            DMA((14,)),
            DMA((5,)),
            DMA((12,)),
            DMA((12,)),
        ],
        compiler_params=pltpu.CompilerParams(
            collective_id=0, has_side_effects=True, vmem_limit_bytes=62 * 1024 * 1024
        ),
        name="atom_block",
    )(
        atom_state,
        norm_gain.reshape(1, channels),
        query_weight,
        key_weight,
        value_weight,
        out_weight,
        token_weight,
        pair_bias.reshape(windows, heads * qw, keys),
        key_start,
        atom_token.reshape(-1, 128),
        cotangent_state,
        cotangent_tokens,
    )
    rescale = 1.0 / math.sqrt(B * A * rows)
    square = jax.ShapeDtypeStruct((channels, channels), f32)
    done = pl.pallas_call(
        functools.partial(finish, rescale),
        out_shape=(
            jax.ShapeDtypeStruct((1, rows, channels), bf16),
            jax.ShapeDtypeStruct((1, toks, width), bf16),
            jax.ShapeDtypeStruct((1, rows, channels), f32),
            jax.ShapeDtypeStruct((1, channels), f32),
            square,
            square,
            square,
            square,
            jax.ShapeDtypeStruct((channels, width), f32),
        ),
        in_specs=[any_spec] * 5,
        out_specs=(any_spec,) * 9,
        scratch_shapes=[
            V((1, rows, channels), f32),
            V((1, rows, channels), bf16),
            V((1, toks, width), bf16),
            V((G, fold, late), bf16),
            V((G, fold, early), bf16),
            V((1, channels), f32),
            V((4, channels, channels), f32),
            V((channels, width), f32),
            DMA((5,)),
            DMA((9,)),
        ],
        compiler_params=pltpu.CompilerParams(vmem_limit_bytes=62 * 1024 * 1024),
        name="finish",
    )(*outs)
    return done[:3] + (done[3].reshape(channels),) + done[4:]


def solution(mesh):
    return jax.shard_map(
        functools.partial(on_device, mesh.shape["atom"], mesh.shape["sample"]),
        mesh=mesh,
        in_specs=(
            P("sample", "atom", None),
            P(),
            P(),
            P(),
            P(),
            P(),
            P(),
            P("atom", None, None, None),
            P("atom"),
            P(),
            P("sample", "atom", None),
            P("sample", "atom", None),
        ),
        out_specs=(
            P("sample", "atom", None),
            P("sample", "atom", None),
            P("sample", "atom", None),
            P(),
            P(),
            P(),
            P(),
            P(),
            P(),
        ),
        check_vma=False,
    )
```

```python
import functools
import math

import jax
import jax.numpy as jnp
from jax import lax
from jax.experimental import pallas as pl
from jax.experimental.pallas import tpu as pltpu
from jax.sharding import PartitionSpec as P

MESH = pl.DeviceIdType.MESH
norm_eps = 1e-05
f32 = jnp.float32
bf16 = jnp.bfloat16


def nn(a, b):
    return lax.dot_general(a, b, (((1,), (0,)), ((), ())), preferred_element_type=f32)


def nt(a, b):
    return lax.dot_general(a, b, (((1,), (1,)), ((), ())), preferred_element_type=f32)


def tn(a, b):
    return lax.dot_general(a, b, (((0,), (0,)), ((), ())), preferred_element_type=f32)


def kernel(
    sizes,
    state_hbm,
    gain_hbm,
    wq_hbm,
    wk_hbm,
    wv_hbm,
    wo_hbm,
    wt_hbm,
    bias_hbm,
    start_hbm,
    token_hbm,
    cots_hbm,
    ctok_hbm,
    state_out_ref,
    rows_out_ref,
    grad_out_ref,
    gain_out,
    query_out,
    key_out,
    value_out,
    output_out,
    token_out,
    gain_ref,
    start_ref,
    token_ref,
    state,
    w3,
    wo,
    wt,
    bias,
    cots,
    ctok,
    ctok_low,
    halo,
    unit,
    inverse,
    normed,
    queries,
    kvf,
    kvw,
    probs,
    attended,
    sel_cat,
    sel_t,
    sel_tlow,
    tokens_back,
    inv_own,
    silu,
    active,
    state_back,
    attended_back,
    low_part,
    high_part,
    shift,
    spread,
    query_back,
    spread_low,
    nback,
    nback_send,
    nback_recv,
    e_src,
    e_rx1,
    e_sum,
    e_rx2,
    e_fin,
    l_src,
    l_rx1,
    l_sum,
    l_rx2,
    l_fin,
    head_mask,
    mean_mat,
    load_sem,
    send_sem,
    recv_sem,
):
    A, B, planes, rows, channels, windows, heads, qw, keys, toks, width = sizes
    state_out, grad_out = state_out_ref.at[0], grad_out_ref.at[0]
    margin = keys // 2 + qw // 2
    full = rows + 2 * margin
    span = keys + 2 * qw
    head_dim = channels // heads
    factor = head_dim ** (-0.5)
    G = A * planes
    Z = B // planes
    half = 2 * channels // G
    me = lax.axis_index("atom")
    smp = lax.axis_index("sample")
    left = {"atom": lax.rem(me + A - 1, A)}
    right = {"atom": lax.rem(me + 1, A)}

    tile = rows // 128
    below = pl.multiple_of(jnp.maximum(me - 1, 0) * tile, 8)
    above = pl.multiple_of(jnp.minimum(me + 1, A - 1) * tile, 8)

    def load(src, dst, index):
        return pltpu.make_async_copy(src, dst, load_sem.at[index])

    loads = [
        load(state_hbm.at[0], state, 0),
        load(wq_hbm, w3.at[:, pl.ds(0, channels)], 1),
        load(wk_hbm, w3.at[:, pl.ds(channels, channels)], 2),
        load(wv_hbm, w3.at[:, pl.ds(2 * channels, channels)], 3),
        load(bias_hbm, bias, 4),
        load(wo_hbm, wo, 5),
        load(wt_hbm, wt, 6),
        load(cots_hbm.at[0], cots, 7),
        load(ctok_hbm.at[0], ctok, 8),
        load(gain_hbm, gain_ref, 9),
        load(start_hbm, start_ref, 10),
        load(token_hbm.at[pl.ds(below, tile)], token_ref.at[pl.ds(0, tile)], 11),
        load(token_hbm.at[pl.ds(pl.multiple_of(me * tile, 8), tile)], token_ref.at[pl.ds(tile, tile)], 12),
        load(token_hbm.at[pl.ds(above, tile)], token_ref.at[pl.ds(2 * tile, tile)], 13),
    ]
    for copy in loads[:4] + loads[9:10]:
        copy.start()

    barrier = pltpu.get_barrier_semaphore()

    rank = lax.div(smp, Z) * A + me
    depth = lax.rem(smp, Z)

    def plane_peer(p):
        return {"sample": lax.div(p, A) * Z + depth, "atom": lax.rem(p, A)}

    def line_peer(q):
        return {"sample": lax.div(smp, Z) * Z + q}

    def greet(d, _):
        pl.semaphore_signal(
            barrier, inc=1, device_id=plane_peer(lax.rem(rank + d, G)), device_id_type=MESH
        )
        return 0

    def greet_line(d, _):
        pl.semaphore_signal(
            barrier, inc=1, device_id=line_peer(lax.rem(depth + d, Z)), device_id_type=MESH
        )
        return 0

    lax.fori_loop(1, G, greet, 0)
    lax.fori_loop(1, Z, greet_line, 0)

    for copy in loads[4:9]:
        copy.start()
    for copy in loads[10:]:
        copy.start()

    def send(src, dst, index, device):
        return pltpu.make_async_remote_copy(
            src_ref=src,
            dst_ref=dst,
            send_sem=send_sem.at[index],
            recv_sem=recv_sem.at[index],
            device_id=device,
            device_id_type=MESH,
        )

    def wait_bytes(ref, sem):
        pltpu.make_async_copy(ref, ref, sem).wait()

    def norm(x):
        average = nn(x, mean_mat[pl.ds(0, channels), pl.ds(0, channels)])
        centred = x.astype(f32) - average
        square = (centred * centred).astype(bf16)
        variance = nn(square, mean_mat[pl.ds(0, channels), pl.ds(0, channels)])
        inv = lax.rsqrt(variance + norm_eps)
        unit_rows = centred * inv
        return unit_rows, inv, (unit_rows * gain_ref[...]).astype(bf16)

    for index in (0, 1, 2, 3, 9):
        loads[index].wait()

    lanes = lax.broadcasted_iota(jnp.int32, (keys, channels), 1)
    subs = lax.broadcasted_iota(jnp.int32, (keys, channels), 0)
    mean_mat[...] = jnp.zeros((2 * channels, 2 * channels), bf16)
    mean_mat[pl.ds(0, channels), pl.ds(0, channels)] = jnp.full(
        (channels, channels), 1.0 / channels, bf16
    )
    mean_mat[pl.ds(channels, channels), pl.ds(channels, channels)] = jnp.full(
        (channels, channels), 1.0 / channels, bf16
    )
    head_mask[...] = jnp.where(subs // qw == lanes // head_dim, 1.0, 0.0).astype(bf16)

    block = 256
    group = 8

    def project(c, _):
        r = pl.multiple_of(c * block, block)
        unit_rows, inv, low = norm(state[pl.ds(r, block), :])
        unit[pl.ds(margin + r, block), :] = unit_rows
        inverse[pl.ds(r, block), :] = inv
        normed[pl.ds(margin + r, block), :] = low
        qkv = nn(low, w3[...]).astype(bf16)
        queries[pl.ds(r, block), :] = qkv[:, :channels]
        kvf[0, pl.ds(margin + r, block), :] = qkv[:, channels : 2 * channels].astype(f32)
        kvf[1, pl.ds(margin + r, block), :] = qkv[:, 2 * channels :].astype(f32)
        return 0

    lax.fori_loop(0, rows // block, project, 0)

    pl.semaphore_wait(barrier, G + Z - 2)

    halo_left = send(
        state_hbm.at[0, pl.ds(rows - margin, margin), :], halo.at[0], 0, right
    )
    halo_right = send(state_hbm.at[0, pl.ds(0, margin), :], halo.at[1], 1, left)
    tokens_up = send(ctok_hbm.at[0], ctok_low, 2, right)
    halo_left.start()
    halo_right.start()
    tokens_up.start()

    spread[...] = jnp.zeros((2, full, channels), f32)
    for slot in range(2 * group):
        shift[slot, pl.ds(0, 2 * qw), :] = jnp.zeros((2 * qw, channels), f32)
        shift[slot, pl.ds(2 * qw + keys, 2 * qw), :] = jnp.zeros((2 * qw, channels), f32)

    for index in (11, 12, 13):
        loads[index].wait()
    base = (me * toks).astype(f32)
    lower = base - toks
    sub_id = subs.astype(f32)
    lane_id = lanes.astype(f32)
    count_own = jnp.zeros((toks, 128), f32)
    count_low = jnp.zeros((toks, 128), f32)
    for r in range(tile):
        row = token_ref[pl.ds(tile + r, 1), :].astype(f32)
        spot = jnp.broadcast_to(row, (128, 128))
        hit = jnp.where(spot - base == sub_id, 1.0, 0.0)
        count_own = count_own + hit
        sel_t[:, pl.ds(r * 128, 128)] = hit.astype(bf16)
        if r < 2:
            hit = jnp.where(spot - lower == sub_id, 1.0, 0.0)
            count_low = count_low + hit
            sel_tlow[:, pl.ds(r * 128, 128)] = hit.astype(bf16)
        column = (spot - lower).astype(bf16).T.astype(f32)
        sel_cat[pl.ds(r * 128, 128), pl.ds(0, 128)] = jnp.where(
            column == lane_id, 1.0, 0.0
        ).astype(bf16)
        sel_cat[pl.ds(r * 128, 128), pl.ds(128, 128)] = jnp.where(
            column == lane_id + toks, 1.0, 0.0
        ).astype(bf16)
    has_above = jnp.where(me < A - 1, 1.0, 0.0)
    for r in range(2):
        row = token_ref[pl.ds(2 * tile + r, 1), :].astype(f32)
        spot = jnp.broadcast_to(row, (128, 128))
        count_own = count_own + jnp.where(spot - base == sub_id, has_above, 0.0)
    has_below = jnp.where(me > 0, 1.0, 0.0)
    for r in range(tile):
        row = token_ref[pl.ds(r, 1), :].astype(f32)
        spot = jnp.broadcast_to(row, (128, 128))
        count_low = count_low + jnp.where(spot - lower == sub_id, has_below, 0.0)

    def inverted(count):
        total = jnp.sum(count, axis=-1, keepdims=True)
        return jnp.where(total > 0.0, 1.0 / jnp.maximum(total, 1.0), 0.0)

    inverse_own = inverted(count_own)
    inverse_low = inverted(count_low)
    inv_own[...] = jnp.broadcast_to(inverse_own, (toks, 128))
    loads[8].wait()
    tokens_back[pl.ds(toks, toks), :] = (ctok[...].astype(f32) * inverse_own).astype(bf16)

    first_atom = me * rows
    last_base = A * rows - span

    def spread_heads(x):
        return jnp.concatenate([x] * heads, axis=0) * head_mask[...]

    def gather_heads(x):
        lane = lax.broadcasted_iota(jnp.int32, (qw, channels), 1)
        out = x[0:qw]
        for h in range(1, heads):
            out = jnp.where(lane >= h * head_dim, x[h * qw : (h + 1) * qw], out)
        return out

    def forward(ws):
        queries_of, keys_of, values_of, scores, weights, mixes = [], [], [], [], [], []
        for w in ws:
            place = jnp.clip(start_ref[w] - first_atom + margin, 0, full - keys)
            keys_of.append(kvf[0, pl.ds(place, keys), :].astype(bf16))
            values_of.append(kvf[1, pl.ds(place, keys), :].astype(bf16))
            q0 = pl.multiple_of(w * qw, qw)
            queries_of.append(spread_heads(queries[pl.ds(q0, qw), :]))
        for w, q, k in zip(ws, queries_of, keys_of):
            scores.append(nt(q, k) * factor + bias[w])
        for s in scores:
            weights.append(jnp.exp(s - jnp.max(s, axis=-1, keepdims=True)))
        ones = jnp.ones((keys, channels), bf16)
        for e, v in zip(weights, values_of):
            mixes.append(nn(e.astype(bf16), jnp.concatenate([v, ones], axis=1)))
        for w, e, mixed, k, v in zip(ws, weights, mixes, keys_of, values_of):
            scale = 1.0 / mixed[:, channels:]
            probs[w] = (e * scale).astype(bf16)
            q0 = pl.multiple_of(w * qw, qw)
            attended[pl.ds(q0, qw), :] = gather_heads(mixed[:, :channels] * scale).astype(bf16)
            kvw[w, :, pl.ds(0, channels)] = k
            kvw[w, :, pl.ds(channels, channels)] = v

    near = group // 2
    loads[4].wait()
    loads[10].wait()

    def forward_group(i, _):
        forward([lax.rem(group * i + j + near, windows) for j in range(group)])
        return 0

    inner = windows // group - 1
    lax.fori_loop(0, inner, forward_group, 0)

    halo_left.wait_recv()
    halo_right.wait_recv()
    for side in range(2):
        there = (me > 0) if side == 0 else (me < A - 1)
        at = 0 if side == 0 else margin + rows
        keep = jnp.where(there, 1.0, 0.0)
        x = jnp.where(jnp.full((margin, channels), keep) > 0.0, halo[side].astype(f32), 0.0)
        unit_rows, _, low = norm(x.astype(bf16))
        unit[pl.ds(at, margin), :] = unit_rows
        normed[pl.ds(at, margin), :] = low
        kv = nn(low, w3[:, channels:]).astype(bf16).astype(f32)
        kvf[0, pl.ds(at, margin), :] = kv[:, :channels]
        kvf[1, pl.ds(at, margin), :] = kv[:, channels:]

    lax.fori_loop(inner, inner + 1, forward_group, 0)

    tokens_up.wait_recv()
    tokens_back[pl.ds(0, toks), :] = (ctok_low[...].astype(f32) * inverse_low).astype(bf16)
    for index in range(5, 8):
        loads[index].wait()

    def token_part(c):
        r = c * block if isinstance(c, int) else pl.multiple_of(c * block, block)
        here = pl.ds(r, block)
        out = (state[here, :].astype(f32) + nn(attended[here, :], wo[...])).astype(bf16)
        state_out[here, :] = out
        before = nn(out, wt[...])
        sigma = 0.5 * jnp.tanh(0.5 * before) + 0.5
        act = before * sigma
        silu[here, :] = act.astype(bf16)
        slope = sigma + act - act * sigma
        per_atom = nn(sel_cat[here, :], tokens_back[...])
        back = (per_atom * slope).astype(bf16)
        active[here, :] = back
        sback = (cots[here, :].astype(f32) + nt(back, wt[...])).astype(bf16)
        state_back[here, :] = sback
        aback = nt(sback, wo[...]).astype(bf16)
        attended_back[here, pl.ds(0, channels)] = aback
        attended_back[here, pl.ds(channels, channels)] = (
            -aback.astype(f32) * attended[here, :].astype(f32)
        ).astype(bf16)

    token_part(0)
    low_part[...] = nn(sel_tlow[...], silu[pl.ds(0, 256), :]).astype(bf16)
    part_down = send(low_part, high_part, 3, left)
    part_down.start()
    lax.fori_loop(1, rows // block, lambda c, _: (token_part(c), 0)[1], 0)

    def stacked(x, y):
        return jnp.concatenate(
            [x.reshape(G // 2, half, channels), y.reshape(G // 2, half, channels)], axis=1
        ).astype(bf16)

    first, second = pl.ds(0, G // 2), pl.ds(G // 2, G // 2)

    token_sum = tn(state_out[...], active[...])
    pieces = [token_sum[:, c : c + channels] for c in range(0, width, channels)]
    output_sum = tn(attended[...], state_back[...])
    output_high = output_sum.astype(bf16).astype(f32)
    e_src[first, :, pl.ds(0, channels)] = stacked(pieces[0], pieces[1])
    e_src[first, :, pl.ds(channels, channels)] = stacked(pieces[2], pieces[3])
    e_src[second, :, pl.ds(0, channels)] = stacked(pieces[4], pieces[5])
    e_src[second, :, pl.ds(channels, channels)] = stacked(output_high, output_sum - output_high)

    def scatter(src, rx, index):
        def one(i, _):
            d = 1 + lax.rem(i + G // 4, G - 1)
            peer = lax.rem(rank + d, G)
            send(src.at[peer], rx.at[d], index, plane_peer(peer)).start()
            return 0

        lax.fori_loop(0, G - 1, one, 0)

    def scattered(src, rx, part, rx2, index):
        wait_bytes(rx.at[pl.ds(1, G - 1)], recv_sem.at[index])
        total = src[rank].astype(f32)
        for d in range(1, G):
            total = total + rx[d].astype(f32)
        low = total.astype(bf16)
        part[...] = low
        rx2[depth] = low

    def exchange(part, rx2, index):
        def one(d, _):
            peer = lax.rem(depth + d, Z)
            send(part, rx2.at[depth], index, line_peer(peer)).start()
            return 0

        lax.fori_loop(1, Z, one, 0)

    def exchanged(rx2, fin, index):
        wait_bytes(rx2.at[pl.ds(0, Z - 1)], recv_sem.at[index])
        total = rx2[0].astype(f32)
        for d in range(1, Z):
            total = total + rx2[d].astype(f32)
        fin[rank] = total.astype(bf16)

    def gather(fin, index):
        def one(i, _):
            peer = lax.rem(rank + 1 + lax.rem(i + G // 4, G - 1), G)
            send(fin.at[rank], fin.at[rank], index, plane_peer(peer)).start()
            return 0

        lax.fori_loop(0, G - 1, one, 0)

    def gathered(fin, index):
        wait_bytes(fin.at[pl.ds(0, G - 1)], recv_sem.at[index])

    scatter(e_src, e_rx1, 4)

    def backward(ws, slots):
        state_of = []
        for w in ws:
            kv = kvw[w]
            q0 = pl.multiple_of(w * qw, qw)
            q = spread_heads(queries[pl.ds(q0, qw), :])
            da = spread_heads(attended_back[pl.ds(q0, qw), pl.ds(0, channels)])
            delta = spread_heads(attended_back[pl.ds(q0, qw), pl.ds(channels, channels)])
            state_of.append((kv, q0, q, da, delta, probs[w]))
        ones = jnp.ones((keys, channels), bf16)
        centred = [
            nt(
                jnp.concatenate([da, delta], axis=1),
                jnp.concatenate([kv[:, channels:], ones], axis=1),
            )
            for kv, q0, q, da, delta, p in state_of
        ]
        lows = [
            (st[5].astype(f32) * c).astype(bf16) for st, c in zip(state_of, centred)
        ]
        for ds, (kv, q0, q, da, delta, p) in zip(lows, state_of):
            dq = gather_heads(nn(ds, kv[:, :channels]))
            query_back[pl.ds(q0, qw), :] = (dq * factor).astype(bf16)
        for slot, ds, (kv, q0, q, da, delta, p) in zip(slots, lows, state_of):
            shift[2 * slot, pl.ds(2 * qw, keys), :] = tn(ds, q) * factor
            shift[2 * slot + 1, pl.ds(2 * qw, keys), :] = tn(p, da)
        for w, slot in zip(ws, slots):
            base_atom = jnp.clip(first_atom + w * qw - margin, 0, last_base)
            off = jnp.clip(start_ref[w] - base_atom, 0, 2 * qw)
            to = pl.ds(pl.multiple_of(base_atom - first_atom + margin, 16), span)
            for part in range(2):
                moved = shift[2 * slot + part, pl.ds(2 * qw - off, span), :]
                spread[part, to, :] = spread[part, to, :] + moved

    def backward_group(i, _):
        backward([group * i + j for j in range(group)], list(range(group)))
        return 0

    lax.fori_loop(0, windows // group, backward_group, 0)

    own = pl.ds(margin, rows)
    spread_low[:, pl.ds(0, channels)] = spread[0].astype(bf16)
    spread_low[:, pl.ds(channels, channels)] = spread[1].astype(bf16)
    query_sum = tn(normed[own, :], query_back[...])
    pair_sum = tn(normed[...], spread_low[...])
    weighted = (
        w3[:, :channels].astype(f32) * query_sum
        + w3[:, channels : 2 * channels].astype(f32) * pair_sum[:, :channels]
        + w3[:, 2 * channels :].astype(f32) * pair_sum[:, channels:]
    )
    gain_part = jnp.sum(weighted.T.reshape(channels // 8, 8, channels), axis=0) / gain_ref[...]
    gain_rows = jnp.concatenate([gain_part, jnp.zeros((channels - 8, channels), f32)], axis=0)
    l_src[first] = stacked(query_sum, pair_sum[:, :channels])
    l_src[second] = stacked(pair_sum[:, channels:], gain_rows)
    scatter(l_src, l_rx1, 9)

    nback[...] = nt(spread_low[...], w3[:, channels:])
    nback_send[0] = nback[pl.ds(0, margin), :].astype(bf16)
    nback_send[1] = nback[pl.ds(margin + rows, margin), :].astype(bf16)
    back_left = send(nback_send.at[0], nback_recv.at[1], 7, left)
    back_right = send(nback_send.at[1], nback_recv.at[0], 8, right)
    back_left.start()
    back_right.start()
    nback[own, :] = nback[own, :] + nt(query_back[...], w3[:, :channels])

    part_down.wait_recv()
    own_part = nn(sel_t[...], silu[...])
    rows_out_ref[0] = (
        (own_part + high_part[...].astype(f32)) * inv_own[:, pl.ds(0, 1)]
    ).astype(bf16)

    def norm_back(r, count, extra):
        here = pl.ds(r, count)
        there = pl.ds(margin + r, count)
        nb = nback[there, :]
        if extra is not None:
            nb = nb + extra
        ub = nb * gain_ref[...]
        un = unit[there, :]
        means = nn(jnp.concatenate([ub, ub * un], axis=1).astype(bf16), mean_mat[...])
        grad_out[here, :] = state_back[here, :].astype(f32) + inverse[here, :] * (
            ub - means[:, :channels] - un * means[:, channels:]
        )

    for r in range(0, rows - 2 * margin, 288):
        norm_back(margin + r, min(288, rows - 2 * margin - r), None)
    scattered(e_src, e_rx1, e_sum, e_rx2, 4)
    exchange(e_sum, e_rx2, 5)
    scattered(l_src, l_rx1, l_sum, l_rx2, 9)
    exchange(l_sum, l_rx2, 10)
    exchanged(e_rx2, e_fin, 5)
    gather(e_fin, 6)
    back_left.wait_recv()
    back_right.wait_recv()
    norm_back(0, margin, nback_recv[0].astype(f32))
    norm_back(rows - margin, margin, nback_recv[1].astype(f32))
    exchanged(l_rx2, l_fin, 10)
    gather(l_fin, 11)
    gathered(e_fin, 6)
    scale = 1.0 / math.sqrt(B * A * rows)
    upper, lower = slice(0, half), slice(half, 2 * half)

    def matrix(ref, part, piece, column):
        chunk = ref[part, piece, column * channels : (column + 1) * channels]
        return chunk.astype(f32).reshape(channels, channels) * scale

    for index, (part, column) in enumerate(((first, 0), (first, 1), (second, 0))):
        for k, piece in enumerate((upper, lower)):
            to = pl.ds((2 * index + k) * channels, channels)
            token_out[:, to] = matrix(e_fin, part, piece, column)
    output_out[...] = matrix(e_fin, second, upper, 1) + matrix(e_fin, second, lower, 1)
    gathered(l_fin, 11)
    query_out[...] = matrix(l_fin, first, upper, 0)
    key_out[...] = matrix(l_fin, first, lower, 0)
    value_out[...] = matrix(l_fin, second, upper, 0)
    gain_out[...] = jnp.sum(matrix(l_fin, second, lower, 0), axis=0, keepdims=True)

    for copy in (halo_left, halo_right, tokens_up, part_down, back_left, back_right):
        copy.wait_send()
    for index, ref, count in (
        (4, e_rx1, G),
        (5, e_rx2, Z),
        (6, e_fin, G),
        (9, l_rx1, G),
        (10, l_rx2, Z),
        (11, l_fin, G),
    ):
        wait_bytes(ref.at[pl.ds(0, count - 1)], send_sem.at[index])


def finish(*refs):
    count = len(refs) // 2
    copies = [
        pltpu.make_async_copy(refs[index], refs[count + index], refs[-1].at[index])
        for index in range(count)
    ]
    for copy in copies:
        copy.start()
    for copy in copies:
        copy.wait()


def on_device(
    A,
    B,
    atom_state,
    norm_gain,
    query_weight,
    key_weight,
    value_weight,
    out_weight,
    token_weight,
    pair_bias,
    key_start,
    atom_token,
    cotangent_state,
    cotangent_tokens,
):
    _, rows, channels = atom_state.shape
    windows, heads, qw, keys = pair_bias.shape
    toks, width = cotangent_tokens.shape[1:]
    planes = 2
    sizes = (A, B, planes, rows, channels, windows, heads, qw, keys, toks, width)
    margin = keys // 2 + qw // 2
    full = rows + 2 * margin
    span = keys + 2 * qw
    G = A * planes
    Z = B // planes
    fold = 4 * channels // G
    early = 2 * channels
    late = channels
    any_spec = pl.BlockSpec(memory_space=pltpu.HBM)
    V = pltpu.VMEM
    DMA = pltpu.SemaphoreType.DMA
    vmem_spec = pl.BlockSpec(memory_space=pltpu.VMEM)
    square = jax.ShapeDtypeStruct((channels, channels), f32)
    shapes = (
        jax.ShapeDtypeStruct((1, rows, channels), bf16),
        jax.ShapeDtypeStruct((1, toks, width), bf16),
        jax.ShapeDtypeStruct((1, rows, channels), f32),
        jax.ShapeDtypeStruct((1, channels), f32),
        square,
        square,
        square,
        square,
        jax.ShapeDtypeStruct((channels, width), f32),
    )
    operands = (
        atom_state,
        norm_gain.reshape(1, channels),
        query_weight,
        key_weight,
        value_weight,
        out_weight,
        token_weight,
        pair_bias.reshape(windows, heads * qw, keys),
        key_start,
        atom_token.reshape(-1, 128),
        cotangent_state,
        cotangent_tokens,
    )
    outs = pl.pallas_call(
        functools.partial(kernel, sizes),
        out_shape=shapes,
        in_specs=[any_spec] * 12,
        out_specs=(vmem_spec,) * 9,
        scratch_shapes=[
            V((1, channels), f32),
            pltpu.SMEM((windows,), jnp.int32),
            V((3 * rows // 128, 128), jnp.int32),
            V((rows, channels), bf16),
            V((channels, 3 * channels), bf16),
            V((channels, channels), bf16),
            V((channels, width), bf16),
            V((windows, heads * qw, keys), f32),
            V((rows, channels), bf16),
            V((toks, width), bf16),
            V((toks, width), bf16),
            V((2, margin, channels), bf16),
            V((full, channels), f32),
            V((rows, channels), f32),
            V((full, channels), bf16),
            V((rows, channels), bf16),
            V((2, full, channels), f32),
            V((windows, keys, 2 * channels), bf16),
            V((windows, heads * qw, keys), bf16),
            V((rows, channels), bf16),
            V((rows, 2 * toks), bf16),
            V((toks, rows), bf16),
            V((toks, 256), bf16),
            V((2 * toks, width), bf16),
            V((toks, 128), f32),
            V((rows, width), bf16),
            V((rows, width), bf16),
            V((rows, channels), bf16),
            V((rows, 2 * channels), bf16),
            V((toks, width), bf16),
            V((toks, width), bf16),
            V((16, keys + 4 * qw, channels), f32),
            V((2, full, channels), f32),
            V((rows, channels), bf16),
            V((full, 2 * channels), bf16),
            V((full, channels), f32),
            V((2, margin, channels), bf16),
            V((2, margin, channels), bf16),
            V((G, fold, early), bf16),
            V((G, fold, early), bf16),
            V((fold, early), bf16),
            V((Z, fold, early), bf16),
            V((G, fold, early), bf16),
            V((G, fold, late), bf16),
            V((G, fold, late), bf16),
            V((fold, late), bf16),
            V((Z, fold, late), bf16),
            V((G, fold, late), bf16),
            V((keys, channels), bf16),
            V((2 * channels, 2 * channels), bf16),
            DMA((14,)),
            DMA((12,)),
            DMA((12,)),
        ],
        compiler_params=pltpu.CompilerParams(
            collective_id=0, has_side_effects=True, vmem_limit_bytes=30 * 1024 * 1024
        ),
        name="atom_block",
    )(*[pltpu.with_memory_space_constraint(x, pltpu.HBM) for x in operands])
    done = pl.pallas_call(
        finish,
        out_shape=shapes,
        in_specs=[vmem_spec] * 9,
        out_specs=(any_spec,) * 9,
        scratch_shapes=[DMA((9,))],
        compiler_params=pltpu.CompilerParams(vmem_limit_bytes=4 * 1024 * 1024),
        name="finish",
    )(*outs)
    return done[:3] + (done[3].reshape(channels),) + done[4:]


def solution(mesh):
    return jax.shard_map(
        functools.partial(on_device, mesh.shape["atom"], mesh.shape["sample"]),
        mesh=mesh,
        in_specs=(
            P("sample", "atom", None),
            P(),
            P(),
            P(),
            P(),
            P(),
            P(),
            P("atom", None, None, None),
            P("atom"),
            P(),
            P("sample", "atom", None),
            P("sample", "atom", None),
        ),
        out_specs=(
            P("sample", "atom", None),
            P("sample", "atom", None),
            P("sample", "atom", None),
            P(),
            P(),
            P(),
            P(),
            P(),
            P(),
        ),
        check_vma=False,
    )
```

```python
import functools
import math

import jax
import jax.numpy as jnp
from jax import lax
from jax.experimental import pallas as pl
from jax.experimental.pallas import tpu as pltpu
from jax.sharding import PartitionSpec as P

MESH = pl.DeviceIdType.MESH
norm_eps = 1e-05
f32 = jnp.float32
bf16 = jnp.bfloat16


def nn(a, b):
    return lax.dot_general(a, b, (((1,), (0,)), ((), ())), preferred_element_type=f32)


def nt(a, b):
    return lax.dot_general(a, b, (((1,), (1,)), ((), ())), preferred_element_type=f32)


def tn(a, b):
    return lax.dot_general(a, b, (((0,), (0,)), ((), ())), preferred_element_type=f32)


def kernel(
    sizes,
    state_hbm,
    gain_hbm,
    wq_hbm,
    wk_hbm,
    wv_hbm,
    wo_hbm,
    wt_hbm,
    bias_hbm,
    start_hbm,
    token_hbm,
    cots_hbm,
    ctok_hbm,
    state_out_ref,
    rows_out_ref,
    grad_out_ref,
    gain_out,
    query_out,
    key_out,
    value_out,
    output_out,
    token_out,
    gain_ref,
    start_ref,
    token_ref,
    state,
    w3,
    wo,
    wt,
    bias,
    cots,
    ctok,
    ctok_low,
    halo,
    unit,
    inverse,
    normed,
    queries,
    kvf,
    kvw,
    probs,
    attended,
    sel_cat,
    sel_t,
    sel_tlow,
    tokens_back,
    inv_own,
    silu,
    active,
    state_back,
    attended_back,
    low_part,
    high_part,
    shift,
    spread,
    query_back,
    spread_low,
    nback,
    nback_send,
    nback_recv,
    e_src,
    e_rx1,
    e_sum,
    e_rx2,
    e_fin,
    l_src,
    l_rx1,
    l_sum,
    l_rx2,
    l_fin,
    head_mask,
    mean_mat,
    load_sem,
    send_sem,
    recv_sem,
):
    A, B, planes, rows, channels, windows, heads, qw, keys, toks, width = sizes
    state_out, grad_out = state_out_ref.at[0], grad_out_ref.at[0]
    margin = keys // 2 + qw // 2
    full = rows + 2 * margin
    span = keys + 2 * qw
    head_dim = channels // heads
    factor = head_dim ** (-0.5)
    G = A * planes
    Z = B // planes
    half = 2 * channels // G
    me = lax.axis_index("atom")
    smp = lax.axis_index("sample")
    left = {"atom": lax.rem(me + A - 1, A)}
    right = {"atom": lax.rem(me + 1, A)}

    tile = rows // 128
    below = pl.multiple_of(jnp.maximum(me - 1, 0) * tile, 8)
    above = pl.multiple_of(jnp.minimum(me + 1, A - 1) * tile, 8)

    def load(src, dst, index):
        return pltpu.make_async_copy(src, dst, load_sem.at[index])

    loads = [
        load(state_hbm.at[0], state, 0),
        load(wq_hbm, w3.at[:, pl.ds(0, channels)], 1),
        load(wk_hbm, w3.at[:, pl.ds(channels, channels)], 2),
        load(wv_hbm, w3.at[:, pl.ds(2 * channels, channels)], 3),
        load(bias_hbm, bias, 4),
        load(wo_hbm, wo, 5),
        load(wt_hbm, wt, 6),
        load(cots_hbm.at[0], cots, 7),
        load(ctok_hbm.at[0], ctok, 8),
        load(gain_hbm, gain_ref, 9),
        load(start_hbm, start_ref, 10),
        load(token_hbm.at[pl.ds(below, tile)], token_ref.at[pl.ds(0, tile)], 11),
        load(token_hbm.at[pl.ds(pl.multiple_of(me * tile, 8), tile)], token_ref.at[pl.ds(tile, tile)], 12),
        load(token_hbm.at[pl.ds(above, tile)], token_ref.at[pl.ds(2 * tile, tile)], 13),
    ]
    for index in (0, 9, 1, 2, 3, 11, 12, 13):
        loads[index].start()

    barrier = pltpu.get_barrier_semaphore()

    plane_pos = lax.div(smp, Z)
    rank = plane_pos * A + me
    depth = lax.rem(smp, Z)

    near_line = smp - depth
    far_line = lax.rem(near_line + Z, B)

    def line_peer(q):
        return {"sample": near_line + q}

    def greet(device):
        pl.semaphore_signal(barrier, inc=1, device_id=device, device_id_type=MESH)
        return 0

    def greet_near(i, _):
        return greet({"atom": lax.rem(me + i, A)})

    def greet_far(i, _):
        return greet({"sample": far_line + depth, "atom": i})

    def greet_line(i, _):
        return greet(line_peer(lax.rem(depth + i, Z)))

    greet(right)
    greet(left)
    lax.fori_loop(2, A - 1, greet_near, 0)
    lax.fori_loop(0, A, greet_far, 0)
    lax.fori_loop(1, Z, greet_line, 0)

    for index in (8, 10, 4, 6, 5, 7):
        loads[index].start()

    def send(src, dst, index, device):
        return pltpu.make_async_remote_copy(
            src_ref=src,
            dst_ref=dst,
            send_sem=send_sem.at[index],
            recv_sem=recv_sem.at[index],
            device_id=device,
            device_id_type=MESH,
        )

    def wait_bytes(ref, sem):
        pltpu.make_async_copy(ref, ref, sem).wait()

    def norm(x):
        average = nn(x, mean_mat[pl.ds(0, channels), pl.ds(0, channels)])
        centred = x.astype(f32) - average
        square = (centred * centred).astype(bf16)
        variance = nn(square, mean_mat[pl.ds(0, channels), pl.ds(0, channels)])
        inv = lax.rsqrt(variance + norm_eps)
        unit_rows = centred * inv
        return unit_rows, inv, (unit_rows * gain_ref[...]).astype(bf16)

    for index in (0, 1, 2, 3, 9):
        loads[index].wait()

    lanes = lax.broadcasted_iota(jnp.int32, (keys, channels), 1)
    subs = lax.broadcasted_iota(jnp.int32, (keys, channels), 0)
    mean_mat[...] = jnp.zeros((2 * channels, 2 * channels), bf16)
    mean_mat[pl.ds(0, channels), pl.ds(0, channels)] = jnp.full(
        (channels, channels), 1.0 / channels, bf16
    )
    mean_mat[pl.ds(channels, channels), pl.ds(channels, channels)] = jnp.full(
        (channels, channels), 1.0 / channels, bf16
    )
    head_mask[...] = jnp.where(subs // qw == lanes // head_dim, 1.0, 0.0).astype(bf16)

    block = 256
    group = 16

    spots = [pl.ds(r, block) for r in range(0, rows, block)]
    wides = [state[here, :] for here in spots]
    means = [nn(x, mean_mat[pl.ds(0, channels), pl.ds(0, channels)]) for x in wides]
    centres = [x.astype(f32) - average for x, average in zip(wides, means)]
    spreads = [
        nn((x * x).astype(bf16), mean_mat[pl.ds(0, channels), pl.ds(0, channels)])
        for x in centres
    ]
    lows = []
    for r, x, variance in zip(range(0, rows, block), centres, spreads):
        inv = lax.rsqrt(variance + norm_eps)
        unit_rows = x * inv
        unit[pl.ds(margin + r, block), :] = unit_rows
        inverse[pl.ds(r, block), :] = inv
        lows.append((unit_rows * gain_ref[...]).astype(bf16))
        normed[pl.ds(margin + r, block), :] = lows[-1]
    for r, low in zip(range(0, rows, block), lows):
        qkv = nn(low, w3[...]).astype(bf16)
        queries[pl.ds(r, block), :] = qkv[:, :channels]
        kvf[0, pl.ds(margin + r, block), :] = qkv[:, channels : 2 * channels].astype(f32)
        kvf[1, pl.ds(margin + r, block), :] = qkv[:, 2 * channels :].astype(f32)

    pl.semaphore_wait(barrier, G + Z - 2)

    halo_left = send(
        state_hbm.at[0, pl.ds(rows - margin, margin), :], halo.at[0], 0, right
    )
    halo_right = send(state_hbm.at[0, pl.ds(0, margin), :], halo.at[1], 1, left)
    tokens_up = send(ctok_hbm.at[0], ctok_low, 2, right)
    halo_left.start()
    halo_right.start()
    tokens_up.start()

    for index in (11, 12, 13):
        loads[index].wait()
    spread[...] = jnp.zeros((2, full, channels), f32)
    for slot in range(2 * group):
        shift[slot, pl.ds(0, 2 * qw), :] = jnp.zeros((2 * qw, channels), f32)
        shift[slot, pl.ds(2 * qw + keys, 2 * qw), :] = jnp.zeros((2 * qw, channels), f32)

    base = (me * toks).astype(f32)
    lower = base - toks
    sub_id = subs.astype(f32)
    lane_id = lanes.astype(f32)
    count_own = jnp.zeros((toks, 128), f32)
    count_low = jnp.zeros((toks, 128), f32)
    for r in range(tile):
        row = token_ref[pl.ds(tile + r, 1), :].astype(f32)
        spot = jnp.broadcast_to(row, (128, 128))
        hit = jnp.where(spot - base == sub_id, 1.0, 0.0)
        count_own = count_own + hit
        sel_t[:, pl.ds(r * 128, 128)] = hit.astype(bf16)
        if r < 2:
            hit = jnp.where(spot - lower == sub_id, 1.0, 0.0)
            count_low = count_low + hit
            sel_tlow[:, pl.ds(r * 128, 128)] = hit.astype(bf16)
        column = (spot - lower).astype(bf16).T.astype(f32)
        here = pl.ds(r * 128, 128)
        sel_cat[here, pl.ds(128, 128)] = jnp.where(column == lane_id + toks, 1.0, 0.0).astype(bf16)
        if r < 2:
            sel_cat[here, pl.ds(0, 128)] = jnp.where(column == lane_id, 1.0, 0.0).astype(bf16)
    has_above = jnp.where(me < A - 1, 1.0, 0.0)
    for r in range(2):
        row = token_ref[pl.ds(2 * tile + r, 1), :].astype(f32)
        spot = jnp.broadcast_to(row, (128, 128))
        count_own = count_own + jnp.where(spot - base == sub_id, has_above, 0.0)
    has_below = jnp.where(me > 0, 1.0, 0.0)
    for r in range(tile):
        row = token_ref[pl.ds(r, 1), :].astype(f32)
        spot = jnp.broadcast_to(row, (128, 128))
        count_low = count_low + jnp.where(spot - lower == sub_id, has_below, 0.0)

    def inverted(count):
        total = jnp.sum(count, axis=-1, keepdims=True)
        return jnp.where(total > 0.0, 1.0 / jnp.maximum(total, 1.0), 0.0)

    inverse_own = inverted(count_own)
    inverse_low = inverted(count_low)
    inv_own[...] = jnp.broadcast_to(inverse_own, (toks, 128))

    loads[8].wait()
    tokens_back[pl.ds(toks, toks), :] = (ctok[...].astype(f32) * inverse_own).astype(bf16)

    first_atom = me * rows
    last_base = A * rows - span

    def spread_heads(x):
        return jnp.concatenate([x] * heads, axis=0) * head_mask[...]

    def gather_heads(x):
        lane = lax.broadcasted_iota(jnp.int32, (qw, channels), 1)
        out = x[0:qw]
        for h in range(1, heads):
            out = jnp.where(lane >= h * head_dim, x[h * qw : (h + 1) * qw], out)
        return out

    def forward(ws):
        queries_of, keys_of, values_of, scores, weights, mixes = [], [], [], [], [], []
        for w in ws:
            place = jnp.clip(start_ref[w] - first_atom + margin, 0, full - keys)
            keys_of.append(kvf[0, pl.ds(place, keys), :].astype(bf16))
            values_of.append(kvf[1, pl.ds(place, keys), :].astype(bf16))
            q0 = pl.multiple_of(w * qw, qw)
            queries_of.append(spread_heads(queries[pl.ds(q0, qw), :]))
        for w, q, k in zip(ws, queries_of, keys_of):
            scores.append(nt(q, k) * factor + bias[w])
        for s in scores:
            weights.append(jnp.exp(s - jnp.max(s, axis=-1, keepdims=True)))
        ones = jnp.ones((keys, channels), bf16)
        for e, v in zip(weights, values_of):
            mixes.append(nn(e.astype(bf16), jnp.concatenate([v, ones], axis=1)))
        for w, e, mixed, k, v in zip(ws, weights, mixes, keys_of, values_of):
            scale = 1.0 / mixed[:, channels:]
            probs[w] = (e * scale).astype(bf16)
            q0 = pl.multiple_of(w * qw, qw)
            attended[pl.ds(q0, qw), :] = gather_heads(mixed[:, :channels] * scale).astype(bf16)
            kvw[w, :, pl.ds(0, channels)] = k
            kvw[w, :, pl.ds(channels, channels)] = v

    near = group // 2
    loads[4].wait()
    loads[10].wait()

    def forward_group(i, _):
        forward([lax.rem(group * i + j + near, windows) for j in range(group)])
        return 0

    inner = windows // group - 1
    lax.fori_loop(0, inner, forward_group, 0)

    halo_left.wait_recv()
    halo_right.wait_recv()
    for side in range(2):
        there = (me > 0) if side == 0 else (me < A - 1)
        at = 0 if side == 0 else margin + rows
        keep = jnp.where(there, 1.0, 0.0)
        x = jnp.where(jnp.full((margin, channels), keep) > 0.0, halo[side].astype(f32), 0.0)
        unit_rows, _, low = norm(x.astype(bf16))
        unit[pl.ds(at, margin), :] = unit_rows
        normed[pl.ds(at, margin), :] = low
        kv = nn(low, w3[:, channels:]).astype(bf16).astype(f32)
        kvf[0, pl.ds(at, margin), :] = kv[:, :channels]
        kvf[1, pl.ds(at, margin), :] = kv[:, channels:]

    lax.fori_loop(inner, inner + 1, forward_group, 0)

    for index in range(5, 8):
        loads[index].wait()

    def token_columns(here, picked):
        for column in range(0, width, 256):
            part = pl.ds(column, 256)
            before = nn(state_out[here, :], wt[:, part])
            sigma = 0.5 * jnp.tanh(0.5 * before) + 0.5
            act = before * sigma
            silu[here, part] = act.astype(bf16)
            slope = sigma + act - act * sigma
            per_atom = nn(sel_cat[here, picked], tokens_back[picked, part])
            active[here, part] = (per_atom * slope).astype(bf16)

    def token_stage(r0, count):
        spots = [pl.ds(r, block) for r in range(r0, r0 + count, block)]
        for here in spots:
            state_out[here, :] = (
                state[here, :].astype(f32) + nn(attended[here, :], wo[...])
            ).astype(bf16)
        for here in spots[1:]:
            token_columns(here, slice(toks, 2 * toks))
        tokens_up.wait_recv()
        tokens_back[pl.ds(0, toks), :] = (ctok_low[...].astype(f32) * inverse_low).astype(bf16)
        token_columns(spots[0], slice(0, 2 * toks))
        for here in spots:
            state_back[here, :] = (
                cots[here, :].astype(f32) + nt(active[here, :], wt[...])
            ).astype(bf16)
        for here in spots:
            aback = nt(state_back[here, :], wo[...]).astype(bf16)
            attended_back[here, pl.ds(0, channels)] = aback
            attended_back[here, pl.ds(channels, channels)] = (
                -aback.astype(f32) * attended[here, :].astype(f32)
            ).astype(bf16)

    token_stage(0, rows)
    low_part[...] = nn(sel_tlow[...], silu[pl.ds(0, 256), :]).astype(bf16)
    part_down = send(low_part, high_part, 3, left)
    part_down.start()

    def stacked(x, y):
        return jnp.concatenate(
            [x.reshape(G // 2, half, channels), y.reshape(G // 2, half, channels)], axis=1
        ).astype(bf16)

    first, second = pl.ds(0, G // 2), pl.ds(G // 2, G // 2)

    token_sum = tn(state_out[...], active[...])
    pieces = [token_sum[:, c : c + channels] for c in range(0, width, channels)]
    output_sum = tn(attended[...], state_back[...])
    output_high = output_sum.astype(bf16).astype(f32)
    e_src[first, :, pl.ds(0, channels)] = stacked(pieces[0], pieces[1])
    e_src[first, :, pl.ds(channels, channels)] = stacked(pieces[2], pieces[3])
    e_src[second, :, pl.ds(0, channels)] = stacked(pieces[4], pieces[5])
    e_src[second, :, pl.ds(channels, channels)] = stacked(output_high, output_sum - output_high)

    far_first = lax.rem(plane_pos + 1, planes) * A
    near_first = plane_pos * A

    def to_plane(start_one):
        def far(i, _):
            atom = lax.rem(me + A // 4 + i, A)
            start_one(far_first + atom, A + i, {"sample": far_line + depth, "atom": atom})
            return 0

        def near(i, _):
            atom = lax.rem(me + i, A)
            start_one(near_first + atom, i, {"atom": atom})
            return 0

        lax.fori_loop(0, A, far, 0)
        lax.fori_loop(1, A, near, 0)

    def scatter(src, rx, index):
        to_plane(lambda peer, slot, device: send(src.at[peer], rx.at[slot], index, device).start())

    def scattered(src, rx, part, rx2, index):
        wait_bytes(rx.at[pl.ds(1, G - 1)], recv_sem.at[index])
        total = src[rank].astype(f32)
        for d in range(1, G):
            total = total + rx[d].astype(f32)
        low = total.astype(bf16)
        part[...] = low
        rx2[depth] = low

    def exchange(part, rx2, index):
        def one(d, _):
            peer = lax.rem(depth + d, Z)
            send(part, rx2.at[depth], index, line_peer(peer)).start()
            return 0

        lax.fori_loop(1, Z, one, 0)

    def exchanged(rx2, fin, index):
        wait_bytes(rx2.at[pl.ds(0, Z - 1)], recv_sem.at[index])
        total = rx2[0].astype(f32)
        for d in range(1, Z):
            total = total + rx2[d].astype(f32)
        fin[rank] = total.astype(bf16)

    def gather(fin, index):
        to_plane(
            lambda peer, slot, device: send(fin.at[rank], fin.at[rank], index, device).start()
        )

    def gathered(fin, index):
        wait_bytes(fin.at[pl.ds(0, G - 1)], recv_sem.at[index])

    scatter(e_src, e_rx1, 4)

    def backward(ws, slots):
        state_of = []
        for w in ws:
            kv = kvw[w]
            q0 = pl.multiple_of(w * qw, qw)
            q = spread_heads(queries[pl.ds(q0, qw), :])
            da = spread_heads(attended_back[pl.ds(q0, qw), pl.ds(0, channels)])
            delta = spread_heads(attended_back[pl.ds(q0, qw), pl.ds(channels, channels)])
            state_of.append((kv, q0, q, da, delta, probs[w]))
        ones = jnp.ones((keys, channels), bf16)
        centred = [
            nt(
                jnp.concatenate([da, delta], axis=1),
                jnp.concatenate([kv[:, channels:], ones], axis=1),
            )
            for kv, q0, q, da, delta, p in state_of
        ]
        lows = [
            (st[5].astype(f32) * c).astype(bf16) for st, c in zip(state_of, centred)
        ]
        for ds, (kv, q0, q, da, delta, p) in zip(lows, state_of):
            dq = gather_heads(nn(ds, kv[:, :channels]))
            query_back[pl.ds(q0, qw), :] = (dq * factor).astype(bf16)
        for slot, ds, (kv, q0, q, da, delta, p) in zip(slots, lows, state_of):
            shift[2 * slot, pl.ds(2 * qw, keys), :] = tn(ds, q) * factor
            shift[2 * slot + 1, pl.ds(2 * qw, keys), :] = tn(p, da)
        for w, slot in zip(ws, slots):
            base_atom = jnp.clip(first_atom + w * qw - margin, 0, last_base)
            off = jnp.clip(start_ref[w] - base_atom, 0, 2 * qw)
            to = pl.ds(pl.multiple_of(base_atom - first_atom + margin, 16), span)
            for part in range(2):
                moved = shift[2 * slot + part, pl.ds(2 * qw - off, span), :]
                spread[part, to, :] = spread[part, to, :] + moved

    def backward_group(i, _):
        backward([group * i + j for j in range(group)], list(range(group)))
        return 0

    lax.fori_loop(0, windows // group, backward_group, 0)

    own = pl.ds(margin, rows)
    spread_low[:, pl.ds(0, channels)] = spread[0].astype(bf16)
    spread_low[:, pl.ds(channels, channels)] = spread[1].astype(bf16)
    query_sum = tn(normed[own, :], query_back[...])
    pair_sum = tn(normed[...], spread_low[...])
    weighted = (
        w3[:, :channels].astype(f32) * query_sum
        + w3[:, channels : 2 * channels].astype(f32) * pair_sum[:, :channels]
        + w3[:, 2 * channels :].astype(f32) * pair_sum[:, channels:]
    )
    gain_part = jnp.sum(weighted.T.reshape(channels // 8, 8, channels), axis=0) / gain_ref[...]
    gain_rows = jnp.concatenate([gain_part, jnp.zeros((channels - 8, channels), f32)], axis=0)
    l_src[first] = stacked(query_sum, pair_sum[:, :channels])
    l_src[second] = stacked(pair_sum[:, channels:], gain_rows)
    scatter(l_src, l_rx1, 9)

    nback[...] = nt(spread_low[...], w3[:, channels:])
    nback_send[0] = nback[pl.ds(0, margin), :].astype(bf16)
    nback_send[1] = nback[pl.ds(margin + rows, margin), :].astype(bf16)
    back_left = send(nback_send.at[0], nback_recv.at[1], 7, left)
    back_right = send(nback_send.at[1], nback_recv.at[0], 8, right)
    back_left.start()
    back_right.start()
    nback[own, :] = nback[own, :] + nt(query_back[...], w3[:, :channels])

    part_down.wait_recv()
    own_part = nn(sel_t[...], silu[...])
    rows_out_ref[0] = (
        (own_part + high_part[...].astype(f32)) * inv_own[:, pl.ds(0, 1)]
    ).astype(bf16)

    def norm_back(r, count, extra):
        here = pl.ds(r, count)
        there = pl.ds(margin + r, count)
        nb = nback[there, :]
        if extra is not None:
            nb = nb + extra
        ub = nb * gain_ref[...]
        un = unit[there, :]
        means = nn(jnp.concatenate([ub, ub * un], axis=1).astype(bf16), mean_mat[...])
        grad_out[here, :] = state_back[here, :].astype(f32) + inverse[here, :] * (
            ub - means[:, :channels] - un * means[:, channels:]
        )

    for r in range(0, rows - 2 * margin, 288):
        norm_back(margin + r, min(288, rows - 2 * margin - r), None)
    scattered(e_src, e_rx1, e_sum, e_rx2, 4)
    exchange(e_sum, e_rx2, 5)
    scattered(l_src, l_rx1, l_sum, l_rx2, 9)
    exchange(l_sum, l_rx2, 10)
    exchanged(e_rx2, e_fin, 5)
    gather(e_fin, 6)
    back_left.wait_recv()
    back_right.wait_recv()
    norm_back(0, margin, nback_recv[0].astype(f32))
    norm_back(rows - margin, margin, nback_recv[1].astype(f32))
    exchanged(l_rx2, l_fin, 10)
    gather(l_fin, 11)
    gathered(e_fin, 6)
    scale = 1.0 / math.sqrt(B * A * rows)
    upper, lower = slice(0, half), slice(half, 2 * half)

    def matrix(ref, part, piece, column):
        chunk = ref[part, piece, column * channels : (column + 1) * channels]
        return chunk.astype(f32).reshape(channels, channels) * scale

    for index, (part, column) in enumerate(((first, 0), (first, 1), (second, 0))):
        for k, piece in enumerate((upper, lower)):
            to = pl.ds((2 * index + k) * channels, channels)
            token_out[:, to] = matrix(e_fin, part, piece, column)
    output_out[...] = matrix(e_fin, second, upper, 1) + matrix(e_fin, second, lower, 1)
    gathered(l_fin, 11)
    query_out[...] = matrix(l_fin, first, upper, 0)
    key_out[...] = matrix(l_fin, first, lower, 0)
    value_out[...] = matrix(l_fin, second, upper, 0)
    gain_out[...] = jnp.sum(matrix(l_fin, second, lower, 0), axis=0, keepdims=True)

    for copy in (halo_left, halo_right, tokens_up, part_down, back_left, back_right):
        copy.wait_send()
    for index, ref, count in (
        (4, e_rx1, G),
        (5, e_rx2, Z),
        (6, e_fin, G),
        (9, l_rx1, G),
        (10, l_rx2, Z),
        (11, l_fin, G),
    ):
        wait_bytes(ref.at[pl.ds(0, count - 1)], send_sem.at[index])


def finish(*refs):
    count = len(refs) // 2
    copies = [
        pltpu.make_async_copy(refs[index], refs[count + index], refs[-1].at[index])
        for index in range(count)
    ]
    for copy in copies:
        copy.start()
    for copy in copies:
        copy.wait()


def on_device(
    A,
    B,
    atom_state,
    norm_gain,
    query_weight,
    key_weight,
    value_weight,
    out_weight,
    token_weight,
    pair_bias,
    key_start,
    atom_token,
    cotangent_state,
    cotangent_tokens,
):
    _, rows, channels = atom_state.shape
    windows, heads, qw, keys = pair_bias.shape
    toks, width = cotangent_tokens.shape[1:]
    planes = 2
    sizes = (A, B, planes, rows, channels, windows, heads, qw, keys, toks, width)
    margin = keys // 2 + qw // 2
    full = rows + 2 * margin
    span = keys + 2 * qw
    G = A * planes
    Z = B // planes
    fold = 4 * channels // G
    early = 2 * channels
    late = channels
    any_spec = pl.BlockSpec(memory_space=pltpu.HBM)
    V = pltpu.VMEM
    DMA = pltpu.SemaphoreType.DMA
    vmem_spec = pl.BlockSpec(memory_space=pltpu.VMEM)
    square = jax.ShapeDtypeStruct((channels, channels), f32)
    shapes = (
        jax.ShapeDtypeStruct((1, rows, channels), bf16),
        jax.ShapeDtypeStruct((1, toks, width), bf16),
        jax.ShapeDtypeStruct((1, rows, channels), f32),
        jax.ShapeDtypeStruct((1, channels), f32),
        square,
        square,
        square,
        square,
        jax.ShapeDtypeStruct((channels, width), f32),
    )
    operands = (
        atom_state,
        norm_gain.reshape(1, channels),
        query_weight,
        key_weight,
        value_weight,
        out_weight,
        token_weight,
        pair_bias.reshape(windows, heads * qw, keys),
        key_start,
        atom_token.reshape(-1, 128),
        cotangent_state,
        cotangent_tokens,
    )
    outs = pl.pallas_call(
        functools.partial(kernel, sizes),
        out_shape=shapes,
        in_specs=[any_spec] * 12,
        out_specs=(vmem_spec,) * 9,
        scratch_shapes=[
            V((1, channels), f32),
            pltpu.SMEM((windows,), jnp.int32),
            V((3 * rows // 128, 128), jnp.int32),
            V((rows, channels), bf16),
            V((channels, 3 * channels), bf16),
            V((channels, channels), bf16),
            V((channels, width), bf16),
            V((windows, heads * qw, keys), f32),
            V((rows, channels), bf16),
            V((toks, width), bf16),
            V((toks, width), bf16),
            V((2, margin, channels), bf16),
            V((full, channels), f32),
            V((rows, channels), f32),
            V((full, channels), bf16),
            V((rows, channels), bf16),
            V((2, full, channels), f32),
            V((windows, keys, 2 * channels), bf16),
            V((windows, heads * qw, keys), bf16),
            V((rows, channels), bf16),
            V((rows, 2 * toks), bf16),
            V((toks, rows), bf16),
            V((toks, 256), bf16),
            V((2 * toks, width), bf16),
            V((toks, 128), f32),
            V((rows, width), bf16),
            V((rows, width), bf16),
            V((rows, channels), bf16),
            V((rows, 2 * channels), bf16),
            V((toks, width), bf16),
            V((toks, width), bf16),
            V((32, keys + 4 * qw, channels), f32),
            V((2, full, channels), f32),
            V((rows, channels), bf16),
            V((full, 2 * channels), bf16),
            V((full, channels), f32),
            V((2, margin, channels), bf16),
            V((2, margin, channels), bf16),
            V((G, fold, early), bf16),
            V((G, fold, early), bf16),
            V((fold, early), bf16),
            V((Z, fold, early), bf16),
            V((G, fold, early), bf16),
            V((G, fold, late), bf16),
            V((G, fold, late), bf16),
            V((fold, late), bf16),
            V((Z, fold, late), bf16),
            V((G, fold, late), bf16),
            V((keys, channels), bf16),
            V((2 * channels, 2 * channels), bf16),
            DMA((14,)),
            DMA((12,)),
            DMA((12,)),
        ],
        compiler_params=pltpu.CompilerParams(
            collective_id=0, has_side_effects=True, vmem_limit_bytes=30 * 1024 * 1024
        ),
        name="atom_block",
    )(*[pltpu.with_memory_space_constraint(x, pltpu.HBM) for x in operands])
    done = pl.pallas_call(
        finish,
        out_shape=shapes,
        in_specs=[vmem_spec] * 9,
        out_specs=(any_spec,) * 9,
        scratch_shapes=[DMA((9,))],
        compiler_params=pltpu.CompilerParams(vmem_limit_bytes=4 * 1024 * 1024),
        name="finish",
    )(*outs)
    return done[:3] + (done[3].reshape(channels),) + done[4:]


def solution(mesh):
    return jax.shard_map(
        functools.partial(on_device, mesh.shape["atom"], mesh.shape["sample"]),
        mesh=mesh,
        in_specs=(
            P("sample", "atom", None),
            P(),
            P(),
            P(),
            P(),
            P(),
            P(),
            P("atom", None, None, None),
            P("atom"),
            P(),
            P("sample", "atom", None),
            P("sample", "atom", None),
        ),
        out_specs=(
            P("sample", "atom", None),
            P("sample", "atom", None),
            P("sample", "atom", None),
            P(),
            P(),
            P(),
            P(),
            P(),
            P(),
        ),
        check_vma=False,
    )
```

```python
import functools
import math

import jax
import jax.numpy as jnp
from jax import lax
from jax.experimental import pallas as pl
from jax.experimental.pallas import tpu as pltpu
from jax.sharding import PartitionSpec as P

MESH = pl.DeviceIdType.MESH
norm_eps = 1e-05
f32 = jnp.float32
bf16 = jnp.bfloat16


def nn(a, b):
    return lax.dot_general(a, b, (((1,), (0,)), ((), ())), preferred_element_type=f32)


def nt(a, b):
    return lax.dot_general(a, b, (((1,), (1,)), ((), ())), preferred_element_type=f32)


def tn(a, b):
    return lax.dot_general(a, b, (((0,), (0,)), ((), ())), preferred_element_type=f32)


def kernel(
    sizes,
    state_hbm,
    gain_hbm,
    wq_hbm,
    wk_hbm,
    wv_hbm,
    wo_hbm,
    wt_hbm,
    bias_hbm,
    start_hbm,
    token_hbm,
    cots_hbm,
    ctok_hbm,
    state_out_ref,
    rows_out_ref,
    grad_out_ref,
    gain_out,
    query_out,
    key_out,
    value_out,
    output_out,
    token_out,
    gain_ref,
    start_ref,
    token_ref,
    state,
    w3,
    wo,
    wt,
    bias,
    cots,
    ctok,
    ctok_low,
    halo,
    unit,
    inverse,
    normed,
    queries,
    kvf,
    kvw,
    probs,
    attended,
    sel_cat,
    sel_t,
    sel_tlow,
    tokens_back,
    inv_own,
    silu,
    active,
    state_back,
    attended_back,
    low_part,
    high_part,
    shift,
    spread,
    query_back,
    spread_low,
    nback,
    nback_send,
    nback_recv,
    e_src,
    e_rx1,
    e_sum,
    e_rx2,
    e_fin,
    l_src,
    l_rx1,
    l_sum,
    l_rx2,
    l_fin,
    head_mask,
    mean_mat,
    load_sem,
    send_sem,
    recv_sem,
):
    A, B, planes, rows, channels, windows, heads, qw, keys, toks, width = sizes
    state_out, grad_out = state_out_ref.at[0], grad_out_ref.at[0]
    margin = keys // 2 + qw // 2
    full = rows + 2 * margin
    span = keys + 2 * qw
    head_dim = channels // heads
    factor = head_dim ** (-0.5)
    G = A * planes
    Z = B // planes
    half = 2 * channels // G
    me = lax.axis_index("atom")
    smp = lax.axis_index("sample")
    left = {"atom": lax.rem(me + A - 1, A)}
    right = {"atom": lax.rem(me + 1, A)}

    tile = rows // 128
    below = pl.multiple_of(jnp.maximum(me - 1, 0) * tile, 8)
    above = pl.multiple_of(jnp.minimum(me + 1, A - 1) * tile, 8)

    def load(src, dst, index):
        return pltpu.make_async_copy(src, dst, load_sem.at[index])

    loads = [
        load(state_hbm.at[0], state, 0),
        load(wq_hbm, w3.at[:, pl.ds(0, channels)], 1),
        load(wk_hbm, w3.at[:, pl.ds(channels, channels)], 2),
        load(wv_hbm, w3.at[:, pl.ds(2 * channels, channels)], 3),
        load(bias_hbm, bias, 4),
        load(wo_hbm, wo, 5),
        load(wt_hbm, wt, 6),
        load(cots_hbm.at[0], cots, 7),
        load(ctok_hbm.at[0], ctok, 8),
        load(gain_hbm, gain_ref, 9),
        load(start_hbm, start_ref, 10),
        load(token_hbm.at[pl.ds(below, tile)], token_ref.at[pl.ds(0, tile)], 11),
        load(token_hbm.at[pl.ds(pl.multiple_of(me * tile, 8), tile)], token_ref.at[pl.ds(tile, tile)], 12),
        load(token_hbm.at[pl.ds(above, tile)], token_ref.at[pl.ds(2 * tile, tile)], 13),
    ]
    for index in (0, 9, 1, 2, 3, 11, 12, 13):
        loads[index].start()

    barrier = pltpu.get_barrier_semaphore()

    plane_pos = lax.div(smp, Z)
    rank = plane_pos * A + me
    depth = lax.rem(smp, Z)

    near_line = smp - depth
    far_line = lax.rem(near_line + Z, B)

    def line_peer(q):
        return {"sample": near_line + q}

    def greet(device):
        pl.semaphore_signal(barrier, inc=1, device_id=device, device_id_type=MESH)
        return 0

    def greet_near(i, _):
        return greet({"atom": lax.rem(me + i, A)})

    def greet_far(i, _):
        return greet({"sample": far_line + depth, "atom": i})

    def greet_line(i, _):
        return greet(line_peer(lax.rem(depth + i, Z)))

    greet(right)
    greet(left)
    lax.fori_loop(2, A - 1, greet_near, 0)
    lax.fori_loop(0, A, greet_far, 0)
    lax.fori_loop(1, Z, greet_line, 0)

    for index in (8, 10, 4, 6, 5, 7):
        loads[index].start()

    def send(src, dst, index, device):
        return pltpu.make_async_remote_copy(
            src_ref=src,
            dst_ref=dst,
            send_sem=send_sem.at[index],
            recv_sem=recv_sem.at[index],
            device_id=device,
            device_id_type=MESH,
        )

    def wait_bytes(ref, sem):
        pltpu.make_async_copy(ref, ref, sem).wait()

    def norm(x):
        average = nn(x, mean_mat[pl.ds(0, channels), pl.ds(0, channels)])
        centred = x.astype(f32) - average
        square = (centred * centred).astype(bf16)
        variance = nn(square, mean_mat[pl.ds(0, channels), pl.ds(0, channels)])
        inv = lax.rsqrt(variance + norm_eps)
        unit_rows = centred * inv
        return unit_rows, inv, (unit_rows * gain_ref[...]).astype(bf16)

    for index in (0, 1, 2, 3, 9):
        loads[index].wait()

    lanes = lax.broadcasted_iota(jnp.int32, (keys, channels), 1)
    subs = lax.broadcasted_iota(jnp.int32, (keys, channels), 0)
    mean_mat[...] = jnp.zeros((2 * channels, 2 * channels), bf16)
    mean_mat[pl.ds(0, channels), pl.ds(0, channels)] = jnp.full(
        (channels, channels), 1.0 / channels, bf16
    )
    mean_mat[pl.ds(channels, channels), pl.ds(channels, channels)] = jnp.full(
        (channels, channels), 1.0 / channels, bf16
    )
    head_mask[...] = jnp.where(subs // qw == lanes // head_dim, 1.0, 0.0).astype(bf16)

    block = 256
    group = 16

    spots = [pl.ds(r, block) for r in range(0, rows, block)]
    wides = [state[here, :] for here in spots]
    means = [nn(x, mean_mat[pl.ds(0, channels), pl.ds(0, channels)]) for x in wides]
    centres = [x.astype(f32) - average for x, average in zip(wides, means)]
    spreads = [
        nn((x * x).astype(bf16), mean_mat[pl.ds(0, channels), pl.ds(0, channels)])
        for x in centres
    ]
    lows = []
    for r, x, variance in zip(range(0, rows, block), centres, spreads):
        inv = lax.rsqrt(variance + norm_eps)
        unit_rows = x * inv
        unit[pl.ds(margin + r, block), :] = unit_rows
        inverse[pl.ds(r, block), :] = inv
        lows.append((unit_rows * gain_ref[...]).astype(bf16))
        normed[pl.ds(margin + r, block), :] = lows[-1]
    for r, low in zip(range(0, rows, block), lows):
        qkv = nn(low, w3[...]).astype(bf16)
        queries[pl.ds(r, block), :] = qkv[:, :channels]
        kvf[0, pl.ds(margin + r, block), :] = qkv[:, channels : 2 * channels].astype(f32)
        kvf[1, pl.ds(margin + r, block), :] = qkv[:, 2 * channels :].astype(f32)

    pl.semaphore_wait(barrier, G + Z - 2)

    halo_left = send(
        state_hbm.at[0, pl.ds(rows - margin, margin), :], halo.at[0], 0, right
    )
    halo_right = send(state_hbm.at[0, pl.ds(0, margin), :], halo.at[1], 1, left)
    tokens_up = send(ctok_hbm.at[0], ctok_low, 2, right)
    halo_left.start()
    halo_right.start()
    tokens_up.start()

    for index in (11, 12, 13):
        loads[index].wait()
    spread[...] = jnp.zeros((2, full, channels), f32)
    for slot in range(2 * group):
        shift[slot, pl.ds(0, 2 * qw), :] = jnp.zeros((2 * qw, channels), f32)
        shift[slot, pl.ds(2 * qw + keys, 2 * qw), :] = jnp.zeros((2 * qw, channels), f32)

    base = (me * toks).astype(f32)
    lower = base - toks
    sub_id = subs.astype(f32)
    lane_id = lanes.astype(f32)
    count_own = jnp.zeros((toks, 128), f32)
    count_low = jnp.zeros((toks, 128), f32)
    for r in range(tile):
        row = token_ref[pl.ds(tile + r, 1), :].astype(f32)
        spot = jnp.broadcast_to(row, (128, 128))
        hit = jnp.where(spot - base == sub_id, 1.0, 0.0)
        count_own = count_own + hit
        sel_t[:, pl.ds(r * 128, 128)] = hit.astype(bf16)
        if r < 2:
            hit = jnp.where(spot - lower == sub_id, 1.0, 0.0)
            count_low = count_low + hit
            sel_tlow[:, pl.ds(r * 128, 128)] = hit.astype(bf16)
        column = (spot - lower).astype(bf16).T.astype(f32)
        here = pl.ds(r * 128, 128)
        sel_cat[here, pl.ds(128, 128)] = jnp.where(column == lane_id + toks, 1.0, 0.0).astype(bf16)
        if r < 2:
            sel_cat[here, pl.ds(0, 128)] = jnp.where(column == lane_id, 1.0, 0.0).astype(bf16)
    has_above = jnp.where(me < A - 1, 1.0, 0.0)
    for r in range(2):
        row = token_ref[pl.ds(2 * tile + r, 1), :].astype(f32)
        spot = jnp.broadcast_to(row, (128, 128))
        count_own = count_own + jnp.where(spot - base == sub_id, has_above, 0.0)
    has_below = jnp.where(me > 0, 1.0, 0.0)
    for r in range(tile):
        row = token_ref[pl.ds(r, 1), :].astype(f32)
        spot = jnp.broadcast_to(row, (128, 128))
        count_low = count_low + jnp.where(spot - lower == sub_id, has_below, 0.0)

    def inverted(count):
        total = jnp.sum(count, axis=-1, keepdims=True)
        return jnp.where(total > 0.0, 1.0 / jnp.maximum(total, 1.0), 0.0)

    inverse_own = inverted(count_own)
    inverse_low = inverted(count_low)
    inv_own[...] = jnp.broadcast_to(inverse_own, (toks, 128))

    loads[8].wait()
    tokens_back[pl.ds(toks, toks), :] = (ctok[...].astype(f32) * inverse_own).astype(bf16)

    first_atom = me * rows
    last_base = A * rows - span

    def spread_heads(x):
        return jnp.concatenate([x] * heads, axis=0) * head_mask[...]

    def gather_heads(x):
        lane = lax.broadcasted_iota(jnp.int32, (qw, channels), 1)
        out = x[0:qw]
        for h in range(1, heads):
            out = jnp.where(lane >= h * head_dim, x[h * qw : (h + 1) * qw], out)
        return out

    def forward(ws):
        queries_of, keys_of, values_of, scores, weights, mixes = [], [], [], [], [], []
        for w in ws:
            place = jnp.clip(start_ref[w] - first_atom + margin, 0, full - keys)
            keys_of.append(kvf[0, pl.ds(place, keys), :].astype(bf16))
            values_of.append(kvf[1, pl.ds(place, keys), :].astype(bf16))
            q0 = pl.multiple_of(w * qw, qw)
            queries_of.append(spread_heads(queries[pl.ds(q0, qw), :]))
        for w, q, k in zip(ws, queries_of, keys_of):
            scores.append(nt(q, k) * factor + bias[w])
        for s in scores:
            weights.append(jnp.exp(s - jnp.max(s, axis=-1, keepdims=True)))
        ones = jnp.ones((keys, channels), bf16)
        for e, v in zip(weights, values_of):
            mixes.append(nn(e.astype(bf16), jnp.concatenate([v, ones], axis=1)))
        for w, e, mixed, k, v in zip(ws, weights, mixes, keys_of, values_of):
            scale = 1.0 / mixed[:, channels:]
            probs[w] = (e * scale).astype(bf16)
            q0 = pl.multiple_of(w * qw, qw)
            attended[pl.ds(q0, qw), :] = gather_heads(mixed[:, :channels] * scale).astype(bf16)
            kvw[w, :, pl.ds(0, channels)] = k
            kvw[w, :, pl.ds(channels, channels)] = v

    near = group // 2
    loads[4].wait()
    loads[10].wait()

    def forward_group(i, _):
        forward([lax.rem(group * i + j + near, windows) for j in range(group)])
        return 0

    inner = windows // group - 1
    lax.fori_loop(0, inner, forward_group, 0)

    halo_left.wait_recv()
    halo_right.wait_recv()
    for side in range(2):
        there = (me > 0) if side == 0 else (me < A - 1)
        at = 0 if side == 0 else margin + rows
        keep = jnp.where(there, 1.0, 0.0)
        x = jnp.where(jnp.full((margin, channels), keep) > 0.0, halo[side].astype(f32), 0.0)
        unit_rows, _, low = norm(x.astype(bf16))
        unit[pl.ds(at, margin), :] = unit_rows
        normed[pl.ds(at, margin), :] = low
        kv = nn(low, w3[:, channels:]).astype(bf16).astype(f32)
        kvf[0, pl.ds(at, margin), :] = kv[:, :channels]
        kvf[1, pl.ds(at, margin), :] = kv[:, channels:]

    lax.fori_loop(inner, inner + 1, forward_group, 0)

    for index in range(5, 8):
        loads[index].wait()

    def token_columns(here, picked):
        for column in range(0, width, 256):
            part = pl.ds(column, 256)
            before = nn(state_out[here, :], wt[:, part])
            sigma = 0.5 * jnp.tanh(0.5 * before) + 0.5
            act = before * sigma
            silu[here, part] = act.astype(bf16)
            slope = sigma + act - act * sigma
            per_atom = nn(sel_cat[here, picked], tokens_back[picked, part])
            active[here, part] = (per_atom * slope).astype(bf16)

    def token_stage(r0, count):
        spots = [pl.ds(r, block) for r in range(r0, r0 + count, block)]
        for here in spots:
            state_out[here, :] = (
                state[here, :].astype(f32) + nn(attended[here, :], wo[...])
            ).astype(bf16)
        for here in spots[1:]:
            token_columns(here, slice(toks, 2 * toks))
        tokens_up.wait_recv()
        tokens_back[pl.ds(0, toks), :] = (ctok_low[...].astype(f32) * inverse_low).astype(bf16)
        token_columns(spots[0], slice(0, 2 * toks))
        for here in spots:
            state_back[here, :] = (
                cots[here, :].astype(f32) + nt(active[here, :], wt[...])
            ).astype(bf16)
        for here in spots:
            aback = nt(state_back[here, :], wo[...]).astype(bf16)
            attended_back[here, pl.ds(0, channels)] = aback
            attended_back[here, pl.ds(channels, channels)] = (
                -aback.astype(f32) * attended[here, :].astype(f32)
            ).astype(bf16)

    token_stage(0, rows)
    low_part[...] = nn(sel_tlow[...], silu[pl.ds(0, 256), :]).astype(bf16)
    part_down = send(low_part, high_part, 3, left)
    part_down.start()

    def stacked(x, y):
        return jnp.concatenate(
            [x.reshape(G // 2, half, channels), y.reshape(G // 2, half, channels)], axis=1
        ).astype(bf16)

    first, second = pl.ds(0, G // 2), pl.ds(G // 2, G // 2)

    token_sum = tn(state_out[...], active[...])
    pieces = [token_sum[:, c : c + channels] for c in range(0, width, channels)]
    output_sum = tn(attended[...], state_back[...])
    output_high = output_sum.astype(bf16).astype(f32)
    e_src[first, :, pl.ds(0, channels)] = stacked(pieces[0], pieces[1])
    e_src[first, :, pl.ds(channels, channels)] = stacked(pieces[2], pieces[3])
    e_src[second, :, pl.ds(0, channels)] = stacked(pieces[4], pieces[5])
    e_src[second, :, pl.ds(channels, channels)] = stacked(output_high, output_sum - output_high)

    far_first = lax.rem(plane_pos + 1, planes) * A
    near_first = plane_pos * A

    def to_plane(start_one):
        def far(i, _):
            atom = lax.rem(me + A // 4 + i, A)
            start_one(far_first + atom, A + i, {"sample": far_line + depth, "atom": atom})
            return 0

        def near(i, _):
            atom = lax.rem(me + i, A)
            start_one(near_first + atom, i, {"atom": atom})
            return 0

        lax.fori_loop(0, A, far, 0, unroll=4)
        lax.fori_loop(1, A, near, 0, unroll=5)

    def scatter(src, rx, index):
        to_plane(lambda peer, slot, device: send(src.at[peer], rx.at[slot], index, device).start())

    def scattered(src, rx, part, rx2, index):
        wait_bytes(rx.at[pl.ds(1, G - 1)], recv_sem.at[index])
        total = src[rank].astype(f32)
        for d in range(1, G):
            total = total + rx[d].astype(f32)
        low = total.astype(bf16)
        part[...] = low
        rx2[depth] = low

    def exchange(part, rx2, index):
        def one(d, _):
            peer = lax.rem(depth + d, Z)
            send(part, rx2.at[depth], index, line_peer(peer)).start()
            return 0

        lax.fori_loop(1, Z, one, 0)

    def exchanged(rx2, fin, index):
        wait_bytes(rx2.at[pl.ds(0, Z - 1)], recv_sem.at[index])
        total = rx2[0].astype(f32)
        for d in range(1, Z):
            total = total + rx2[d].astype(f32)
        fin[rank] = total.astype(bf16)

    def gather(fin, index):
        to_plane(
            lambda peer, slot, device: send(fin.at[rank], fin.at[rank], index, device).start()
        )

    def gathered(fin, index):
        wait_bytes(fin.at[pl.ds(0, G - 1)], recv_sem.at[index])

    scatter(e_src, e_rx1, 4)

    def backward(ws, slots):
        state_of = []
        for w in ws:
            kv = kvw[w]
            q0 = pl.multiple_of(w * qw, qw)
            q = spread_heads(queries[pl.ds(q0, qw), :])
            da = spread_heads(attended_back[pl.ds(q0, qw), pl.ds(0, channels)])
            delta = spread_heads(attended_back[pl.ds(q0, qw), pl.ds(channels, channels)])
            state_of.append((kv, q0, q, da, delta, probs[w]))
        ones = jnp.ones((keys, channels), bf16)
        centred = [
            nt(
                jnp.concatenate([da, delta], axis=1),
                jnp.concatenate([kv[:, channels:], ones], axis=1),
            )
            for kv, q0, q, da, delta, p in state_of
        ]
        lows = [
            (st[5].astype(f32) * c).astype(bf16) for st, c in zip(state_of, centred)
        ]
        for ds, (kv, q0, q, da, delta, p) in zip(lows, state_of):
            dq = gather_heads(nn(ds, kv[:, :channels]))
            query_back[pl.ds(q0, qw), :] = (dq * factor).astype(bf16)
        for slot, ds, (kv, q0, q, da, delta, p) in zip(slots, lows, state_of):
            shift[2 * slot, pl.ds(2 * qw, keys), :] = tn(ds, q) * factor
            shift[2 * slot + 1, pl.ds(2 * qw, keys), :] = tn(p, da)
        for w, slot in zip(ws, slots):
            base_atom = jnp.clip(first_atom + w * qw - margin, 0, last_base)
            off = jnp.clip(start_ref[w] - base_atom, 0, 2 * qw)
            to = pl.ds(pl.multiple_of(base_atom - first_atom + margin, 16), span)
            for part in range(2):
                moved = shift[2 * slot + part, pl.ds(2 * qw - off, span), :]
                spread[part, to, :] = spread[part, to, :] + moved

    def backward_group(i, _):
        backward([group * i + j for j in range(group)], list(range(group)))
        return 0

    lax.fori_loop(0, windows // group, backward_group, 0)

    own = pl.ds(margin, rows)
    spread_low[:, pl.ds(0, channels)] = spread[0].astype(bf16)
    spread_low[:, pl.ds(channels, channels)] = spread[1].astype(bf16)
    query_sum = tn(normed[own, :], query_back[...])
    pair_sum = tn(normed[...], spread_low[...])
    weighted = (
        w3[:, :channels].astype(f32) * query_sum
        + w3[:, channels : 2 * channels].astype(f32) * pair_sum[:, :channels]
        + w3[:, 2 * channels :].astype(f32) * pair_sum[:, channels:]
    )
    gain_part = jnp.sum(weighted.T.reshape(channels // 8, 8, channels), axis=0) / gain_ref[...]
    gain_rows = jnp.concatenate([gain_part, jnp.zeros((channels - 8, channels), f32)], axis=0)
    l_src[first] = stacked(query_sum, pair_sum[:, :channels])
    l_src[second] = stacked(pair_sum[:, channels:], gain_rows)
    scatter(l_src, l_rx1, 9)

    nback[...] = nt(spread_low[...], w3[:, channels:])
    nback_send[0] = nback[pl.ds(0, margin), :].astype(bf16)
    nback_send[1] = nback[pl.ds(margin + rows, margin), :].astype(bf16)
    back_left = send(nback_send.at[0], nback_recv.at[1], 7, left)
    back_right = send(nback_send.at[1], nback_recv.at[0], 8, right)
    back_left.start()
    back_right.start()
    scattered(e_src, e_rx1, e_sum, e_rx2, 4)
    exchange(e_sum, e_rx2, 5)
    nback[own, :] = nback[own, :] + nt(query_back[...], w3[:, :channels])

    part_down.wait_recv()
    own_part = nn(sel_t[...], silu[...])
    rows_out_ref[0] = (
        (own_part + high_part[...].astype(f32)) * inv_own[:, pl.ds(0, 1)]
    ).astype(bf16)

    def norm_back(r, count, extra):
        here = pl.ds(r, count)
        there = pl.ds(margin + r, count)
        nb = nback[there, :]
        if extra is not None:
            nb = nb + extra
        ub = nb * gain_ref[...]
        un = unit[there, :]
        means = nn(jnp.concatenate([ub, ub * un], axis=1).astype(bf16), mean_mat[...])
        grad_out[here, :] = state_back[here, :].astype(f32) + inverse[here, :] * (
            ub - means[:, :channels] - un * means[:, channels:]
        )

    for r in range(0, rows - 2 * margin, 288):
        norm_back(margin + r, min(288, rows - 2 * margin - r), None)
    scattered(l_src, l_rx1, l_sum, l_rx2, 9)
    exchange(l_sum, l_rx2, 10)
    exchanged(e_rx2, e_fin, 5)
    gather(e_fin, 6)
    back_left.wait_recv()
    back_right.wait_recv()
    norm_back(0, margin, nback_recv[0].astype(f32))
    norm_back(rows - margin, margin, nback_recv[1].astype(f32))
    exchanged(l_rx2, l_fin, 10)
    gather(l_fin, 11)
    gathered(e_fin, 6)
    scale = 1.0 / math.sqrt(B * A * rows)
    upper, lower = slice(0, half), slice(half, 2 * half)

    def matrix(ref, part, piece, column):
        chunk = ref[part, piece, column * channels : (column + 1) * channels]
        return chunk.astype(f32).reshape(channels, channels) * scale

    for index, (part, column) in enumerate(((first, 0), (first, 1), (second, 0))):
        for k, piece in enumerate((upper, lower)):
            to = pl.ds((2 * index + k) * channels, channels)
            token_out[:, to] = matrix(e_fin, part, piece, column)
    output_out[...] = matrix(e_fin, second, upper, 1) + matrix(e_fin, second, lower, 1)
    gathered(l_fin, 11)
    query_out[...] = matrix(l_fin, first, upper, 0)
    key_out[...] = matrix(l_fin, first, lower, 0)
    value_out[...] = matrix(l_fin, second, upper, 0)
    gain_out[...] = jnp.sum(matrix(l_fin, second, lower, 0), axis=0, keepdims=True)

    for copy in (halo_left, halo_right, tokens_up, part_down, back_left, back_right):
        copy.wait_send()
    for index, ref, count in (
        (4, e_rx1, G),
        (5, e_rx2, Z),
        (6, e_fin, G),
        (9, l_rx1, G),
        (10, l_rx2, Z),
        (11, l_fin, G),
    ):
        wait_bytes(ref.at[pl.ds(0, count - 1)], send_sem.at[index])


def finish(*refs):
    count = len(refs) // 2
    copies = [
        pltpu.make_async_copy(refs[index], refs[count + index], refs[-1].at[index])
        for index in range(count)
    ]
    for copy in copies:
        copy.start()
    for copy in copies:
        copy.wait()


def on_device(
    A,
    B,
    atom_state,
    norm_gain,
    query_weight,
    key_weight,
    value_weight,
    out_weight,
    token_weight,
    pair_bias,
    key_start,
    atom_token,
    cotangent_state,
    cotangent_tokens,
):
    _, rows, channels = atom_state.shape
    windows, heads, qw, keys = pair_bias.shape
    toks, width = cotangent_tokens.shape[1:]
    planes = 2
    sizes = (A, B, planes, rows, channels, windows, heads, qw, keys, toks, width)
    margin = keys // 2 + qw // 2
    full = rows + 2 * margin
    span = keys + 2 * qw
    G = A * planes
    Z = B // planes
    fold = 4 * channels // G
    early = 2 * channels
    late = channels
    any_spec = pl.BlockSpec(memory_space=pltpu.HBM)
    V = pltpu.VMEM
    DMA = pltpu.SemaphoreType.DMA
    vmem_spec = pl.BlockSpec(memory_space=pltpu.VMEM)
    square = jax.ShapeDtypeStruct((channels, channels), f32)
    shapes = (
        jax.ShapeDtypeStruct((1, rows, channels), bf16),
        jax.ShapeDtypeStruct((1, toks, width), bf16),
        jax.ShapeDtypeStruct((1, rows, channels), f32),
        jax.ShapeDtypeStruct((1, channels), f32),
        square,
        square,
        square,
        square,
        jax.ShapeDtypeStruct((channels, width), f32),
    )
    operands = (
        atom_state,
        norm_gain.reshape(1, channels),
        query_weight,
        key_weight,
        value_weight,
        out_weight,
        token_weight,
        pair_bias.reshape(windows, heads * qw, keys),
        key_start,
        atom_token.reshape(-1, 128),
        cotangent_state,
        cotangent_tokens,
    )
    outs = pl.pallas_call(
        functools.partial(kernel, sizes),
        out_shape=shapes,
        in_specs=[any_spec] * 12,
        out_specs=(vmem_spec,) * 9,
        scratch_shapes=[
            V((1, channels), f32),
            pltpu.SMEM((windows,), jnp.int32),
            V((3 * rows // 128, 128), jnp.int32),
            V((rows, channels), bf16),
            V((channels, 3 * channels), bf16),
            V((channels, channels), bf16),
            V((channels, width), bf16),
            V((windows, heads * qw, keys), f32),
            V((rows, channels), bf16),
            V((toks, width), bf16),
            V((toks, width), bf16),
            V((2, margin, channels), bf16),
            V((full, channels), f32),
            V((rows, channels), f32),
            V((full, channels), bf16),
            V((rows, channels), bf16),
            V((2, full, channels), f32),
            V((windows, keys, 2 * channels), bf16),
            V((windows, heads * qw, keys), bf16),
            V((rows, channels), bf16),
            V((rows, 2 * toks), bf16),
            V((toks, rows), bf16),
            V((toks, 256), bf16),
            V((2 * toks, width), bf16),
            V((toks, 128), f32),
            V((rows, width), bf16),
            V((rows, width), bf16),
            V((rows, channels), bf16),
            V((rows, 2 * channels), bf16),
            V((toks, width), bf16),
            V((toks, width), bf16),
            V((32, keys + 4 * qw, channels), f32),
            V((2, full, channels), f32),
            V((rows, channels), bf16),
            V((full, 2 * channels), bf16),
            V((full, channels), f32),
            V((2, margin, channels), bf16),
            V((2, margin, channels), bf16),
            V((G, fold, early), bf16),
            V((G, fold, early), bf16),
            V((fold, early), bf16),
            V((Z, fold, early), bf16),
            V((G, fold, early), bf16),
            V((G, fold, late), bf16),
            V((G, fold, late), bf16),
            V((fold, late), bf16),
            V((Z, fold, late), bf16),
            V((G, fold, late), bf16),
            V((keys, channels), bf16),
            V((2 * channels, 2 * channels), bf16),
            DMA((14,)),
            DMA((12,)),
            DMA((12,)),
        ],
        compiler_params=pltpu.CompilerParams(
            collective_id=0, has_side_effects=True, vmem_limit_bytes=30 * 1024 * 1024
        ),
        name="atom_block",
    )(*[pltpu.with_memory_space_constraint(x, pltpu.HBM) for x in operands])
    done = pl.pallas_call(
        finish,
        out_shape=shapes,
        in_specs=[vmem_spec] * 9,
        out_specs=(any_spec,) * 9,
        scratch_shapes=[DMA((9,))],
        compiler_params=pltpu.CompilerParams(vmem_limit_bytes=4 * 1024 * 1024),
        name="finish",
    )(*outs)
    return done[:3] + (done[3].reshape(channels),) + done[4:]


def solution(mesh):
    return jax.shard_map(
        functools.partial(on_device, mesh.shape["atom"], mesh.shape["sample"]),
        mesh=mesh,
        in_specs=(
            P("sample", "atom", None),
            P(),
            P(),
            P(),
            P(),
            P(),
            P(),
            P("atom", None, None, None),
            P("atom"),
            P(),
            P("sample", "atom", None),
            P("sample", "atom", None),
        ),
        out_specs=(
            P("sample", "atom", None),
            P("sample", "atom", None),
            P("sample", "atom", None),
            P(),
            P(),
            P(),
            P(),
            P(),
            P(),
        ),
        check_vma=False,
    )
```
